256 devices in a mesh: dp: 8 (over y, core), batch: 32 (over z, x).
Axes of the slice: x: 4, y: 4, z: 8, core: 2. Of those that a mesh axis runs over, the one named last changes fastest.
Arguments:
- waveform: float32 [2048, 512], P(('dp', 'batch')), may hold values from -6 to 6
- lengths: int32 [2048], P(('dp', 'batch')), may hold values from 256 to 512
- destination: int32 [2048], P(('dp', 'batch')), may hold values from 0 to 31, as said below
- tokens: int32 [2048], P(('dp', 'batch')), may hold values from 1 to 32
- cotangent: bfloat16 [2048, 24, 512], P(('dp', 'batch')), may hold values from -6000 to 6000
- initial_filter_weight: bfloat16 [512, 10], P('dp'), may hold values from -2 to 2
- middle_filter_weight: bfloat16 [512, 1536], P('dp'), may hold values from -0.15625 to 0.15625
- final_filter_weight: bfloat16 [512, 1536], P('dp'), may hold values from -0.15625 to 0.15625
Outputs:
- grad_first: float32 [512, 10], P('dp')
- grad_second: float32 [512, 1536], P('dp')
- grad_third: float32 [512, 1536], P('dp')
- grad_rms: float32 [1], replicated
The draws below stay inside these ranges and needn't reach their ends.
Inputs may be any that keep to these rules, and one draw needn't show every extreme that they name: `destination`: every device receives exactly 8 segments from the devices of its dp row; at most 2 segments go from one device to one device, and every device sends exactly 2 to some device.
All inputs are finite; a program needn't handle non-finite values.
Results may differ from the reference program's by a relative error of at most 0.0063.
Values may be sent and summed in bfloat16 or wider, within the bound.
A program may use at most 64 MiB of HBM per device.

```python
import jax
import jax.numpy as jnp
from jax import lax

D = 512
SEG_DEV = 8
MAXLEN = 512
F2 = 24
CAP = 2
SEGS = 2048
N_DP = 8
N_BATCH = 32


def draw_lengths(key, part):
    key = jax.random.fold_in(key, 12)
    drawn = jax.random.randint(key, (SEGS,), MAXLEN // 2, MAXLEN + 1)
    return drawn.at[0].set(MAXLEN).at[1].set(MAXLEN // 2).astype(jnp.int32)


def draw_tokens(key, part):
    key = jax.random.fold_in(key, 13)
    device_index = jnp.arange(SEGS, dtype=jnp.int32) // SEG_DEV
    highest = 4 + 28 * device_index // (N_DP * N_BATCH - 1)
    drawn = jax.random.randint(key, (SEGS,), 1, highest + 1)
    return drawn.at[0].set(1).at[SEGS - 1].set(32).astype(jnp.int32)


def one_row(row_key):
    key_one, key_two, key_three, key_four = jax.random.split(row_key, 4)
    pool_size = N_BATCH * CAP
    shuffled = jax.random.permutation(key_one, pool_size)
    offset_pool = shuffled // CAP
    chosen = offset_pool[0]
    places = jnp.arange(pool_size, dtype=jnp.int32)
    priority = jnp.where(offset_pool == chosen, places - pool_size, places)
    ordering = jnp.argsort(priority, stable=True)
    offsets = offset_pool[ordering][:SEG_DEV]
    offsets = offsets[jax.random.permutation(key_two, SEG_DEV)]
    relabel_out = jax.random.permutation(key_three, N_BATCH)
    relabel_in = jax.random.permutation(key_four, N_BATCH)
    targets = relabel_out[(relabel_in[:, None] + offsets[None, :]) % N_BATCH]
    return targets.reshape(-1)


def draw_destination(key, part):
    key = jax.random.fold_in(key, 11)
    row_keys = jax.random.split(key, N_DP)
    return jax.vmap(one_row)(row_keys).reshape(-1).astype(jnp.int32)


def draw_cotangent(key, part):
    key = jax.random.fold_in(key, 14)
    key_one = jax.random.fold_in(key, 0)
    channel = jnp.arange(D, dtype=jnp.float32) / (D - 1)
    scales = 100.0 * 10.0 ** channel
    values = jnp.clip(jax.random.normal(key_one, (SEGS, F2, D), jnp.float32), -6.0, 6.0)
    return (values * scales[None, None, :]).astype(jnp.bfloat16)


def steps_of(rng, shape, cuts, least, largest):
    def one(axis_at, parts):
        draws = jax.random.uniform(jax.random.fold_in(jax.random.fold_in(rng, 6), axis_at), (parts,), jnp.float32, least / len(cuts), largest / len(cuts))
        return jnp.repeat(jnp.exp(draws), shape[axis_at] // parts).reshape((-1,) + (1,) * (len(shape) - axis_at - 1))

    loudness = one(*cuts[0])
    for cut in cuts[1:]:
        loudness = loudness * one(*cut)
    return loudness


def gaussian(stream_key, extent, scale, reach, cuts=(), kind=jnp.bfloat16):
    result = jax.random.normal(stream_key, extent, jnp.float32) * scale
    if len(cuts) > 0:
        result = steps_of(stream_key, extent, cuts, -0.22, 0.18) * result
    return jnp.clip(result, min=-reach, max=reach).astype(kind)


def setup_inputs(seed: int = 0) -> dict:
    key_of = jax.random.split(jax.random.key(seed), 9)
    waveform = gaussian(key_of[0], (SEGS, MAXLEN), 1.0, 6.0, ((0, 256),), jnp.float32)
    lengths = draw_lengths(jax.random.fold_in(key_of[8], 71), 0)
    destination = draw_destination(jax.random.fold_in(key_of[8], 71), 0)
    tokens = draw_tokens(jax.random.fold_in(key_of[8], 71), 0)
    cotangent = draw_cotangent(jax.random.fold_in(key_of[8], 71), 0)
    initial_filter_weight = gaussian(key_of[5], (D, 10), 10 ** -0.5, 2.0, ((0, 8),))
    middle_filter_weight = gaussian(key_of[6], (D, 3 * D), (3 * D) ** -0.5, 0.15625, ((0, 8),))
    final_filter_weight = gaussian(key_of[7], (D, 3 * D), (3 * D) ** -0.5, 0.15625, ((0, 8),))
    return {"waveform": waveform, "lengths": lengths, "destination": destination, "tokens": tokens, "cotangent": cotangent, "initial_filter_weight": initial_filter_weight, "middle_filter_weight": middle_filter_weight, "final_filter_weight": final_filter_weight}


def out_length(amount, kernel, stride):
    return (amount - kernel) // stride + 1

def layer_norm(hidden):
    average = lax.optimization_barrier(jnp.mean(hidden, axis=-1, keepdims=True))
    centred = hidden - average
    variance = lax.optimization_barrier(jnp.mean(centred * centred, axis=-1, keepdims=True))
    inverse = lax.rsqrt(variance + 1e-05)
    return (centred * inverse, inverse)

def norm_back(grad_out, normed, inverse):
    first_mean = lax.optimization_barrier(jnp.mean(grad_out, axis=-1, keepdims=True))
    second_mean = lax.optimization_barrier(jnp.mean(grad_out * normed, axis=-1, keepdims=True))
    return inverse * (grad_out - first_mean - normed * second_mean)

def gelu_slope(normed):
    return 0.5 * (1.0 + lax.erf(normed * 0.7071067811865476)) + normed * jnp.exp(-0.5 * normed * normed) * 0.3989422804014327

def strided_taps(values, frames):
    return jnp.concatenate([values[:, tap_index:tap_index + 2 * (frames - 1) + 1:2] for tap_index in range(3)], axis=-1)

def spread_back(patch_delta, frames_in, chan_width):
    first_tap = patch_delta[..., :chan_width]
    middle_tap = patch_delta[..., chan_width:2 * chan_width]
    last_tap = patch_delta[..., 2 * chan_width:]
    even_rows = jnp.pad(first_tap, ((0, 0), (0, 1), (0, 0))) + jnp.pad(last_tap, ((0, 0), (1, 0), (0, 0)))
    odd_rows = jnp.pad(middle_tap, ((0, 0), (0, 1), (0, 0)))
    merged = jnp.stack([even_rows, odd_rows], axis=2)
    return merged.reshape(merged.shape[0], -1, chan_width)[:, :frames_in]

def segment_gradient_list(waveform, lengths, token_weight, cotangent, first_weight, second_weight, third_weight):
    seg_count, samples = waveform.shape
    chan_width = second_weight.shape[0]
    position = jnp.arange(samples, dtype=jnp.int32)
    inside = (position[None, :] < lengths[:, None]).astype(jnp.float32)
    length_float = lengths.astype(jnp.float32)[:, None]
    average = lax.optimization_barrier(jnp.sum(waveform * inside, axis=1, keepdims=True)) / length_float
    centred = (waveform - average) * inside
    variance = lax.optimization_barrier(jnp.sum(centred * centred, axis=1, keepdims=True)) / length_float
    normal_wave = centred * lax.rsqrt(variance + 1e-07)
    frames0 = out_length(samples, 10, 5)
    frames1 = out_length(frames0, 3, 2)
    frames2 = out_length(frames1, 3, 2)
    patches0 = jnp.stack([normal_wave[:, tap_index:tap_index + 5 * (frames0 - 1) + 1:5] for tap_index in range(10)], axis=-1)
    hidden0 = jnp.einsum('sfk,ck->sfc', patches0, first_weight.astype(jnp.float32), precision=lax.Precision.HIGHEST)
    normed0, inverse0 = layer_norm(hidden0)
    active0 = jax.nn.gelu(normed0, approximate=False).astype(jnp.bfloat16)
    patches1 = strided_taps(active0, frames1).reshape(seg_count * frames1, 3 * chan_width)
    hidden1 = jnp.dot(patches1, second_weight.T, preferred_element_type=jnp.float32).reshape(seg_count, frames1, chan_width)
    normed1, inverse1 = layer_norm(hidden1)
    active1 = jax.nn.gelu(normed1, approximate=False).astype(jnp.bfloat16)
    patches2 = strided_taps(active1, frames2).reshape(seg_count * frames2, 3 * chan_width)
    hidden2 = jnp.dot(patches2, third_weight.T, preferred_element_type=jnp.float32).reshape(seg_count, frames2, chan_width)
    normed2, inverse2 = layer_norm(hidden2)
    valid_two = out_length(out_length(out_length(lengths, 10, 5), 3, 2), 3, 2)
    frame_weight = (jnp.arange(frames2, dtype=jnp.int32)[None, :] < valid_two[:, None]).astype(jnp.float32) * token_weight[:, None]
    upward2 = cotangent.astype(jnp.float32) * frame_weight[:, :, None] * gelu_slope(normed2)
    delta_two = norm_back(upward2, normed2, inverse2).astype(jnp.bfloat16).reshape(seg_count * frames2, chan_width)
    grad_third = jnp.dot(delta_two.T, patches2, preferred_element_type=jnp.float32)
    patch_delta2 = jnp.dot(delta_two, third_weight, preferred_element_type=jnp.float32).reshape(seg_count, frames2, 3 * chan_width)
    upward1 = spread_back(patch_delta2, frames1, chan_width) * gelu_slope(normed1)
    delta_one = norm_back(upward1, normed1, inverse1).astype(jnp.bfloat16).reshape(seg_count * frames1, chan_width)
    grad_second = jnp.dot(delta_one.T, patches1, preferred_element_type=jnp.float32)
    patch_delta1 = jnp.dot(delta_one, second_weight, preferred_element_type=jnp.float32).reshape(seg_count, frames1, 3 * chan_width)
    upward0 = spread_back(patch_delta1, frames0, chan_width) * gelu_slope(normed0)
    delta_zero = norm_back(upward0, normed0, inverse0)
    grad_first = jnp.einsum('sfc,sfk->ck', delta_zero, patches0, precision=lax.Precision.HIGHEST)
    return (grad_first, grad_second, grad_third)

def reference(waveform, lengths, destination, tokens, cotangent, initial_filter_weight, middle_filter_weight, final_filter_weight):
    seg_total = waveform.shape[0]
    row_segs = seg_total // N_DP
    rows_dest = destination.reshape(N_DP, row_segs)
    order = jnp.arange(row_segs, dtype=jnp.int32)
    matching = rows_dest[:, :, None] == rows_dest[:, None, :]
    earlier = order[None, :] < order[:, None]
    ranking = lax.optimization_barrier(jnp.sum(jnp.logical_and(matching, earlier[None]), axis=2)).astype(jnp.int32)
    arrival = ((jnp.arange(N_DP, dtype=jnp.int32)[:, None] * N_BATCH + rows_dest) * SEG_DEV + ranking).reshape(-1)
    source_index = jnp.zeros((seg_total,), jnp.int32).at[arrival].set(jnp.arange(seg_total, dtype=jnp.int32))
    moved_wave = waveform[source_index]
    moved_lengths = lengths[source_index]
    moved_tokens = tokens[source_index].astype(jnp.float32)
    blocks = seg_total // SEG_DEV
    chan_width = middle_filter_weight.shape[0]
    samples = waveform.shape[1]

    def accumulate(running_total, pieces):
        waveform_block, length_slice_block, token_slice_block, cotangent_block = pieces
        summand_terms = segment_gradient_list(waveform_block, length_slice_block, token_slice_block, cotangent_block, initial_filter_weight, middle_filter_weight, final_filter_weight)
        return ((running_total[0] + summand_terms[0], running_total[1] + summand_terms[1], running_total[2] + summand_terms[2]), None)
    start = (jnp.zeros((chan_width, 10), jnp.float32), jnp.zeros((chan_width, 3 * chan_width), jnp.float32), jnp.zeros((chan_width, 3 * chan_width), jnp.float32))
    sums, unused = lax.scan(accumulate, start, (moved_wave.reshape(blocks, SEG_DEV, samples), moved_lengths.reshape(blocks, SEG_DEV), moved_tokens.reshape(blocks, SEG_DEV), cotangent.reshape(blocks, SEG_DEV, cotangent.shape[1], chan_width)))
    token_sum = jnp.sum(tokens.astype(jnp.float32))
    scaled_first = sums[0] / token_sum
    scaled_second = sums[1] / token_sum
    scaled_third = sums[2] / token_sum
    param_count = chan_width * 10 + 6 * chan_width * chan_width
    squares = jnp.sum(scaled_first * scaled_first) + jnp.sum(scaled_second * scaled_second) + jnp.sum(scaled_third * scaled_third)
    rms_value = jnp.sqrt(squares / param_count)
    factor = 1.0 / jnp.maximum(rms_value, 1.0)
    return (scaled_first * factor, scaled_second * factor, scaled_third * factor, jnp.reshape(rms_value, (1,)))
```

```python
import functools

import jax
import jax.numpy as jnp
from jax import lax
from jax.experimental import pallas as pl
from jax.experimental.pallas import tpu as pltpu
from jax.sharding import PartitionSpec as P

F32 = jnp.float32
BF16 = jnp.bfloat16
D = 512
SEG = 8
J = 26
ROWS = J * SEG
F2 = 24
ROWS2 = F2 * SEG
NT = (((1,), (1,)), ((), ()))
TN = (((0,), (0,)), ((), ()))
NN = (((1,), (0,)), ((), ()))


def mm(a, b, dims):
    return lax.dot_general(a, b, dims, preferred_element_type=F32)


def iota(shape, dim):
    return lax.broadcasted_iota(jnp.int32, shape, dim)


def mean(x):
    return jnp.sum(x, axis=-1, keepdims=True) * (1.0 / D)


def norm_gelu(hidden):
    centred = hidden - mean(hidden)
    inverse = lax.rsqrt(mean(centred * centred) + 1e-05)
    normed = centred * inverse
    cdf = 0.5 + 0.5 * lax.erf(normed * 0.7071067811865476)
    slope = cdf + normed * jnp.exp(-0.5 * normed * normed) * 0.3989422804014327
    return normed, inverse, normed * cdf, slope


def norm_back(grad, normed, inverse):
    return inverse * (grad - mean(grad) - normed * mean(grad * normed))


def pick_waves(got):
    lane_pick = (iota((SEG, 128), 1) == 127).astype(BF16)
    token_row = mm(lane_pick, got, NT)
    column = iota((SEG, 512), 1)
    carries = jnp.logical_and(column % 16 >= 8, column % 4 == 3)
    filled = jnp.where(jnp.logical_and(carries, token_row > 0.5), 1.0, 0.0).astype(BF16)
    row_slot = iota((512, 512), 0)
    row_slot = (row_slot // 16) * 2 + (row_slot // 4) % 2
    column_slot = iota((512, 512), 1)
    column_slot = (column_slot // 16) * 2 + (column_slot // 4) % 2
    weight = jnp.where(row_slot < column_slot, 1.0, 0.0) + jnp.where(
        row_slot == column_slot, 64.0, 0.0
    )
    place = mm(filled, weight.astype(BF16), NN) - 64.0
    target = place + ((column // 8) % 2 * 32 + (column % 4) * 8).astype(F32)
    target = jnp.where(place > -0.5, target, -1.0)
    picking = jnp.where(iota((64, 512), 0).astype(F32) == target[0:1], 1.0, 0.0).astype(BF16)
    picked = mm(picking, got, NN)
    last = picked[56:64]
    length = last[:, 126:127] + 256.0
    tokens = last[:, 127:128]
    low_last = jnp.where(iota((SEG, 128), 1) < 126, last, 0.0)
    pieces = [picked[8 * i : 8 * i + 8] + picked[32 + 8 * i : 40 + 8 * i] for i in range(3)]
    pieces.append(picked[24:32] + low_last)
    return jnp.concatenate(pieces, axis=1), length, tokens


def first_taps(wave, length):
    inside = iota((SEG, D), 1).astype(F32) < length
    average = jnp.sum(jnp.where(inside, wave, 0.0), axis=1, keepdims=True) / length
    centred = jnp.where(inside, wave - average, 0.0)
    variance = jnp.sum(centred * centred, axis=1, keepdims=True) / length
    normal = centred * lax.rsqrt(variance + 1e-07)
    padded = jnp.concatenate([normal, jnp.zeros((SEG, 256), F32)], axis=1)
    rows = []
    for j in range(J):
        tile, shift = (20 * j) // 128, (20 * j) % 128
        pair = padded[:, tile * 128 : tile * 128 + 256]
        if shift:
            pair = pltpu.roll(pair, 256 - shift, axis=1)
        rows.append(pair[:, :128])
    taps = jnp.concatenate(rows, axis=0)
    return jnp.where(iota((ROWS, 128), 1) < 32, taps, 0.0)


def forward_first(got, w0_ref, r):
    wave, length, tokens = pick_waves(got)
    taps = first_taps(wave, length)
    high = taps.astype(BF16).astype(F32)
    both = high + pltpu.roll(taps - high, 32, axis=1)
    both_narrow = both.astype(BF16)
    narrow_lane = iota((ROWS, 128), 1)
    for c in range(4):
        moved = pltpu.roll(both, 128 - 5 * c, axis=1) if c else both
        keep = narrow_lane % 32 < 10
        moved = jnp.where(jnp.logical_and(keep, narrow_lane < 64), moved, 0.0)
        r["x4"][c * ROWS : (c + 1) * ROWS] = moved.astype(BF16)
    w0 = w0_ref[...]
    tap_row, tap_column = iota((128, 128), 0), iota((128, 128), 1)
    for c in range(4):
        placing = jnp.logical_and(tap_row % 32 == tap_column + 5 * c, tap_row < 64)
        placing = jnp.logical_and(placing, tap_column < 10)
        weight = mm(jnp.where(placing, 1.0, 0.0).astype(BF16), w0, NT).astype(BF16)
        r["z0"][c * ROWS : (c + 1) * ROWS] = mm(both_narrow, weight, NN)
    l2 = ((((length - 10.0) * 0.2).astype(jnp.int32) + 1 - 3) // 2 + 1 - 3) // 2 + 1
    r["info"][0:8] = jnp.broadcast_to(l2.astype(F32), (SEG, 128))
    r["info"][8:16] = jnp.broadcast_to(tokens, (SEG, 128))

    for c in range(4):

        def body(m, carry, c=c):
            at = pl.multiple_of(m * 16, 16)
            rows = pl.ds(pl.multiple_of(c * ROWS + m * 16, 16), 16)
            here = pl.ds(at, 16)
            normed, inverse, active, slope = norm_gelu(r["z0"][rows])
            r["z0"][rows] = normed
            r["s0"][rows] = slope
            r["r0"][rows] = jnp.broadcast_to(inverse, (16, 128))
            narrow = active.astype(BF16)
            if c < 3:
                r["p1"][here, c * D : (c + 1) * D] = narrow
            if c == 0:
                r["shift"][here] = active
            else:
                odd = pl.ds(pl.multiple_of(ROWS + m * 16, 16), 16)
                if c >= 2:
                    r["p1"][odd, (c - 2) * D : (c - 1) * D] = narrow
            return carry

        lax.fori_loop(0, ROWS // 16, body, 0)
    r["shift"][ROWS : ROWS + 8] = jnp.zeros((8, D), F32)

    def shifted(m, carry):
        rows = pl.ds(pl.multiple_of(8 + m * 16, 8), 16)
        odd = pl.ds(pl.multiple_of(ROWS + m * 16, 16), 16)
        r["p1"][odd, 2 * D :] = r["shift"][rows].astype(BF16)
        return carry

    lax.fori_loop(0, ROWS // 16, shifted, 0)


def forward_second(w1_ref, r):
    r["z1"][...] = mm(r["p1"][...], w1_ref[...], NT)

    def even(m, carry):
        rows = pl.ds(pl.multiple_of(m * 16, 16), 16)
        normed, inverse, active, slope = norm_gelu(r["z1"][rows])
        r["z1"][rows] = normed
        r["s1"][rows] = slope
        r["r1"][rows] = jnp.broadcast_to(inverse, (16, 128))
        r["shift"][rows] = active
        return carry

    lax.fori_loop(0, ROWS // 16, even, 0)

    def odd(m, carry):
        rows = pl.ds(pl.multiple_of(ROWS + m * 16, 16), 16)
        here = pl.ds(pl.multiple_of(m * 16, 16), 16)
        normed, inverse, active, slope = norm_gelu(r["z1"][rows])
        r["z1"][rows] = normed
        r["s1"][rows] = slope
        r["r1"][rows] = jnp.broadcast_to(inverse, (16, 128))
        r["p2"][here, D : 2 * D] = active.astype(BF16)
        return carry

    lax.fori_loop(0, ROWS // 16, odd, 0)

    def spread(m, carry):
        here = pl.ds(pl.multiple_of(m * 16, 16), 16)
        after = pl.ds(pl.multiple_of(8 + m * 16, 8), 16)
        r["p2"][here, 0:D] = r["shift"][here].astype(BF16)
        r["p2"][here, 2 * D :] = r["shift"][after].astype(BF16)
        return carry

    lax.fori_loop(0, ROWS // 16, spread, 0)


def third_layer(cot_ref, w2_ref, r):
    r["z2"][...] = mm(r["p2"][0:ROWS2], w2_ref[...], NT)
    row, column = iota((ROWS2, ROWS2), 0), iota((ROWS2, ROWS2), 1)
    order = jnp.where(column == (row % SEG) * F2 + row // SEG, 1.0, 0.0).astype(BF16)
    r["c2"][...] = mm(order, cot_ref[...], NN)
    limit = jnp.concatenate([r["info"][0:8, 0:1]] * 2, axis=0)
    tokens = jnp.concatenate([r["info"][8:16, 0:1]] * 2, axis=0)
    half = (iota((16, 1), 0) // 8).astype(F32)

    def body(m, carry):
        rows = pl.ds(pl.multiple_of(m * 16, 16), 16)
        normed, inverse, active, slope = norm_gelu(r["z2"][rows])
        frame = half + (2 * m).astype(F32)
        weight = jnp.where(frame < limit, tokens, 0.0)
        grad = r["c2"][rows] * weight * slope
        r["d2"][rows] = norm_back(grad, normed, inverse).astype(BF16)
        return carry

    lax.fori_loop(0, ROWS2 // 16, body, 0)


def grad_third(out_ref, r):
    out_ref[...] = mm(r["d2"][...], r["p2"][0:ROWS2], TN).astype(out_ref.dtype)


def back_second(w2_ref, r):
    r["u"][0:8] = jnp.zeros((8, 3 * D), F32)
    r["u"][8 + ROWS2 : 32 + ROWS2] = jnp.zeros((24, 3 * D), F32)
    r["u"][8 : 8 + ROWS2] = mm(r["d2"][...], w2_ref[...], NN)

    def even(m, carry):
        rows = pl.ds(pl.multiple_of(m * 16, 16), 16)
        after = pl.ds(pl.multiple_of(8 + m * 16, 8), 16)
        up = r["u"][after, 0:D] + r["u"][rows, 2 * D :]
        delta = norm_back(up * r["s1"][rows], r["z1"][rows], r["r1"][rows, 0:1])
        r["d1"][rows] = delta.astype(BF16)
        return carry

    lax.fori_loop(0, ROWS // 16, even, 0)

    def odd(m, carry):
        rows = pl.ds(pl.multiple_of(ROWS + m * 16, 16), 16)
        after = pl.ds(pl.multiple_of(8 + m * 16, 8), 16)
        up = r["u"][after, D : 2 * D]
        delta = norm_back(up * r["s1"][rows], r["z1"][rows], r["r1"][rows, 0:1])
        r["d1"][rows] = delta.astype(BF16)
        return carry

    lax.fori_loop(0, ROWS // 16, odd, 0)


def grad_second(out_ref, r):
    out_ref[...] = mm(r["d1"][...], r["p1"][...], TN).astype(out_ref.dtype)


def back_first(w1_ref, r):
    r["ue"][...] = mm(r["d1"][0:ROWS], w1_ref[...], NN)
    r["uo"][0:8] = jnp.zeros((8, 3 * D), F32)
    r["uo"][8:] = mm(r["d1"][ROWS:], w1_ref[...], NN)
    for c in range(4):

        def body(m, carry, c=c):
            here = pl.ds(pl.multiple_of(m * 16, 16), 16)
            after = pl.ds(pl.multiple_of(8 + m * 16, 8), 16)
            rows = pl.ds(pl.multiple_of(c * ROWS + m * 16, 16), 16)
            if c == 0:
                up = r["ue"][here, 0:D] + r["uo"][here, 2 * D :]
            elif c == 1:
                up = r["ue"][here, D : 2 * D]
            elif c == 2:
                up = r["ue"][here, 2 * D :] + r["uo"][after, 0:D]
            else:
                up = r["uo"][after, D : 2 * D]
            delta = norm_back(up * r["s0"][rows], r["z0"][rows], r["r0"][rows, 0:1])
            r["d0"][rows] = delta.astype(BF16)
            return carry

        lax.fori_loop(0, ROWS // 16, body, 0)


def grad_first(out_ref, r):
    found = mm(r["d0"][...], r["x4"][...], TN)
    found = found + pltpu.roll(found, 96, axis=1)
    found = jnp.where(iota((D, 128), 1) < 10, found, 0.0)
    out_ref[...] = found.astype(out_ref.dtype)


COMPUTE_SCRATCH = {
    "x4": ((4 * ROWS, 128), BF16),
    "z0": ((4 * ROWS, D), F32),
    "s0": ((4 * ROWS, D), F32),
    "r0": ((4 * ROWS, 128), F32),
    "d0": ((4 * ROWS, D), BF16),
    "info": ((16, 128), F32),
    "shift": ((ROWS + 8, D), F32),
    "p1": ((2 * ROWS, 3 * D), BF16),
    "z1": ((2 * ROWS, D), F32),
    "s1": ((2 * ROWS, D), F32),
    "r1": ((2 * ROWS, 128), F32),
    "d1": ((2 * ROWS, D), BF16),
    "p2": ((ROWS, 3 * D), BF16),
    "z2": ((ROWS2, D), F32),
    "c2": ((ROWS2, D), F32),
    "d2": ((ROWS2, D), BF16),
    "u": ((ROWS2 + 32, 3 * D), F32),
    "ue": ((ROWS, 3 * D), F32),
    "uo": ((ROWS + 8, 3 * D), F32),
}


def compute_kernel(got, w0, w1, w2, cot, grads, *scratch):
    r = dict(zip(COMPUTE_SCRATCH, scratch))
    forward_first(got[...], w0, r)
    forward_second(w1, r)
    third_layer(cot, w2, r)
    grad_third(grads.at[:, 0 : 3 * D], r)
    back_second(w2, r)
    grad_second(grads.at[:, 3 * D : 6 * D], r)
    back_first(w1, r)
    grad_first(grads.at[:, 6 * D :], r)


def compute(got, w0, w1, w2, cot):
    vmem = pl.BlockSpec(memory_space=pltpu.VMEM)
    return pl.pallas_call(
        compute_kernel,
        out_shape=jax.ShapeDtypeStruct((D, 6 * D + 128), BF16),
        in_specs=[vmem] * 5,
        out_specs=vmem,
        scratch_shapes=[pltpu.VMEM(s, t) for s, t in COMPUTE_SCRATCH.values()],
        compiler_params=pltpu.CompilerParams(vmem_limit_bytes=56 << 20),
        cost_estimate=pl.CostEstimate(flops=3000000000, bytes_accessed=8000000, transcendentals=1400000),
    )(got, w0, w1, w2, cot)


def place():
    dp, batch = lax.axis_index("dp"), lax.axis_index("batch")
    return dp, batch, dp // 2, dp % 2, batch // 4, batch % 4


def signal_to(sem, dp, batch):
    pl.semaphore_signal(sem, inc=1, device_id=(dp, batch), device_id_type=pl.DeviceIdType.MESH)


def remote(src, dst, send, recv, dp, batch):
    return pltpu.make_async_remote_copy(
        src_ref=src,
        dst_ref=dst,
        send_sem=send,
        recv_sem=recv,
        device_id=(dp, batch),
        device_id_type=pl.DeviceIdType.MESH,
    )


def landed(ref, sem):
    pltpu.make_async_copy(ref, ref, sem).wait()


def loop(first, last, step):
    def body(i, carry):
        step(i)
        return carry

    lax.fori_loop(first, last, body, 0)


def pack_waves(wave, dest, length, tokens):
    high = wave.astype(BF16).astype(F32)
    low = wave - high
    lane, row = iota((SEG, 128), 1), iota((SEG, 128), 0)
    target = lane // 32 * 8 + (lane // 8) % 4
    extra = jnp.zeros((SEG, 128), F32)
    for s in range(SEG):
        here = dest[s]
        rank = 0
        for t in range(s):
            rank = rank + jnp.where(dest[t] == here, 1, 0)
        target = target + jnp.where(lane % 8 == s, here * 16 + rank * 4, 0)
        detail = jnp.where(lane == 126, length[s] - 256, tokens[s]).astype(F32)
        extra = jnp.where(row == s, detail, extra)
    rows = [high[:, 128 * i : 128 * i + 128] for i in range(4)]
    rows += [low[:, 128 * i : 128 * i + 128] for i in range(3)]
    rows.append(jnp.where(lane < 126, low[:, 384:], extra))
    data = jnp.concatenate(rows, axis=0).astype(BF16)
    select = jnp.where(iota((512, 64), 0) == target[0:1, 0:64], 1.0, 0.0).astype(BF16)
    return mm(select, data, NN).astype(BF16)


def exchange_kernel(
    wave, dest, length, tokens, w0, w1, w2, got, f0, f1, f2,
    send, mine0, wave_send, wave_recv, row_send, row_recv, pass_send, pass_recv,
):
    dp, batch, y, core, z, x = place()
    barrier = pltpu.get_barrier_semaphore()
    loop(1, 32, lambda k: signal_to(barrier, dp, lax.rem(batch + k, 32)))
    for k in range(1, 4):
        signal_to(barrier, lax.rem(y + k, 4) * 2 + core, batch)
    signal_to(barrier, y * 2 + 1 - core, batch)
    mine0[...] = jnp.concatenate([w0[...], jnp.zeros((64, 118), BF16)], axis=1)
    send[...] = pack_waves(wave[...], dest, length, tokens).reshape(32, 16, 128)
    pl.semaphore_wait(barrier, 35)

    def wave_copy(k):
        to = lax.rem(batch + k, 32)
        return remote(send.at[to], got.at[batch], wave_send, wave_recv, dp, to)

    loop(1, 32, lambda k: wave_copy(k).start())
    sources, fulls = (mine0, w1, w2), (f0, f1, f2)

    def block(full, who):
        return full.at[pl.ds(pl.multiple_of(who * 64, 64), 64)]

    def row_copy(w, k):
        to = lax.rem(y + k, 4) * 2 + core
        return remote(sources[w], block(fulls[w], dp), row_send.at[w, k], row_recv.at[w, k], to, batch)

    def pass_copy(w, k):
        owner = lax.rem(y + 4 - k, 4) * 2 + core
        source = sources[w] if k == 0 else block(fulls[w], owner)
        to = y * 2 + 1 - core
        return remote(source, block(fulls[w], owner), pass_send.at[w, k], pass_recv.at[w, k], to, batch)

    for w in range(3):
        for k in (2, 1, 3):
            row_copy(w, k).start()
        pass_copy(w, 0).start()
    got[batch] = send[batch]
    for w in range(3):
        block(fulls[w], dp)[...] = sources[w][...]
    for w in range(3):
        for k in (1, 3, 2):
            row_copy(w, k).wait_recv()
            pass_copy(w, k).start()
    landed(send.at[0:31], wave_recv)
    landed(send.at[0:31], wave_send)
    for w in range(3):
        for k in range(4):
            pass_copy(w, k).wait()
            if k:
                row_copy(w, k).wait_send()


def exchange(wave, dest, length, tokens, w0, w1, w2):
    vmem = pl.BlockSpec(memory_space=pltpu.VMEM)
    smem = pl.BlockSpec(memory_space=pltpu.SMEM)
    return pl.pallas_call(
        exchange_kernel,
        out_shape=(
            jax.ShapeDtypeStruct((32, 16, 128), BF16),
            jax.ShapeDtypeStruct((D, 128), BF16),
            jax.ShapeDtypeStruct((D, 3 * D), BF16),
            jax.ShapeDtypeStruct((D, 3 * D), BF16),
        ),
        in_specs=[vmem, smem, smem, smem, vmem, vmem, vmem],
        out_specs=(vmem,) * 4,
        scratch_shapes=[
            pltpu.VMEM((32, 16, 128), BF16),
            pltpu.VMEM((64, 128), BF16),
            pltpu.SemaphoreType.DMA,
            pltpu.SemaphoreType.DMA,
            pltpu.SemaphoreType.DMA((3, 4)),
            pltpu.SemaphoreType.DMA((3, 4)),
            pltpu.SemaphoreType.DMA((3, 4)),
            pltpu.SemaphoreType.DMA((3, 4)),
        ],
        compiler_params=pltpu.CompilerParams(
            collective_id=0, has_side_effects=True, vmem_limit_bytes=40 << 20
        ),
    )(wave, dest, length, tokens, w0, w1, w2)


WIDE = 6 * D + 128
PIECES = ((0, 3 * D), (3 * D, 3 * D), (6 * D, 128))
COUNT = D * 10 + 6 * D * D


def reduce_kernel(
    grads, tokens, out,
    rc, ys, yr, xs, xr, zs, zr, fz, fx, fr, ta, tb, sa, sb, my_t, my_t2, my_s, my_s2,
    core_send, core_recv, y_send, y_recv, x_send, x_recv, z_send, z_recv, fz_send, fz_recv, fx_send, fx_recv,
    ta_send, ta_recv, tb_send, tb_recv, sa_send, sa_recv, sb_send, sb_recv,
):
    dp, batch, y, core, z, x = place()
    barrier = pltpu.get_barrier_semaphore()
    group = dp * 4 + x

    def group_peer(k):
        other = lax.rem(group + k, 32)
        return other // 4, z * 4 + other % 4

    def z_peer(k):
        return lax.rem(z + k, 8) * 4 + x

    def x_peer(k):
        return z * 4 + lax.rem(x + k, 4)

    loop(1, 32, lambda k: signal_to(barrier, *group_peer(k)))
    loop(1, 8, lambda k: signal_to(barrier, dp, z_peer(k)))
    total = tokens[0]
    for s in range(1, SEG):
        total = total + tokens[s]
    my_t[...] = jnp.broadcast_to(total.astype(F32), (8, 128))
    pl.semaphore_wait(barrier, 38)

    def core_copy(p, k):
        start, width = PIECES[p]
        step = lax.rem(y + k, 4)
        rows = pl.ds(pl.multiple_of((step * 2 + 1 - core) * 64, 64), 64)
        return remote(
            grads.at[rows, start : start + width], rc.at[step, :, start : start + width],
            core_send.at[p, k], core_recv.at[p, k], y * 2 + 1 - core, batch,
        )

    def y_copy(p, k):
        start, width = PIECES[p]
        to = lax.rem(y + k, 4)
        return remote(
            ys.at[to, :, start : start + width], yr.at[y, :, start : start + width],
            y_send.at[p, k], y_recv.at[p, k], to * 2 + core, batch,
        )

    def x_copy(k):
        to = lax.rem(x + k, 4)
        return remote(
            xs.at[pl.ds(pl.multiple_of(to * 16, 16), 16)], xr.at[x],
            x_send.at[k], x_recv.at[k], dp, z * 4 + to,
        )

    def z_copy(k):
        to = lax.rem(z + k, 8)
        return remote(zs.at[to], zr.at[z], z_send, z_recv, dp, to * 4 + x)

    def fz_copy(k):
        return remote(fz.at[z], fz.at[z], fz_send, fz_recv, dp, z_peer(k))

    def fx_copy(k):
        return remote(fr.at[x], fr.at[x], fx_send, fx_recv, dp, x_peer(k))

    def ta_copy(k):
        return remote(my_t, ta.at[group], ta_send, ta_recv, *group_peer(k))

    def tb_copy(k):
        return remote(my_t2, tb.at[z], tb_send, tb_recv, dp, z_peer(k))

    def sa_copy(k):
        return remote(my_s, sa.at[z], sa_send, sa_recv, dp, z_peer(k))

    def sb_copy(k):
        return remote(my_s2, sb.at[group], sb_send, sb_recv, *group_peer(k))

    for p in range(3):
        for k in (2, 1, 3, 0):
            core_copy(p, k).start()
    loop(1, 32, lambda k: ta_copy(k).start())
    ta[group] = my_t[...]
    for p in range(3):
        start, width = PIECES[p]
        for k in (2, 1, 3, 0):
            core_copy(p, k).wait_recv()
            step = lax.rem(y + k, 4)
            rows = pl.ds(pl.multiple_of((step * 2 + core) * 64, 64), 64)
            own = grads[rows, start : start + width].astype(F32)
            ys[step, :, start : start + width] = (
                own + rc[step, :, start : start + width].astype(F32)
            ).astype(BF16)
            if k:
                y_copy(p, k).start()
    landed(ta.at[0:31], ta_recv)
    my_t2[...] = jnp.sum(ta[...], axis=0)
    tb[z] = my_t2[...]
    loop(1, 8, lambda k: tb_copy(k).start())
    for p in range(3):
        start, width = PIECES[p]
        found = ys[y, :, start : start + width].astype(F32)
        for k in (1, 3, 2):
            y_copy(p, k).wait_recv()
            found = found + yr[lax.rem(y + 4 - k, 4), :, start : start + width].astype(F32)
        xs[:, start : start + width] = found.astype(BF16)
    for k in (2, 1, 3):
        x_copy(k).start()
    found = xs[pl.ds(pl.multiple_of(x * 16, 16), 16)].astype(F32)
    for k in (1, 3, 2):
        x_copy(k).wait_recv()
        found = found + xr[lax.rem(x + 4 - k, 4)].astype(F32)
    for q in range(8):
        zs[q, :, 0:384] = found[:, q * 384 : q * 384 + 384].astype(BF16)
        zs[q, :, 384:] = found[:, 6 * D :].astype(BF16)
    loop(1, 8, lambda k: z_copy(k).start())
    zr[z] = zs[z]
    landed(tb.at[0:7], tb_recv)
    token_sum = jnp.sum(tb[...], axis=0)
    landed(zr.at[0:7], z_recv)
    found = jnp.sum(zr[...].astype(F32), axis=0)
    fz[z] = found[:, 0:384].astype(BF16)
    loop(1, 8, lambda k: fz_copy(k).start())
    scaled = found * (1.0 / token_sum[0:1, 0:1])
    own = jnp.sum(scaled[:, 0:384] * scaled[:, 0:384], keepdims=True)
    first = jnp.sum(scaled[:, 384:] * scaled[:, 384:], keepdims=True)
    my_s[...] = jnp.broadcast_to(own + jnp.where(z == 0, first, 0.0), (8, 128))
    loop(1, 8, lambda k: sa_copy(k).start())
    sa[z] = my_s[...]
    fr[x, :, 6 * D :] = found[:, 384:].astype(BF16)
    landed(fz.at[0:7], fz_recv)
    for q in range(8):
        fr[x, :, q * 384 : q * 384 + 384] = fz[q]
    for k in (2, 1, 3):
        fx_copy(k).start()
    landed(sa.at[0:7], sa_recv)
    my_s2[...] = jnp.sum(sa[...], axis=0)
    loop(1, 32, lambda k: sb_copy(k).start())
    sb[group] = my_s2[...]
    landed(sb.at[0:31], sb_recv)
    squares = jnp.sum(sb[...], axis=0)
    rms = jnp.sqrt(squares * (1.0 / COUNT))
    factor = (1.0 / (token_sum * jnp.maximum(rms, 1.0)))[0:1, 0:1]
    landed(fr.at[0:3], fx_recv)
    out[0:64] = fr[...].reshape(64, WIDE).astype(F32) * factor
    out[64:72] = jnp.broadcast_to(rms[0:1, 0:1], (8, WIDE))
    for p in range(3):
        for k in range(4):
            core_copy(p, k).wait_send()
            if k:
                y_copy(p, k).wait_send()
    for k in range(1, 4):
        x_copy(k).wait_send()
    landed(zr.at[0:7], z_send)
    landed(fz.at[0:7], fz_send)
    landed(fr.at[0:3], fx_send)
    landed(ta.at[0:31], ta_send)
    landed(sb.at[0:31], sb_send)
    landed(tb.at[0:7], tb_send)
    landed(sa.at[0:7], sa_send)


def reduce_grads(grads, tokens):
    vmem = pl.BlockSpec(memory_space=pltpu.VMEM)
    smem = pl.BlockSpec(memory_space=pltpu.SMEM)
    dma = pltpu.SemaphoreType.DMA
    return pl.pallas_call(
        reduce_kernel,
        out_shape=jax.ShapeDtypeStruct((72, WIDE), F32),
        in_specs=[vmem, smem],
        out_specs=vmem,
        scratch_shapes=[
            pltpu.VMEM((4, 64, WIDE), BF16),
            pltpu.VMEM((4, 64, WIDE), BF16),
            pltpu.VMEM((4, 64, WIDE), BF16),
            pltpu.VMEM((64, WIDE), BF16),
            pltpu.VMEM((4, 16, WIDE), BF16),
            pltpu.VMEM((8, 16, 512), BF16),
            pltpu.VMEM((8, 16, 512), BF16),
            pltpu.VMEM((8, 16, 384), BF16),
            pltpu.VMEM((16, WIDE), BF16),
            pltpu.VMEM((4, 16, WIDE), BF16),
            pltpu.VMEM((32, 8, 128), F32),
            pltpu.VMEM((8, 8, 128), F32),
            pltpu.VMEM((8, 8, 128), F32),
            pltpu.VMEM((32, 8, 128), F32),
        ]
        + [pltpu.VMEM((8, 128), F32)] * 4
        + [dma((3, 4))] * 4
        + [dma((4,))] * 2
        + [dma] * 14,
        compiler_params=pltpu.CompilerParams(
            collective_id=1, has_side_effects=True, vmem_limit_bytes=40 << 20
        ),
    )(grads, tokens)


def local(wave, length, dest, tokens, cot, w0, w1, w2):
    got, f0, f1, f2 = exchange(wave, dest, length, tokens, w0, w1, w2)
    grads = compute(got.reshape(512, 128), f0, f1, f2, cot.reshape(ROWS2, D))
    out = reduce_grads(grads, tokens)
    return (
        out[0:64, 6 * D : 6 * D + 10],
        out[0:64, 3 * D : 6 * D],
        out[0:64, 0 : 3 * D],
        out[64, 0:1],
    )


def solution(mesh):
    row = P(("dp", "batch"))
    return jax.shard_map(
        local,
        mesh=mesh,
        in_specs=(row, row, row, row, row, P("dp"), P("dp"), P("dp")),
        out_specs=(P("dp"), P("dp"), P("dp"), P()),
        check_vma=False,
    )
```

```python
import functools

import jax
import jax.numpy as jnp
from jax import lax
from jax.experimental import pallas as pl
from jax.experimental.pallas import tpu as pltpu
from jax.sharding import PartitionSpec as P

F32 = jnp.float32
BF16 = jnp.bfloat16
D = 512
SEG = 8
J = 26
ROWS = J * SEG
F2 = 24
UNROLL = True
ROWS2 = F2 * SEG
NT = (((1,), (1,)), ((), ()))
TN = (((0,), (0,)), ((), ()))
NN = (((1,), (0,)), ((), ()))


def mm(a, b, dims):
    return lax.dot_general(a, b, dims, preferred_element_type=F32)


def iota(shape, dim):
    return lax.broadcasted_iota(jnp.int32, shape, dim)


def mean(x):
    return jnp.sum(x, axis=-1, keepdims=True) * (1.0 / D)


def norm_gelu(hidden):
    centred = hidden - mean(hidden)
    inverse = lax.rsqrt(mean(centred * centred) + 1e-05)
    normed = centred * inverse
    cdf = 0.5 + 0.5 * lax.erf(normed * 0.7071067811865476)
    slope = cdf + normed * jnp.exp(-0.5 * normed * normed) * 0.3989422804014327
    return normed, inverse, normed * cdf, slope


def norm_back(grad, normed, inverse):
    return inverse * (grad - mean(grad) - normed * mean(grad * normed))


def pick_waves(got):
    lane_pick = (iota((SEG, 128), 1) == 127).astype(BF16)
    token_row = mm(lane_pick, got, NT)
    column = iota((SEG, 512), 1)
    carries = jnp.logical_and(column % 16 >= 8, column % 4 == 3)
    filled = jnp.where(jnp.logical_and(carries, token_row > 0.5), 1.0, 0.0).astype(BF16)
    row_slot = iota((512, 512), 0)
    row_slot = (row_slot // 16) * 2 + (row_slot // 4) % 2
    column_slot = iota((512, 512), 1)
    column_slot = (column_slot // 16) * 2 + (column_slot // 4) % 2
    weight = jnp.where(row_slot < column_slot, 1.0, 0.0) + jnp.where(
        row_slot == column_slot, 64.0, 0.0
    )
    place = mm(filled, weight.astype(BF16), NN) - 64.0
    target = place + ((column // 8) % 2 * 32 + (column % 4) * 8).astype(F32)
    target = jnp.where(place > -0.5, target, -1.0)
    picking = jnp.where(iota((64, 512), 0).astype(F32) == target[0:1], 1.0, 0.0).astype(BF16)
    picked = mm(picking, got, NN)
    last = picked[56:64]
    length = last[:, 126:127] + 256.0
    tokens = last[:, 127:128]
    low_last = jnp.where(iota((SEG, 128), 1) < 126, last, 0.0)
    pieces = [picked[8 * i : 8 * i + 8] + picked[32 + 8 * i : 40 + 8 * i] for i in range(3)]
    pieces.append(picked[24:32] + low_last)
    return jnp.concatenate(pieces, axis=1), length, tokens


def first_taps(wave, length):
    inside = iota((SEG, D), 1).astype(F32) < length
    average = jnp.sum(jnp.where(inside, wave, 0.0), axis=1, keepdims=True) / length
    centred = jnp.where(inside, wave - average, 0.0)
    variance = jnp.sum(centred * centred, axis=1, keepdims=True) / length
    normal = centred * lax.rsqrt(variance + 1e-07)
    padded = jnp.concatenate([normal, jnp.zeros((SEG, 256), F32)], axis=1)
    rows = []
    for j in range(J):
        tile, shift = (20 * j) // 128, (20 * j) % 128
        pair = padded[:, tile * 128 : tile * 128 + 256]
        if shift:
            pair = pltpu.roll(pair, 256 - shift, axis=1)
        rows.append(pair[:, :128])
    taps = jnp.concatenate(rows, axis=0)
    return jnp.where(iota((ROWS, 128), 1) < 32, taps, 0.0)


def forward_first(got, w0_ref, r):
    wave, length, tokens = pick_waves(got)
    taps = first_taps(wave, length)
    high = taps.astype(BF16).astype(F32)
    both = high + pltpu.roll(taps - high, 32, axis=1)
    both_narrow = both.astype(BF16)
    narrow_lane = iota((ROWS, 128), 1)
    for c in range(4):
        moved = pltpu.roll(both, 128 - 5 * c, axis=1) if c else both
        keep = narrow_lane % 32 < 10
        moved = jnp.where(jnp.logical_and(keep, narrow_lane < 64), moved, 0.0)
        r["x4"][c * ROWS : (c + 1) * ROWS] = moved.astype(BF16)
    w0 = w0_ref[...]
    tap_row, tap_column = iota((128, 128), 0), iota((128, 128), 1)
    for c in range(4):
        placing = jnp.logical_and(tap_row % 32 == tap_column + 5 * c, tap_row < 64)
        placing = jnp.logical_and(placing, tap_column < 10)
        weight = mm(jnp.where(placing, 1.0, 0.0).astype(BF16), w0, NT).astype(BF16)
        r["z0"][c * ROWS : (c + 1) * ROWS] = mm(both_narrow, weight, NN)
    l2 = ((((length - 10.0) * 0.2).astype(jnp.int32) + 1 - 3) // 2 + 1 - 3) // 2 + 1
    r["info"][0:8] = jnp.broadcast_to(l2.astype(F32), (SEG, 128))
    r["info"][8:16] = jnp.broadcast_to(tokens, (SEG, 128))

    for c in range(4):

        def body(m, carry, c=c):
            at = pl.multiple_of(m * 16, 16)
            rows = pl.ds(pl.multiple_of(c * ROWS + m * 16, 16), 16)
            here = pl.ds(at, 16)
            normed, inverse, active, slope = norm_gelu(r["z0"][rows])
            r["z0"][rows] = normed
            r["s0"][rows] = slope
            r["r0"][rows] = jnp.broadcast_to(inverse, (16, 128))
            narrow = active.astype(BF16)
            if c < 3:
                r["p1"][here, c * D : (c + 1) * D] = narrow
            if c == 0:
                r["shift"][here] = active
            else:
                odd = pl.ds(pl.multiple_of(ROWS + m * 16, 16), 16)
                if c >= 2:
                    r["p1"][odd, (c - 2) * D : (c - 1) * D] = narrow
            return carry

        lax.fori_loop(0, ROWS // 16, body, 0, unroll=UNROLL)
    r["shift"][ROWS : ROWS + 8] = jnp.zeros((8, D), F32)

    def shifted(m, carry):
        rows = pl.ds(pl.multiple_of(8 + m * 16, 8), 16)
        odd = pl.ds(pl.multiple_of(ROWS + m * 16, 16), 16)
        r["p1"][odd, 2 * D :] = r["shift"][rows].astype(BF16)
        return carry

    lax.fori_loop(0, ROWS // 16, shifted, 0, unroll=UNROLL)


def forward_second(w1_ref, r):
    r["z1"][...] = mm(r["p1"][...], w1_ref[...], NT)

    def even(m, carry):
        rows = pl.ds(pl.multiple_of(m * 16, 16), 16)
        normed, inverse, active, slope = norm_gelu(r["z1"][rows])
        r["z1"][rows] = normed
        r["s1"][rows] = slope
        r["r1"][rows] = jnp.broadcast_to(inverse, (16, 128))
        r["shift"][rows] = active
        return carry

    lax.fori_loop(0, ROWS // 16, even, 0, unroll=UNROLL)

    def odd(m, carry):
        rows = pl.ds(pl.multiple_of(ROWS + m * 16, 16), 16)
        here = pl.ds(pl.multiple_of(m * 16, 16), 16)
        normed, inverse, active, slope = norm_gelu(r["z1"][rows])
        r["z1"][rows] = normed
        r["s1"][rows] = slope
        r["r1"][rows] = jnp.broadcast_to(inverse, (16, 128))
        r["p2"][here, D : 2 * D] = active.astype(BF16)
        return carry

    lax.fori_loop(0, ROWS // 16, odd, 0, unroll=UNROLL)

    def spread(m, carry):
        here = pl.ds(pl.multiple_of(m * 16, 16), 16)
        after = pl.ds(pl.multiple_of(8 + m * 16, 8), 16)
        r["p2"][here, 0:D] = r["shift"][here].astype(BF16)
        r["p2"][here, 2 * D :] = r["shift"][after].astype(BF16)
        return carry

    lax.fori_loop(0, ROWS // 16, spread, 0, unroll=UNROLL)


def third_layer(cot_ref, w2_ref, r):
    r["z2"][...] = mm(r["p2"][0:ROWS2], w2_ref[...], NT)
    row, column = iota((ROWS2, ROWS2), 0), iota((ROWS2, ROWS2), 1)
    order = jnp.where(column == (row % SEG) * F2 + row // SEG, 1.0, 0.0).astype(BF16)
    r["c2"][...] = mm(order, cot_ref[...], NN)
    limit = jnp.concatenate([r["info"][0:8, 0:1]] * 2, axis=0)
    tokens = jnp.concatenate([r["info"][8:16, 0:1]] * 2, axis=0)
    half = (iota((16, 1), 0) // 8).astype(F32)

    def body(m, carry):
        rows = pl.ds(pl.multiple_of(m * 16, 16), 16)
        normed, inverse, active, slope = norm_gelu(r["z2"][rows])
        frame = half + (2 * m).astype(F32)
        weight = jnp.where(frame < limit, tokens, 0.0)
        grad = r["c2"][rows] * weight * slope
        r["d2"][rows] = norm_back(grad, normed, inverse).astype(BF16)
        return carry

    lax.fori_loop(0, ROWS2 // 16, body, 0, unroll=UNROLL)


def grad_third(out_ref, r):
    out_ref[...] = mm(r["d2"][...], r["p2"][0:ROWS2], TN).astype(out_ref.dtype)


def back_second(w2_ref, r):
    r["u"][0:8] = jnp.zeros((8, 3 * D), F32)
    r["u"][8 + ROWS2 : 32 + ROWS2] = jnp.zeros((24, 3 * D), F32)
    r["u"][8 : 8 + ROWS2] = mm(r["d2"][...], w2_ref[...], NN)

    def even(m, carry):
        rows = pl.ds(pl.multiple_of(m * 16, 16), 16)
        after = pl.ds(pl.multiple_of(8 + m * 16, 8), 16)
        up = r["u"][after, 0:D] + r["u"][rows, 2 * D :]
        delta = norm_back(up * r["s1"][rows], r["z1"][rows], r["r1"][rows, 0:1])
        r["d1"][rows] = delta.astype(BF16)
        return carry

    lax.fori_loop(0, ROWS // 16, even, 0, unroll=UNROLL)

    def odd(m, carry):
        rows = pl.ds(pl.multiple_of(ROWS + m * 16, 16), 16)
        after = pl.ds(pl.multiple_of(8 + m * 16, 8), 16)
        up = r["u"][after, D : 2 * D]
        delta = norm_back(up * r["s1"][rows], r["z1"][rows], r["r1"][rows, 0:1])
        r["d1"][rows] = delta.astype(BF16)
        return carry

    lax.fori_loop(0, ROWS // 16, odd, 0, unroll=UNROLL)


def grad_second(out_ref, r):
    out_ref[...] = mm(r["d1"][...], r["p1"][...], TN).astype(out_ref.dtype)


def back_first(w1_ref, r):
    r["ue"][...] = mm(r["d1"][0:ROWS], w1_ref[...], NN)
    r["uo"][0:8] = jnp.zeros((8, 3 * D), F32)
    r["uo"][8:] = mm(r["d1"][ROWS:], w1_ref[...], NN)
    for c in range(4):

        def body(m, carry, c=c):
            here = pl.ds(pl.multiple_of(m * 16, 16), 16)
            after = pl.ds(pl.multiple_of(8 + m * 16, 8), 16)
            rows = pl.ds(pl.multiple_of(c * ROWS + m * 16, 16), 16)
            if c == 0:
                up = r["ue"][here, 0:D] + r["uo"][here, 2 * D :]
            elif c == 1:
                up = r["ue"][here, D : 2 * D]
            elif c == 2:
                up = r["ue"][here, 2 * D :] + r["uo"][after, 0:D]
            else:
                up = r["uo"][after, D : 2 * D]
            delta = norm_back(up * r["s0"][rows], r["z0"][rows], r["r0"][rows, 0:1])
            r["d0"][rows] = delta.astype(BF16)
            return carry

        lax.fori_loop(0, ROWS // 16, body, 0, unroll=UNROLL)


def grad_first(out_ref, r):
    found = mm(r["d0"][...], r["x4"][...], TN)
    found = found + pltpu.roll(found, 96, axis=1)
    found = jnp.where(iota((D, 128), 1) < 10, found, 0.0)
    out_ref[...] = found.astype(out_ref.dtype)


COMPUTE_SCRATCH = {
    "x4": ((4 * ROWS, 128), BF16),
    "z0": ((4 * ROWS, D), F32),
    "s0": ((4 * ROWS, D), F32),
    "r0": ((4 * ROWS, 128), F32),
    "d0": ((4 * ROWS, D), BF16),
    "info": ((16, 128), F32),
    "shift": ((ROWS + 8, D), F32),
    "p1": ((2 * ROWS, 3 * D), BF16),
    "z1": ((2 * ROWS, D), F32),
    "s1": ((2 * ROWS, D), F32),
    "r1": ((2 * ROWS, 128), F32),
    "d1": ((2 * ROWS, D), BF16),
    "p2": ((ROWS, 3 * D), BF16),
    "z2": ((ROWS2, D), F32),
    "c2": ((ROWS2, D), F32),
    "d2": ((ROWS2, D), BF16),
    "u": ((ROWS2 + 32, 3 * D), F32),
    "ue": ((ROWS, 3 * D), F32),
    "uo": ((ROWS + 8, 3 * D), F32),
}


def place():
    dp, batch = lax.axis_index("dp"), lax.axis_index("batch")
    return dp, batch, dp // 2, dp % 2, batch // 4, batch % 4


def signal_to(sem, dp, batch):
    pl.semaphore_signal(sem, inc=1, device_id=(dp, batch), device_id_type=pl.DeviceIdType.MESH)


def remote(src, dst, send, recv, dp, batch):
    return pltpu.make_async_remote_copy(
        src_ref=src,
        dst_ref=dst,
        send_sem=send,
        recv_sem=recv,
        device_id=(dp, batch),
        device_id_type=pl.DeviceIdType.MESH,
    )


def landed(ref, sem):
    pltpu.make_async_copy(ref, ref, sem).wait()


def loop(first, last, step):
    def body(i, carry):
        step(i)
        return carry

    lax.fori_loop(first, last, body, 0)


def pack_waves(wave, dest, length, tokens):
    high = wave.astype(BF16).astype(F32)
    low = wave - high
    lane, row = iota((SEG, 128), 1), iota((SEG, 128), 0)
    target = lane // 32 * 8 + (lane // 8) % 4
    extra = jnp.zeros((SEG, 128), F32)
    for s in range(SEG):
        here = dest[s]
        rank = 0
        for t in range(s):
            rank = rank + jnp.where(dest[t] == here, 1, 0)
        target = target + jnp.where(lane % 8 == s, here * 16 + rank * 4, 0)
        detail = jnp.where(lane == 126, length[s] - 256, tokens[s]).astype(F32)
        extra = jnp.where(row == s, detail, extra)
    rows = [high[:, 128 * i : 128 * i + 128] for i in range(4)]
    rows += [low[:, 128 * i : 128 * i + 128] for i in range(3)]
    rows.append(jnp.where(lane < 126, low[:, 384:], extra))
    data = jnp.concatenate(rows, axis=0).astype(BF16)
    select = jnp.where(iota((512, 64), 0) == target[0:1, 0:64], 1.0, 0.0).astype(BF16)
    return mm(select, data, NN).astype(BF16)


HALF = 768
CUT = 512
COUNT = D * 10 + 6 * D * D

SCRATCH = {
    "wave": ((SEG, D), F32),
    "w0t": ((10, 64), BF16),
    "cot": ((ROWS2, D), BF16),
    "mine0": ((64, 128), BF16),
    "send": ((32, 16, 128), BF16),
    "got": ((32, 16, 128), BF16),
    "f0": ((D, 128), BF16),
    "f1": ((D, 3 * D), BF16),
    "f2": ((D, 3 * D), BF16),
    "g0": ((D, 3 * D), BF16),
    "g1": ((D, 3 * D), BF16),
    "gf": ((D, 128), BF16),
    "rc0": ((4, 64, 3 * D), BF16),
    "rc1": ((4, 64, 3 * D), BF16),
    "rcf": ((4, 64, 128), BF16),
    "ys0": ((4, 64, 3 * D), BF16),
    "ys1": ((4, 64, 3 * D), BF16),
    "ysf": ((4, 64, 128), BF16),
    "yr0": ((4, 64, HALF), BF16),
    "yr1": ((4, 64, HALF), BF16),
    "yrf": ((4, 64, 128), BF16),
    "bx0": ((4, 4, 16, HALF), BF16),
    "bx1": ((4, 4, 16, HALF), BF16),
    "xs0": ((64, HALF), BF16),
    "xs1": ((64, HALF), BF16),
    "xsf": ((64, 128), BF16),
    "xr0": ((4, 16, HALF), BF16),
    "xr1": ((4, 16, HALF), BF16),
    "xrf": ((4, 16, 128), BF16),
    "by0": ((4, 16, HALF), BF16),
    "by1": ((4, 16, HALF), BF16),
    "bz0": ((4, 16, HALF), BF16),
    "bz1": ((4, 16, HALF), BF16),
    "zs0": ((8, 16, 256), BF16),
    "zs1": ((8, 16, 256), BF16),
    "zr0": ((8, 16, 256), BF16),
    "zr1": ((8, 16, 256), BF16),
    "fz0": ((8, 16, 256), BF16),
    "fz1": ((8, 16, 256), BF16),
    "fr0": ((4, 16, 3 * D), BF16),
    "fr1": ((4, 16, 3 * D + 128), BF16),
}
SCRATCH.update(COMPUTE_SCRATCH)
for kind in ("t", "s"):
    for axis, size in (("z", 8), ("x", 4), ("d", 8)):
        SCRATCH["all" + kind + axis] = ((size, 8, 128), F32)
        SCRATCH["my" + kind + axis] = ((8, 128), F32)

SEMS = {
    "load": 7,
    "wave": 0,
    "w0row": 4,
    "pass0": 4,
    "rowa": 8,
    "rowb": 8,
    "rowx": 32,
    "passa": 8,
    "passb": 8,
    "core": 12,
    "y": 12,
    "bx": 8,
    "x": 12,
    "by": 8,
    "z": 2,
    "fz": 2,
    "fx": 8,
    "sum": 6,
}


def whole_kernel(
    wave_in, dest_in, length_in, tokens_in, cot_in, w0_in, w1_in, w2_in,
    third_out, second_out, first_out, rms_out, dest, length, tokens, *rest,
):
    r = dict(zip(SCRATCH, rest))
    sems = rest[len(SCRATCH) :]
    sent = dict(zip(SEMS, sems[0::2]))
    came = dict(zip(SEMS, sems[1::2]))
    dp, batch, y, core, z, x = place()
    sibling = y * 2 + 1 - core

    def dp_peer(k):
        return lax.rem(dp + k, 8)

    def y_peer(k):
        return lax.rem(y + k, 4) * 2 + core

    def z_peer(k):
        return lax.rem(z + k, 8) * 4 + x

    def x_peer(k):
        return z * 4 + lax.rem(x + k, 4)

    def block(ref, who, start=0, width=3 * D):
        return ref.at[pl.ds(pl.multiple_of(who * 64, 64), 64), start : start + width]

    def quarter(ref, who, which, start, width):
        return ref.at[pl.ds(pl.multiple_of(who * 64 + which * 16, 16), 16), start : start + width]

    barrier = pltpu.get_barrier_semaphore()
    loads = [
        (wave_in, r["wave"]),
        (dest_in, dest),
        (length_in, length),
        (tokens_in, tokens),
        (cot_in, r["cot"]),
        (w0_in, r["w0t"]),
    ]
    loads = [pltpu.make_async_copy(a, b, came["load"].at[i]) for i, (a, b) in enumerate(loads)]
    full = (r["f1"], r["f2"])
    loads.append(pltpu.make_async_copy(w1_in, block(full[0], dp), came["load"].at[6]))
    loads.append(pltpu.make_async_copy(w2_in, block(full[1], dp), sent["load"].at[6]))
    for copy in loads:
        copy.start()
    loop(1, 32, lambda k: signal_to(barrier, dp, lax.rem(batch + k, 32)))
    loop(1, 8, lambda k: signal_to(barrier, dp_peer(k), batch))

    def sum_copy(kind, axis, k):
        which = 3 * (kind == "s") + "zxd".index(axis)
        mine, every = r["my" + kind + axis], r["all" + kind + axis]
        me = {"z": z, "x": x, "d": dp}[axis]
        to = {"z": (dp, z_peer(k)), "x": (dp, x_peer(k)), "d": (dp_peer(k), batch)}[axis]
        return remote(mine, every.at[me], sent["sum"].at[which], came["sum"].at[which], *to)

    def sum_start(kind, axis, value):
        size = 4 if axis == "x" else 8
        r["my" + kind + axis][...] = value
        loop(1, size, lambda k: sum_copy(kind, axis, k).start())
        r["all" + kind + axis][{"z": z, "x": x, "d": dp}[axis]] = value

    def sum_end(kind, axis):
        size = 4 if axis == "x" else 8
        every = r["all" + kind + axis]
        landed(every.at[0 : size - 1], came["sum"].at[3 * (kind == "s") + "zxd".index(axis)])
        return jnp.sum(every[...], axis=0)

    def sum_sent(kind, axis):
        size = 4 if axis == "x" else 8
        every = r["all" + kind + axis]
        landed(every.at[0 : size - 1], sent["sum"].at[3 * (kind == "s") + "zxd".index(axis)])

    for i in range(6):
        loads[i].wait()
    total = tokens[0]
    for s in range(1, SEG):
        total = total + tokens[s]
    eye = jnp.where(iota((10, 128), 0) == iota((10, 128), 1), 1.0, 0.0).astype(BF16)
    r["mine0"][...] = mm(r["w0t"][...], eye, TN).astype(BF16)
    r["send"][...] = pack_waves(r["wave"][...], dest, length, tokens).reshape(32, 16, 128)
    loads[6].wait()
    loads[7].wait()
    pl.semaphore_wait(barrier, 38)

    def wave_copy(k):
        to = lax.rem(batch + k, 32)
        return remote(r["send"].at[to], r["got"].at[batch], sent["wave"], came["wave"], dp, to)

    def w0_copy(k):
        return remote(
            r["mine0"], block(r["f0"], dp, 0, 128), sent["w0row"].at[k], came["w0row"].at[k], y_peer(k), batch
        )

    def pass0_copy(k):
        owner = y_peer(4 - k)
        here = block(r["f0"], owner, 0, 128)
        source = here if k else r["mine0"]
        return remote(source, here, sent["pass0"].at[k], came["pass0"].at[k], sibling, batch)

    def rowa_copy(w, k):
        here = block(full[w], dp, 0, CUT)
        return remote(here, here, sent["rowa"].at[w * 4 + k], came["rowa"].at[w * 4 + k], y_peer(k), batch)

    def rowb_copy(w, k):
        here = quarter(full[w], dp, x, CUT, 3 * D - CUT)
        return remote(here, here, sent["rowb"].at[w * 4 + k], came["rowb"].at[w * 4 + k], y_peer(k), batch)

    def rowx_copy(w, k, j):
        here = quarter(full[w], y_peer(4 - k), x, CUT, 3 * D - CUT)
        at = w * 16 + k * 4 + j
        return remote(here, here, sent["rowx"].at[at], came["rowx"].at[at], dp, x_peer(j))

    def passa_copy(w, k):
        here = block(full[w], y_peer(4 - k), 0, CUT)
        return remote(here, here, sent["passa"].at[w * 4 + k], came["passa"].at[w * 4 + k], sibling, batch)

    def passb_copy(w, k):
        here = block(full[w], y_peer(4 - k), CUT, 3 * D - CUT)
        return remote(here, here, sent["passb"].at[w * 4 + k], came["passb"].at[w * 4 + k], sibling, batch)

    loop(1, 32, lambda k: wave_copy(k).start())
    for k in (2, 1, 3):
        w0_copy(k).start()
    for w in range(2):
        for k in (2, 1, 3):
            rowb_copy(w, k).start()
    for w in range(2):
        for k in (2, 1, 3):
            rowa_copy(w, k).start()
    pass0_copy(0).start()
    for w in range(2):
        passa_copy(w, 0).start()
        passb_copy(w, 0).start()
    r["got"][batch] = r["send"][batch]
    block(r["f0"], dp, 0, 128)[...] = r["mine0"][...]
    sum_start("t", "z", jnp.broadcast_to(total.astype(F32), (8, 128)))
    for k in (1, 3, 2):
        w0_copy(k).wait_recv()
        pass0_copy(k).start()
    for w in range(2):
        for k in (1, 3, 2):
            rowb_copy(w, k).wait_recv()
            for j in (2, 1, 3):
                rowx_copy(w, k, j).start()

    def pass_on(w):
        for k in (1, 3, 2):
            rowa_copy(w, k).wait_recv()
            passa_copy(w, k).start()
        for k in (1, 3, 2):
            for j in (1, 3, 2):
                rowx_copy(w, k, j).wait_recv()
            passb_copy(w, k).start()

    def gathered(w):
        for k in range(4):
            passa_copy(w, k).wait_recv()
            passb_copy(w, k).wait_recv()

    landed(r["send"].at[0:31], came["wave"])
    for k in range(4):
        pass0_copy(k).wait_recv()
    forward_first(r["got"][...].reshape(512, 128), r["f0"], r)
    pass_on(0)
    sum_start("t", "x", sum_end("t", "z"))
    gathered(0)
    forward_second(full[0], r)
    pass_on(1)
    sum_start("t", "d", sum_end("t", "x"))
    gathered(1)

    def core_copy(p, k):
        step = lax.rem(y + k, 4)
        grads = r["g" + str(p)]
        width = 128 if p == "f" else 3 * D
        at = (2 if p == "f" else p) * 4 + k
        return remote(
            block(grads, step * 2 + 1 - core, 0, width), r["rc" + str(p)].at[step],
            sent["core"].at[at], came["core"].at[at], sibling, batch,
        )

    def y_copy(p, k):
        to = lax.rem(y + k, 4)
        width = 128 if p == "f" else HALF
        at = (2 if p == "f" else p) * 4 + k
        return remote(
            r["ys" + str(p)].at[to, :, 0:width], r["yr" + str(p)].at[y],
            sent["y"].at[at], came["y"].at[at], to * 2 + core, batch,
        )

    def bx_copy(p, k):
        to = lax.rem(x + k, 4)
        rows = pl.ds(pl.multiple_of(to * 16, 16), 16)
        return remote(
            r["ys" + str(p)].at[:, rows, HALF:], r["bx" + str(p)].at[x],
            sent["bx"].at[p * 4 + k], came["bx"].at[p * 4 + k], dp, z * 4 + to,
        )

    def x_copy(p, k):
        to = lax.rem(x + k, 4)
        rows = pl.ds(pl.multiple_of(to * 16, 16), 16)
        at = (2 if p == "f" else p) * 4 + k
        return remote(
            r["xs" + str(p)].at[rows], r["xr" + str(p)].at[x],
            sent["x"].at[at], came["x"].at[at], dp, z * 4 + to,
        )

    def by_copy(p, k):
        to = lax.rem(y + k, 4)
        return remote(
            r["by" + str(p)].at[to], r["bz" + str(p)].at[y],
            sent["by"].at[p * 4 + k], came["by"].at[p * 4 + k], to * 2 + core, batch,
        )

    def z_copy(p, k):
        to = lax.rem(z + k, 8)
        return remote(
            r["zs" + str(p)].at[to], r["zr" + str(p)].at[z], sent["z"].at[p], came["z"].at[p], dp, z_peer(k)
        )

    def fz_copy(p, k):
        here = r["fz" + str(p)].at[z]
        return remote(here, here, sent["fz"].at[p], came["fz"].at[p], dp, z_peer(k))

    def fx_copy(p, k):
        here = r["fr" + str(p)].at[x]
        return remote(here, here, sent["fx"].at[p * 4 + k], came["fx"].at[p * 4 + k], dp, x_peer(k))

    def core_start(p):
        for k in (2, 1, 3, 0):
            core_copy(p, k).start()

    def core_end(p):
        for k in (2, 1, 3, 0):
            step = lax.rem(y + k, 4)
            core_copy(p, k).wait_recv()
            for m in range(4):
                rows = pl.ds(pl.multiple_of((step * 2 + core) * 64 + m * 16, 16), 16)
                here = slice(m * 16, m * 16 + 16)
                own = r["g" + str(p)][rows].astype(F32)
                r["ys" + str(p)][step, here] = (own + r["rc" + str(p)][step, here].astype(F32)).astype(BF16)
            if k:
                y_copy(p, k).start()
        if p != "f":
            for k in (2, 1, 3):
                bx_copy(p, k).start()

    def y_end(p):
        width = 128 if p == "f" else HALF
        for k in (1, 3, 2):
            y_copy(p, k).wait_recv()
        for m in range(4):
            here = slice(m * 16, m * 16 + 16)
            found = r["ys" + str(p)][y, here, 0:width].astype(F32)
            for k in (1, 2, 3):
                found = found + r["yr" + str(p)][lax.rem(y + k, 4), here].astype(F32)
            r["xs" + str(p)][here] = found.astype(BF16)
        for k in (2, 1, 3):
            x_copy(p, k).start()

    def bx_end(p):
        for k in (1, 3, 2):
            bx_copy(p, k).wait_recv()
        rows = pl.ds(pl.multiple_of(x * 16, 16), 16)
        for step in range(4):
            found = r["ys" + str(p)][step, rows, HALF:].astype(F32)
            for k in (1, 2, 3):
                found = found + r["bx" + str(p)][lax.rem(x + k, 4), step].astype(F32)
            r["by" + str(p)][step] = found.astype(BF16)
        for k in (2, 1, 3):
            by_copy(p, k).start()

    def x_end(p):
        for k in (1, 3, 2):
            x_copy(p, k).wait_recv()
        found = r["xs" + str(p)][pl.ds(pl.multiple_of(x * 16, 16), 16)].astype(F32)
        for k in (1, 2, 3):
            found = found + r["xr" + str(p)][lax.rem(x + k, 4)].astype(F32)
        return found

    def by_end(p):
        for k in (1, 3, 2):
            by_copy(p, k).wait_recv()
        found = r["by" + str(p)][y].astype(F32)
        for k in (1, 2, 3):
            found = found + r["bz" + str(p)][lax.rem(y + k, 4)].astype(F32)
        return found

    def z_start(p):
        low, high = x_end(p), by_end(p)
        out = r["zs" + str(p)]
        for q in range(3):
            out[q] = low[:, q * 256 : q * 256 + 256].astype(BF16)
            out[q + 3] = high[:, q * 256 : q * 256 + 256].astype(BF16)
        out[6] = jnp.zeros((16, 256), BF16)
        out[7] = jnp.zeros((16, 256), BF16)
        if p == 1:
            out[6, :, 0:128] = x_end("f").astype(BF16)
        loop(1, 8, lambda k: z_copy(p, k).start())
        r["zr" + str(p)][z] = out[z]

    def z_end(p):
        landed(r["zr" + str(p)].at[0:7], came["z"].at[p])
        found = jnp.sum(r["zr" + str(p)][...].astype(F32), axis=0)
        r["fz" + str(p)][z] = found.astype(BF16)
        loop(1, 8, lambda k: fz_copy(p, k).start())
        return found

    def fx_start(p):
        landed(r["fz" + str(p)].at[0:7], came["fz"].at[p])
        out = r["fr" + str(p)]
        for q in range(6):
            out[x, :, q * 256 : q * 256 + 256] = r["fz" + str(p)][q]
        if p == 1:
            out[x, :, 3 * D :] = r["fz1"][6, :, 0:128]
        for k in (2, 1, 3):
            fx_copy(p, k).start()

    third_layer(r["cot"], full[1], r)
    grad_third(r["g0"], r)
    core_start(0)
    back_second(full[1], r)
    core_end(0)
    grad_second(r["g1"], r)
    core_start(1)
    back_first(full[0], r)
    core_end(1)
    grad_first(r["gf"], r)
    core_start("f")
    y_end(0)
    bx_end(0)
    core_end("f")
    token_sum = sum_end("t", "d")
    per_token = (1.0 / token_sum)[0:1, 0:1]
    z_start(0)
    y_end(1)
    bx_end(1)
    y_end("f")
    found = z_end(0) * per_token
    squares = jnp.sum(found * found, keepdims=True)
    z_start(1)
    fx_start(0)
    found = z_end(1) * per_token
    squares = squares + jnp.sum(found * found, keepdims=True)
    sum_start("s", "z", jnp.broadcast_to(squares, (8, 128)))
    fx_start(1)
    sum_start("s", "x", sum_end("s", "z"))
    sum_start("s", "d", sum_end("s", "x"))
    rms = jnp.sqrt(sum_end("s", "d") * (1.0 / COUNT))
    factor = (1.0 / (token_sum * jnp.maximum(rms, 1.0)))[0:1, 0:1]
    for k in (1, 3, 2):
        fx_copy(0, k).wait_recv()
    third_out[...] = r["fr0"][...].reshape(64, 3 * D).astype(F32) * factor
    for k in (1, 3, 2):
        fx_copy(1, k).wait_recv()
    second_out[...] = r["fr1"][:, :, 0 : 3 * D].reshape(64, 3 * D).astype(F32) * factor
    first = r["fr1"][:, :, 3 * D :].reshape(64, 128).astype(F32) * factor
    square = jnp.concatenate([first, jnp.zeros((64, 128), F32)], axis=0)
    first_out[...] = square.T[0:10, 0:64]
    rms_out[...] = rms

    landed(r["send"].at[0:31], sent["wave"])
    for k in range(4):
        pass0_copy(k).wait_send()
        if k:
            w0_copy(k).wait_send()
        for w in range(2):
            passa_copy(w, k).wait_send()
            passb_copy(w, k).wait_send()
            if k:
                rowa_copy(w, k).wait_send()
                rowb_copy(w, k).wait_send()
                for j in range(1, 4):
                    rowx_copy(w, k, j).wait_send()
        for p in (0, 1, "f"):
            core_copy(p, k).wait_send()
            if k:
                y_copy(p, k).wait_send()
                x_copy(p, k).wait_send()
                if p != "f":
                    bx_copy(p, k).wait_send()
                    by_copy(p, k).wait_send()
                    fx_copy(p, k).wait_send()
    for p in range(2):
        landed(r["zr" + str(p)].at[0:7], sent["z"].at[p])
        landed(r["fz" + str(p)].at[0:7], sent["fz"].at[p])
    for kind in "ts":
        for axis in "zxd":
            sum_sent(kind, axis)


def whole(wave, dest, length, tokens, cot, w0, w1, w2):
    vmem = pl.BlockSpec(memory_space=pltpu.VMEM)
    anywhere = pl.BlockSpec(memory_space=pl.ANY)
    sems = []
    for count in SEMS.values():
        sems += [pltpu.SemaphoreType.DMA((count,)) if count else pltpu.SemaphoreType.DMA] * 2
    return pl.pallas_call(
        whole_kernel,
        out_shape=(
            jax.ShapeDtypeStruct((64, 3 * D), F32),
            jax.ShapeDtypeStruct((64, 3 * D), F32),
            jax.ShapeDtypeStruct((10, 64), F32),
            jax.ShapeDtypeStruct((8, 128), F32),
        ),
        in_specs=[anywhere] * 8,
        out_specs=(vmem,) * 4,
        scratch_shapes=[pltpu.SMEM((SEG,), jnp.int32)] * 3
        + [pltpu.VMEM(s, t) for s, t in SCRATCH.values()]
        + sems,
        compiler_params=pltpu.CompilerParams(
            collective_id=0, has_side_effects=True, vmem_limit_bytes=58 << 20
        ),
        cost_estimate=pl.CostEstimate(flops=3000000000, bytes_accessed=3000000, transcendentals=1400000),
    )(wave, dest, length, tokens, cot, w0, w1, w2)


def local(wave, length, dest, tokens, cot, w0, w1, w2):
    third, second, first, rms = whole(
        wave, dest, length, tokens, cot.reshape(ROWS2, D), w0.T, w1, w2
    )
    return first.T, second, third, rms[0, 0:1]


def solution(mesh):
    row = P(("dp", "batch"))
    return jax.shard_map(
        local,
        mesh=mesh,
        in_specs=(row, row, row, row, row, P("dp"), P("dp"), P("dp")),
        out_specs=(P("dp"), P("dp"), P("dp"), P()),
        check_vma=False,
    )
```

```python
import functools

import jax
import jax.numpy as jnp
from jax import lax
from jax.experimental import pallas as pl
from jax.experimental.pallas import tpu as pltpu
from jax.sharding import PartitionSpec as P

F32 = jnp.float32
BF16 = jnp.bfloat16
D = 512
SEG = 8
J = 26
ROWS = J * SEG
F2 = 24
UNROLL = True
ROWS2 = F2 * SEG
NT = (((1,), (1,)), ((), ()))
TN = (((0,), (0,)), ((), ()))
NN = (((1,), (0,)), ((), ()))


def mm(a, b, dims):
    return lax.dot_general(a, b, dims, preferred_element_type=F32)


def iota(shape, dim):
    return lax.broadcasted_iota(jnp.int32, shape, dim)


def mean(x):
    return jnp.sum(x, axis=-1, keepdims=True) * (1.0 / D)


def norm_gelu(hidden):
    centred = hidden - mean(hidden)
    inverse = lax.rsqrt(mean(centred * centred) + 1e-05)
    normed = centred * inverse
    cdf = 0.5 + 0.5 * lax.erf(normed * 0.7071067811865476)
    slope = cdf + normed * jnp.exp(-0.5 * normed * normed) * 0.3989422804014327
    return normed, inverse, normed * cdf, slope


def norm_back(grad, normed, inverse):
    return inverse * (grad - mean(grad) - normed * mean(grad * normed))


def pick_waves(got):
    lane_pick = (iota((SEG, 128), 1) == 127).astype(BF16)
    token_row = mm(lane_pick, got, NT)
    column = iota((SEG, 512), 1)
    carries = jnp.logical_and(column % 16 >= 8, column % 4 == 3)
    filled = jnp.where(jnp.logical_and(carries, token_row > 0.5), 1.0, 0.0).astype(BF16)
    row_slot = iota((512, 512), 0)
    row_slot = (row_slot // 16) * 2 + (row_slot // 4) % 2
    column_slot = iota((512, 512), 1)
    column_slot = (column_slot // 16) * 2 + (column_slot // 4) % 2
    weight = jnp.where(row_slot < column_slot, 1.0, 0.0) + jnp.where(
        row_slot == column_slot, 64.0, 0.0
    )
    place = mm(filled, weight.astype(BF16), NN) - 64.0
    target = place + ((column // 8) % 2 * 32 + (column % 4) * 8).astype(F32)
    target = jnp.where(place > -0.5, target, -1.0)
    picking = jnp.where(iota((64, 512), 0).astype(F32) == target[0:1], 1.0, 0.0).astype(BF16)
    picked = mm(picking, got, NN)
    last = picked[56:64]
    length = last[:, 126:127] + 256.0
    tokens = last[:, 127:128]
    low_last = jnp.where(iota((SEG, 128), 1) < 126, last, 0.0)
    pieces = [picked[8 * i : 8 * i + 8] + picked[32 + 8 * i : 40 + 8 * i] for i in range(3)]
    pieces.append(picked[24:32] + low_last)
    return jnp.concatenate(pieces, axis=1), length, tokens


def first_taps(wave, length):
    inside = iota((SEG, D), 1).astype(F32) < length
    average = jnp.sum(jnp.where(inside, wave, 0.0), axis=1, keepdims=True) / length
    centred = jnp.where(inside, wave - average, 0.0)
    variance = jnp.sum(centred * centred, axis=1, keepdims=True) / length
    normal = centred * lax.rsqrt(variance + 1e-07)
    padded = jnp.concatenate([normal, jnp.zeros((SEG, 256), F32)], axis=1)
    rows = []
    for j in range(J):
        tile, shift = (20 * j) // 128, (20 * j) % 128
        pair = padded[:, tile * 128 : tile * 128 + 256]
        if shift:
            pair = pltpu.roll(pair, 256 - shift, axis=1)
        rows.append(pair[:, :128])
    taps = jnp.concatenate(rows, axis=0)
    return jnp.where(iota((ROWS, 128), 1) < 32, taps, 0.0)


def forward_first(got, w0_ref, r):
    wave, length, tokens = pick_waves(got)
    taps = first_taps(wave, length)
    high = taps.astype(BF16).astype(F32)
    both = high + pltpu.roll(taps - high, 32, axis=1)
    both_narrow = both.astype(BF16)
    narrow_lane = iota((ROWS, 128), 1)
    for c in range(4):
        moved = pltpu.roll(both, 128 - 5 * c, axis=1) if c else both
        keep = narrow_lane % 32 < 10
        moved = jnp.where(jnp.logical_and(keep, narrow_lane < 64), moved, 0.0)
        r["x4"][c * ROWS : (c + 1) * ROWS] = moved.astype(BF16)
    w0 = w0_ref[...]
    tap_row, tap_column = iota((128, 128), 0), iota((128, 128), 1)
    for c in range(4):
        placing = jnp.logical_and(tap_row % 32 == tap_column + 5 * c, tap_row < 64)
        placing = jnp.logical_and(placing, tap_column < 10)
        weight = mm(jnp.where(placing, 1.0, 0.0).astype(BF16), w0, NT).astype(BF16)
        r["z0"][c * ROWS : (c + 1) * ROWS] = mm(both_narrow, weight, NN)
    l2 = ((((length - 10.0) * 0.2).astype(jnp.int32) + 1 - 3) // 2 + 1 - 3) // 2 + 1
    r["info"][0:8] = jnp.broadcast_to(l2.astype(F32), (SEG, 128))
    r["info"][8:16] = jnp.broadcast_to(tokens, (SEG, 128))

    for c in range(4):

        def body(m, carry, c=c):
            at = pl.multiple_of(m * 16, 16)
            rows = pl.ds(pl.multiple_of(c * ROWS + m * 16, 16), 16)
            here = pl.ds(at, 16)
            normed, inverse, active, slope = norm_gelu(r["z0"][rows])
            r["z0"][rows] = normed
            r["s0"][rows] = slope
            r["r0"][rows] = jnp.broadcast_to(inverse, (16, 128))
            narrow = active.astype(BF16)
            if c < 3:
                r["p1"][here, c * D : (c + 1) * D] = narrow
            if c == 0:
                r["shift"][here] = active
            else:
                odd = pl.ds(pl.multiple_of(ROWS + m * 16, 16), 16)
                if c >= 2:
                    r["p1"][odd, (c - 2) * D : (c - 1) * D] = narrow
            return carry

        lax.fori_loop(0, ROWS // 16, body, 0, unroll=UNROLL)
    r["shift"][ROWS : ROWS + 8] = jnp.zeros((8, D), F32)

    def shifted(m, carry):
        rows = pl.ds(pl.multiple_of(8 + m * 16, 8), 16)
        odd = pl.ds(pl.multiple_of(ROWS + m * 16, 16), 16)
        r["p1"][odd, 2 * D :] = r["shift"][rows].astype(BF16)
        return carry

    lax.fori_loop(0, ROWS // 16, shifted, 0, unroll=UNROLL)


def forward_second(w1_ref, r):
    r["z1"][...] = mm(r["p1"][...], w1_ref[...], NT)

    def even(m, carry):
        rows = pl.ds(pl.multiple_of(m * 16, 16), 16)
        normed, inverse, active, slope = norm_gelu(r["z1"][rows])
        r["z1"][rows] = normed
        r["s1"][rows] = slope
        r["r1"][rows] = jnp.broadcast_to(inverse, (16, 128))
        r["shift"][rows] = active
        return carry

    lax.fori_loop(0, ROWS // 16, even, 0, unroll=UNROLL)

    def odd(m, carry):
        rows = pl.ds(pl.multiple_of(ROWS + m * 16, 16), 16)
        here = pl.ds(pl.multiple_of(m * 16, 16), 16)
        normed, inverse, active, slope = norm_gelu(r["z1"][rows])
        r["z1"][rows] = normed
        r["s1"][rows] = slope
        r["r1"][rows] = jnp.broadcast_to(inverse, (16, 128))
        r["p2"][here, D : 2 * D] = active.astype(BF16)
        return carry

    lax.fori_loop(0, ROWS // 16, odd, 0, unroll=UNROLL)

    def spread(m, carry):
        here = pl.ds(pl.multiple_of(m * 16, 16), 16)
        after = pl.ds(pl.multiple_of(8 + m * 16, 8), 16)
        r["p2"][here, 0:D] = r["shift"][here].astype(BF16)
        r["p2"][here, 2 * D :] = r["shift"][after].astype(BF16)
        return carry

    lax.fori_loop(0, ROWS // 16, spread, 0, unroll=UNROLL)


def third_layer(cot_ref, w2_ref, r):
    r["z2"][...] = mm(r["p2"][0:ROWS2], w2_ref[...], NT)
    row, column = iota((ROWS2, ROWS2), 0), iota((ROWS2, ROWS2), 1)
    order = jnp.where(column == (row % SEG) * F2 + row // SEG, 1.0, 0.0).astype(BF16)
    r["c2"][...] = mm(order, cot_ref[...], NN)
    limit = jnp.concatenate([r["info"][0:8, 0:1]] * 2, axis=0)
    tokens = jnp.concatenate([r["info"][8:16, 0:1]] * 2, axis=0)
    half = (iota((16, 1), 0) // 8).astype(F32)

    def body(m, carry):
        rows = pl.ds(pl.multiple_of(m * 16, 16), 16)
        normed, inverse, active, slope = norm_gelu(r["z2"][rows])
        frame = half + (2 * m).astype(F32)
        weight = jnp.where(frame < limit, tokens, 0.0)
        grad = r["c2"][rows] * weight * slope
        r["d2"][rows] = norm_back(grad, normed, inverse).astype(BF16)
        return carry

    lax.fori_loop(0, ROWS2 // 16, body, 0, unroll=UNROLL)


def grad_third(rows, r):
    r["g0"][rows] = mm(r["d2"][:, rows], r["p2"][0:ROWS2], TN).astype(BF16)


def back_second(w2_ref, r):
    r["u"][0:8] = jnp.zeros((8, 3 * D), F32)
    r["u"][8 + ROWS2 : 32 + ROWS2] = jnp.zeros((24, 3 * D), F32)
    r["u"][8 : 8 + ROWS2] = mm(r["d2"][...], w2_ref[...], NN)

    def even(m, carry):
        rows = pl.ds(pl.multiple_of(m * 16, 16), 16)
        after = pl.ds(pl.multiple_of(8 + m * 16, 8), 16)
        up = r["u"][after, 0:D] + r["u"][rows, 2 * D :]
        delta = norm_back(up * r["s1"][rows], r["z1"][rows], r["r1"][rows, 0:1])
        r["d1"][rows] = delta.astype(BF16)
        return carry

    lax.fori_loop(0, ROWS // 16, even, 0, unroll=UNROLL)

    def odd(m, carry):
        rows = pl.ds(pl.multiple_of(ROWS + m * 16, 16), 16)
        after = pl.ds(pl.multiple_of(8 + m * 16, 8), 16)
        up = r["u"][after, D : 2 * D]
        delta = norm_back(up * r["s1"][rows], r["z1"][rows], r["r1"][rows, 0:1])
        r["d1"][rows] = delta.astype(BF16)
        return carry

    lax.fori_loop(0, ROWS // 16, odd, 0, unroll=UNROLL)


def grad_second(rows, r):
    r["g1"][rows] = mm(r["d1"][:, rows], r["p1"][...], TN).astype(BF16)


def back_first(w1_ref, r):
    r["ue"][...] = mm(r["d1"][0:ROWS], w1_ref[...], NN)
    r["uo"][0:8] = jnp.zeros((8, 3 * D), F32)
    r["uo"][8:] = mm(r["d1"][ROWS:], w1_ref[...], NN)
    for c in range(4):

        def body(m, carry, c=c):
            here = pl.ds(pl.multiple_of(m * 16, 16), 16)
            after = pl.ds(pl.multiple_of(8 + m * 16, 8), 16)
            rows = pl.ds(pl.multiple_of(c * ROWS + m * 16, 16), 16)
            if c == 0:
                up = r["ue"][here, 0:D] + r["uo"][here, 2 * D :]
            elif c == 1:
                up = r["ue"][here, D : 2 * D]
            elif c == 2:
                up = r["ue"][here, 2 * D :] + r["uo"][after, 0:D]
            else:
                up = r["uo"][after, D : 2 * D]
            delta = norm_back(up * r["s0"][rows], r["z0"][rows], r["r0"][rows, 0:1])
            r["d0"][rows] = delta.astype(BF16)
            return carry

        lax.fori_loop(0, ROWS // 16, body, 0, unroll=UNROLL)


def grad_first(out_ref, r):
    found = mm(r["d0"][...], r["x4"][...], TN)
    found = found + pltpu.roll(found, 96, axis=1)
    found = jnp.where(iota((D, 128), 1) < 10, found, 0.0)
    out_ref[...] = found.astype(out_ref.dtype)


COMPUTE_SCRATCH = {
    "x4": ((4 * ROWS, 128), BF16),
    "z0": ((4 * ROWS, D), F32),
    "s0": ((4 * ROWS, D), F32),
    "r0": ((4 * ROWS, 128), F32),
    "d0": ((4 * ROWS, D), BF16),
    "info": ((16, 128), F32),
    "shift": ((ROWS + 8, D), F32),
    "p1": ((2 * ROWS, 3 * D), BF16),
    "z1": ((2 * ROWS, D), F32),
    "s1": ((2 * ROWS, D), F32),
    "r1": ((2 * ROWS, 128), F32),
    "d1": ((2 * ROWS, D), BF16),
    "p2": ((ROWS, 3 * D), BF16),
    "z2": ((ROWS2, D), F32),
    "c2": ((ROWS2, D), F32),
    "d2": ((ROWS2, D), BF16),
    "u": ((ROWS2 + 32, 3 * D), F32),
    "ue": ((ROWS, 3 * D), F32),
    "uo": ((ROWS + 8, 3 * D), F32),
}


def place():
    dp, batch = lax.axis_index("dp"), lax.axis_index("batch")
    return dp, batch, dp // 2, dp % 2, batch // 4, batch % 4


def signal_to(sem, dp, batch):
    pl.semaphore_signal(sem, inc=1, device_id=(dp, batch), device_id_type=pl.DeviceIdType.MESH)


def remote(src, dst, send, recv, dp, batch):
    return pltpu.make_async_remote_copy(
        src_ref=src,
        dst_ref=dst,
        send_sem=send,
        recv_sem=recv,
        device_id=(dp, batch),
        device_id_type=pl.DeviceIdType.MESH,
    )


def landed(ref, sem):
    pltpu.make_async_copy(ref, ref, sem).wait()


def loop(first, last, step):
    def body(i, carry):
        step(i)
        return carry

    lax.fori_loop(first, last, body, 0)


def pack_waves(wave, dest, length, tokens):
    high = wave.astype(BF16).astype(F32)
    low = wave - high
    lane, row = iota((SEG, 128), 1), iota((SEG, 128), 0)
    target = lane // 32 * 8 + (lane // 8) % 4
    extra = jnp.zeros((SEG, 128), F32)
    for s in range(SEG):
        here = dest[s]
        rank = 0
        for t in range(s):
            rank = rank + jnp.where(dest[t] == here, 1, 0)
        target = target + jnp.where(lane % 8 == s, here * 16 + rank * 4, 0)
        detail = jnp.where(lane == 126, length[s] - 256, tokens[s]).astype(F32)
        extra = jnp.where(row == s, detail, extra)
    rows = [high[:, 128 * i : 128 * i + 128] for i in range(4)]
    rows += [low[:, 128 * i : 128 * i + 128] for i in range(3)]
    rows.append(jnp.where(lane < 126, low[:, 384:], extra))
    data = jnp.concatenate(rows, axis=0).astype(BF16)
    select = jnp.where(iota((512, 64), 0) == target[0:1, 0:64], 1.0, 0.0).astype(BF16)
    return mm(select, data, NN).astype(BF16)


HALF = 768
CUT = 768
COUNT = D * 10 + 6 * D * D

SCRATCH = {
    "wave": ((SEG, D), F32),
    "w0t": ((10, 64), BF16),
    "cot": ((ROWS2, D), BF16),
    "mine0": ((64, 128), BF16),
    "send": ((32, 16, 128), BF16),
    "got": ((32, 16, 128), BF16),
    "f0": ((D, 128), BF16),
    "f1": ((D, 3 * D), BF16),
    "f2": ((D, 3 * D), BF16),
    "g0": ((D, 3 * D), BF16),
    "g1": ((D, 3 * D), BF16),
    "gf": ((D, 128), BF16),
    "rc0": ((4, 64, 3 * D), BF16),
    "rc1": ((4, 64, 3 * D), BF16),
    "rcf": ((4, 64, 128), BF16),
    "ys0": ((4, 64, 3 * D), BF16),
    "ys1": ((4, 64, 3 * D), BF16),
    "ysf": ((4, 64, 128), BF16),
    "yr0": ((4, 64, HALF), BF16),
    "yr1": ((4, 64, HALF), BF16),
    "yrf": ((4, 64, 128), BF16),
    "bx0": ((4, 4, 16, HALF), BF16),
    "bx1": ((4, 4, 16, HALF), BF16),
    "xs0": ((64, HALF), BF16),
    "xs1": ((64, HALF), BF16),
    "xsf": ((64, 128), BF16),
    "xr0": ((4, 16, HALF), BF16),
    "xr1": ((4, 16, HALF), BF16),
    "xrf": ((4, 16, 128), BF16),
    "by0": ((4, 16, HALF), BF16),
    "by1": ((4, 16, HALF), BF16),
    "bz0": ((4, 16, HALF), BF16),
    "bz1": ((4, 16, HALF), BF16),
    "zs0": ((8, 16, 256), BF16),
    "zs1": ((8, 16, 256), BF16),
    "zr0": ((8, 16, 256), BF16),
    "zr1": ((8, 16, 256), BF16),
    "fz0": ((8, 16, 256), BF16),
    "fz1": ((8, 16, 256), BF16),
}
SCRATCH.update(COMPUTE_SCRATCH)
for kind in ("t", "s"):
    for axis in "zg":
        SCRATCH["all" + kind + axis] = ((16, 8, 128), F32)
        SCRATCH["my" + kind + axis] = ((8, 128), F32)

SEMS = {
    "load": 7,
    "wave": 0,
    "w0row": 4,
    "pass0": 4,
    "rowa": 8,
    "rowb": 8,
    "rowx": 32,
    "passa": 8,
    "passb": 8,
    "core": 12,
    "y": 12,
    "bx": 8,
    "x": 12,
    "by": 8,
    "z": 2,
    "fz": 2,
    "fx": 8,
    "sum": 4,
}


def whole_kernel(
    wave_in, dest_in, length_in, tokens_in, cot_in, w0_in, w1_in, w2_in,
    third_out, second_out, stat_out, dest, length, tokens, *rest,
):
    r = dict(zip(SCRATCH, rest), fr0=third_out, fr1=second_out)
    sems = rest[len(SCRATCH) :]
    sent = dict(zip(SEMS, sems[0::2]))
    came = dict(zip(SEMS, sems[1::2]))
    dp, batch, y, core, z, x = place()
    sibling = y * 2 + 1 - core

    column, plane = z * 2 + core, y * 4 + x

    def column_peer(k):
        other = lax.rem(column + k, 16)
        return y * 2 + other % 2, other // 2 * 4 + x

    def plane_peer(k):
        other = lax.rem(plane + k, 16)
        return other // 4 * 2 + core, z * 4 + other % 4

    def y_peer(k):
        return lax.rem(y + k, 4) * 2 + core

    def z_peer(k):
        return lax.rem(z + k, 8) * 4 + x

    def x_peer(k):
        return z * 4 + lax.rem(x + k, 4)

    def block(ref, who, start=0, width=3 * D):
        return ref.at[pl.ds(pl.multiple_of(who * 64, 64), 64), start : start + width]

    def quarter(ref, who, which, start, width):
        return ref.at[pl.ds(pl.multiple_of(who * 64 + which * 16, 16), 16), start : start + width]

    barrier = pltpu.get_barrier_semaphore()
    loads = [
        (wave_in, r["wave"]),
        (dest_in, dest),
        (length_in, length),
        (tokens_in, tokens),
        (cot_in, r["cot"]),
        (w0_in, r["w0t"]),
    ]
    loads = [pltpu.make_async_copy(a, b, came["load"].at[i]) for i, (a, b) in enumerate(loads)]
    full = (r["f1"], r["f2"])
    loads.append(pltpu.make_async_copy(w1_in, block(full[0], dp), came["load"].at[6]))
    loads.append(pltpu.make_async_copy(w2_in, block(full[1], dp), sent["load"].at[6]))
    for copy in loads:
        copy.start()
    loop(1, 32, lambda k: signal_to(barrier, dp, lax.rem(batch + k, 32)))
    loop(0, 8, lambda k: signal_to(barrier, sibling, z_peer(k)))
    loop(4, 16, lambda k: signal_to(barrier, lax.rem(y + k // 4, 4) * 2 + core, z * 4 + k % 4))

    def sum_copy(kind, axis, k):
        which = 2 * (kind == "s") + (axis == "g")
        mine, every = r["my" + kind + axis], r["all" + kind + axis]
        if axis == "z":
            me, to = column, column_peer(k)
        else:
            me, to = plane, plane_peer(k)
        return remote(mine, every.at[me], sent["sum"].at[which], came["sum"].at[which], *to)

    def sum_start(kind, axis, value):
        r["my" + kind + axis][...] = value
        loop(1, 16, lambda k: sum_copy(kind, axis, k).start())
        r["all" + kind + axis][column if axis == "z" else plane] = value

    def sum_end(kind, axis):
        every = r["all" + kind + axis]
        landed(every.at[0:15], came["sum"].at[2 * (kind == "s") + (axis == "g")])
        return jnp.sum(every[...], axis=0)

    def sum_sent(kind, axis):
        every = r["all" + kind + axis]
        landed(every.at[0:15], sent["sum"].at[2 * (kind == "s") + (axis == "g")])

    def wave_copy(k):
        to = lax.rem(batch + k, 32)
        return remote(r["send"].at[to], r["got"].at[batch], sent["wave"], came["wave"], dp, to)

    def w0_copy(k):
        return remote(
            r["mine0"], block(r["f0"], dp, 0, 128), sent["w0row"].at[k], came["w0row"].at[k], y_peer(k), batch
        )

    def pass0_copy(k):
        owner = y_peer(4 - k)
        here = block(r["f0"], owner, 0, 128)
        source = here if k else r["mine0"]
        return remote(source, here, sent["pass0"].at[k], came["pass0"].at[k], sibling, batch)

    def rowa_copy(w, k):
        here = block(full[w], dp, 0, CUT)
        return remote(here, here, sent["rowa"].at[w * 4 + k], came["rowa"].at[w * 4 + k], y_peer(k), batch)

    def rowb_copy(w, k):
        here = quarter(full[w], dp, x, CUT, 3 * D - CUT)
        return remote(here, here, sent["rowb"].at[w * 4 + k], came["rowb"].at[w * 4 + k], y_peer(k), batch)

    def rowx_copy(w, k, j):
        here = quarter(full[w], y_peer(4 - k), x, CUT, 3 * D - CUT)
        at = w * 16 + k * 4 + j
        return remote(here, here, sent["rowx"].at[at], came["rowx"].at[at], dp, x_peer(j))

    def passa_copy(w, k):
        here = block(full[w], y_peer(4 - k), 0, CUT)
        return remote(here, here, sent["passa"].at[w * 4 + k], came["passa"].at[w * 4 + k], sibling, batch)

    def passb_copy(w, k):
        here = block(full[w], y_peer(4 - k), CUT, 3 * D - CUT)
        return remote(here, here, sent["passb"].at[w * 4 + k], came["passb"].at[w * 4 + k], sibling, batch)

    loads[6].wait()
    loads[7].wait()
    pl.semaphore_wait(barrier, 51)
    for w in range(2):
        for k in (2, 1, 3):
            rowb_copy(w, k).start()
    for i in range(6):
        if i != 4:
            loads[i].wait()
    total = tokens[0]
    for s in range(1, SEG):
        total = total + tokens[s]
    eye = jnp.where(iota((10, 128), 0) == iota((10, 128), 1), 1.0, 0.0).astype(BF16)
    r["mine0"][...] = mm(r["w0t"][...], eye, TN).astype(BF16)
    for k in (2, 1, 3):
        w0_copy(k).start()
    pass0_copy(0).start()
    r["send"][...] = pack_waves(r["wave"][...], dest, length, tokens).reshape(32, 16, 128)
    loop(11, 42, lambda k: wave_copy(1 + lax.rem(k, 31)).start())
    for w in range(2):
        for k in (2, 1, 3):
            rowa_copy(w, k).start()
    for w in range(2):
        passa_copy(w, 0).start()
        passb_copy(w, 0).start()
    r["got"][batch] = r["send"][batch]
    block(r["f0"], dp, 0, 128)[...] = r["mine0"][...]
    sum_start("t", "z", jnp.broadcast_to(total.astype(F32), (8, 128)))
    for k in (1, 3, 2):
        w0_copy(k).wait_recv()
        pass0_copy(k).start()
    for w in range(2):
        for k in (1, 3, 2):
            rowb_copy(w, k).wait_recv()
            for j in (2, 1, 3):
                rowx_copy(w, k, j).start()

    def pass_on(w):
        for k in (1, 3, 2):
            rowa_copy(w, k).wait_recv()
            passa_copy(w, k).start()
        for k in (1, 3, 2):
            for j in (1, 3, 2):
                rowx_copy(w, k, j).wait_recv()
            passb_copy(w, k).start()

    def gathered(w):
        for k in range(4):
            passa_copy(w, k).wait_recv()
            passb_copy(w, k).wait_recv()

    landed(r["send"].at[0:31], came["wave"])
    for k in range(4):
        pass0_copy(k).wait_recv()
    forward_first(r["got"][...].reshape(512, 128), r["f0"], r)
    pass_on(0)
    sum_start("t", "g", sum_end("t", "z"))
    gathered(0)
    forward_second(full[0], r)
    pass_on(1)
    gathered(1)

    def core_copy(p, k):
        step = lax.rem(y + k, 4)
        grads = r["g" + str(p)]
        width = 128 if p == "f" else 3 * D
        at = (2 if p == "f" else p) * 4 + k
        return remote(
            block(grads, step * 2 + 1 - core, 0, width), r["rc" + str(p)].at[step],
            sent["core"].at[at], came["core"].at[at], sibling, batch,
        )

    def y_copy(p, k):
        to = lax.rem(y + k, 4)
        width = 128 if p == "f" else HALF
        at = (2 if p == "f" else p) * 4 + k
        return remote(
            r["ys" + str(p)].at[to, :, 0:width], r["yr" + str(p)].at[y],
            sent["y"].at[at], came["y"].at[at], to * 2 + core, batch,
        )

    def bx_copy(p, k):
        to = lax.rem(x + k, 4)
        rows = pl.ds(pl.multiple_of(to * 16, 16), 16)
        return remote(
            r["ys" + str(p)].at[:, rows, HALF:], r["bx" + str(p)].at[x],
            sent["bx"].at[p * 4 + k], came["bx"].at[p * 4 + k], dp, z * 4 + to,
        )

    def x_copy(p, k):
        to = lax.rem(x + k, 4)
        rows = pl.ds(pl.multiple_of(to * 16, 16), 16)
        at = (2 if p == "f" else p) * 4 + k
        return remote(
            r["xs" + str(p)].at[rows], r["xr" + str(p)].at[x],
            sent["x"].at[at], came["x"].at[at], dp, z * 4 + to,
        )

    def by_copy(p, k):
        to = lax.rem(y + k, 4)
        return remote(
            r["by" + str(p)].at[to], r["bz" + str(p)].at[y],
            sent["by"].at[p * 4 + k], came["by"].at[p * 4 + k], to * 2 + core, batch,
        )

    def z_copy(p, k):
        to = lax.rem(z + k, 8)
        return remote(
            r["zs" + str(p)].at[to], r["zr" + str(p)].at[z], sent["z"].at[p], came["z"].at[p], dp, z_peer(k)
        )

    def fz_copy(p, k):
        here = r["fz" + str(p)].at[z]
        return remote(here, here, sent["fz"].at[p], came["fz"].at[p], dp, z_peer(k))

    def fx_copy(p, k):
        here = r["fr" + str(p)].at[x]
        return remote(here, here, sent["fx"].at[p * 4 + k], came["fx"].at[p * 4 + k], dp, x_peer(k))

    def core_start(p, grad=None):
        for k in (2, 1, 3, 0):
            if grad is not None:
                grad(pl.ds(pl.multiple_of(lax.rem(y + k, 4) * 128, 128), 128), r)
            core_copy(p, k).start()

    def core_end(p):
        for k in (2, 1, 3, 0):
            step = lax.rem(y + k, 4)
            core_copy(p, k).wait_recv()
            for m in range(4):
                rows = pl.ds(pl.multiple_of((step * 2 + core) * 64 + m * 16, 16), 16)
                here = slice(m * 16, m * 16 + 16)
                own = r["g" + str(p)][rows].astype(F32)
                r["ys" + str(p)][step, here] = (own + r["rc" + str(p)][step, here].astype(F32)).astype(BF16)
            if k:
                y_copy(p, k).start()
        if p != "f":
            for k in (2, 1, 3):
                bx_copy(p, k).start()

    def y_end(p):
        width = 128 if p == "f" else HALF
        for k in (1, 3, 2):
            y_copy(p, k).wait_recv()
        for m in range(4):
            here = slice(m * 16, m * 16 + 16)
            found = r["ys" + str(p)][y, here, 0:width].astype(F32)
            for k in (1, 2, 3):
                found = found + r["yr" + str(p)][lax.rem(y + k, 4), here].astype(F32)
            r["xs" + str(p)][here] = found.astype(BF16)
        for k in (2, 1, 3):
            x_copy(p, k).start()

    def bx_end(p):
        for k in (1, 3, 2):
            bx_copy(p, k).wait_recv()
        rows = pl.ds(pl.multiple_of(x * 16, 16), 16)
        for step in range(4):
            found = r["ys" + str(p)][step, rows, HALF:].astype(F32)
            for k in (1, 2, 3):
                found = found + r["bx" + str(p)][lax.rem(x + k, 4), step].astype(F32)
            r["by" + str(p)][step] = found.astype(BF16)
        for k in (2, 1, 3):
            by_copy(p, k).start()

    def x_end(p):
        for k in (1, 3, 2):
            x_copy(p, k).wait_recv()
        found = r["xs" + str(p)][pl.ds(pl.multiple_of(x * 16, 16), 16)].astype(F32)
        for k in (1, 2, 3):
            found = found + r["xr" + str(p)][lax.rem(x + k, 4)].astype(F32)
        return found

    def by_end(p):
        for k in (1, 3, 2):
            by_copy(p, k).wait_recv()
        found = r["by" + str(p)][y].astype(F32)
        for k in (1, 2, 3):
            found = found + r["bz" + str(p)][lax.rem(y + k, 4)].astype(F32)
        return found

    def z_start(p):
        low, high = x_end(p), by_end(p)
        out = r["zs" + str(p)]
        for q in range(3):
            out[q] = low[:, q * 256 : q * 256 + 256].astype(BF16)
            out[q + 3] = high[:, q * 256 : q * 256 + 256].astype(BF16)
        out[6] = jnp.zeros((16, 256), BF16)
        out[7] = jnp.zeros((16, 256), BF16)
        if p == 1:
            out[6, :, 0:128] = x_end("f").astype(BF16)
        loop(1, 8, lambda k: z_copy(p, k).start())
        r["zr" + str(p)][z] = out[z]

    def z_end(p, per_token, other=None):
        landed(r["zr" + str(p)].at[0:7], came["z"].at[p])
        found = jnp.sum(r["zr" + str(p)][...].astype(F32), axis=0)
        r["fz" + str(p)][z] = found.astype(BF16)
        found = found * per_token
        squares = jnp.sum(found * found, keepdims=True)
        if p == 1:
            sum_start("s", "z", jnp.broadcast_to(squares + other, (8, 128)))
        loop(1, 8, lambda k: fz_copy(p, k).start())
        return squares

    def fx_start(p):
        landed(r["fz" + str(p)].at[0:7], came["fz"].at[p])
        out = r["fr" + str(p)]
        for q in range(6):
            out[x, :, q * 256 : q * 256 + 256] = r["fz" + str(p)][q]
        if p == 1:
            out[x, :, 3 * D :] = r["fz1"][6, :, 0:128]
        for k in (2, 1, 3):
            fx_copy(p, k).start()

    loads[4].wait()
    third_layer(r["cot"], full[1], r)
    core_start(0, grad_third)
    back_second(full[1], r)
    core_end(0)
    core_start(1, grad_second)
    back_first(full[0], r)
    core_end(1)
    grad_first(r["gf"], r)
    core_start("f")
    core_end("f")
    y_end(0)
    bx_end(0)
    token_sum = sum_end("t", "g")
    per_token = (1.0 / token_sum)[0:1, 0:1]
    z_start(0)
    y_end(1)
    bx_end(1)
    y_end("f")
    z_start(1)
    squares = z_end(0, per_token)
    fx_start(0)
    z_end(1, per_token, squares)
    fx_start(1)
    sum_start("s", "g", sum_end("s", "z"))
    rms = jnp.sqrt(sum_end("s", "g") * (1.0 / COUNT))
    factor = (1.0 / (token_sum * jnp.maximum(rms, 1.0)))[0:1, 0:1]
    stat_out[0:8] = jnp.broadcast_to(factor, (8, 128))
    stat_out[8:16] = rms
    for p in range(2):
        for k in (1, 3, 2):
            fx_copy(p, k).wait_recv()

    landed(r["send"].at[0:31], sent["wave"])
    for k in range(4):
        pass0_copy(k).wait_send()
        if k:
            w0_copy(k).wait_send()
        for w in range(2):
            passa_copy(w, k).wait_send()
            passb_copy(w, k).wait_send()
            if k:
                rowa_copy(w, k).wait_send()
                rowb_copy(w, k).wait_send()
                for j in range(1, 4):
                    rowx_copy(w, k, j).wait_send()
        for p in (0, 1, "f"):
            core_copy(p, k).wait_send()
            if k:
                y_copy(p, k).wait_send()
                x_copy(p, k).wait_send()
                if p != "f":
                    bx_copy(p, k).wait_send()
                    by_copy(p, k).wait_send()
                    fx_copy(p, k).wait_send()
    for p in range(2):
        landed(r["zr" + str(p)].at[0:7], sent["z"].at[p])
        landed(r["fz" + str(p)].at[0:7], sent["fz"].at[p])
    for kind in "ts":
        for axis in "zg":
            sum_sent(kind, axis)


def whole(wave, dest, length, tokens, cot, w0, w1, w2):
    vmem = pl.BlockSpec(memory_space=pltpu.VMEM)
    anywhere = pl.BlockSpec(memory_space=pl.ANY)
    sems = []
    for count in SEMS.values():
        sems += [pltpu.SemaphoreType.DMA((count,)) if count else pltpu.SemaphoreType.DMA] * 2
    return pl.pallas_call(
        whole_kernel,
        out_shape=(
            jax.ShapeDtypeStruct((4, 16, 3 * D), BF16),
            jax.ShapeDtypeStruct((4, 16, 3 * D + 128), BF16),
            jax.ShapeDtypeStruct((16, 128), F32),
        ),
        in_specs=[anywhere] * 8,
        out_specs=(vmem,) * 3,
        scratch_shapes=[pltpu.SMEM((SEG,), jnp.int32)] * 3
        + [pltpu.VMEM(s, t) for s, t in SCRATCH.values()]
        + sems,
        compiler_params=pltpu.CompilerParams(
            collective_id=0, has_side_effects=True, vmem_limit_bytes=58 << 20
        ),
        cost_estimate=pl.CostEstimate(flops=3000000000, bytes_accessed=3000000, transcendentals=1400000),
    )(wave, dest, length, tokens, cot, w0, w1, w2)


def scale_kernel(third, second, stat, third_out, second_out, first_out, rms_out):
    factor = stat[0:1, 0:1]
    third_out[...] = third[...].astype(F32) * factor
    second_out[...] = second[:, 0 : 3 * D].astype(F32) * factor
    first = second[:, 3 * D :].astype(F32) * factor
    square = jnp.concatenate([first, jnp.zeros((64, 128), F32)], axis=0)
    first_out[...] = square.T[0:10, 0:64]
    rms_out[0] = jnp.max(stat[8:16])


def local(wave, length, dest, tokens, cot, w0, w1, w2):
    third, second, stat = whole(wave, dest, length, tokens, cot.reshape(ROWS2, D), w0.T, w1, w2)
    vmem = pl.BlockSpec(memory_space=pltpu.VMEM)
    third, second, first, rms = pl.pallas_call(
        scale_kernel,
        out_shape=(
            jax.ShapeDtypeStruct((64, 3 * D), F32),
            jax.ShapeDtypeStruct((64, 3 * D), F32),
            jax.ShapeDtypeStruct((10, 64), F32),
            jax.ShapeDtypeStruct((1,), F32),
        ),
        in_specs=[vmem] * 3,
        out_specs=(vmem, vmem, vmem, pl.BlockSpec(memory_space=pltpu.SMEM)),
        compiler_params=pltpu.CompilerParams(vmem_limit_bytes=16 << 20),
    )(third.reshape(64, 3 * D), second.reshape(64, 3 * D + 128), stat)
    return first.T, second, third, rms


def solution(mesh):
    row = P(("dp", "batch"))
    return jax.shard_map(
        local,
        mesh=mesh,
        in_specs=(row, row, row, row, row, P("dp"), P("dp"), P("dp")),
        out_specs=(P("dp"), P("dp"), P("dp"), P()),
        check_vma=False,
    )
```

```python
import functools

import jax
import jax.numpy as jnp
from jax import lax
from jax.experimental import pallas as pl
from jax.experimental.pallas import tpu as pltpu
from jax.sharding import PartitionSpec as P

F32 = jnp.float32
BF16 = jnp.bfloat16
D = 512
SEG = 8
J = 26
ROWS = J * SEG
F2 = 24
UNROLL = True
ROWS2 = F2 * SEG
NT = (((1,), (1,)), ((), ()))
TN = (((0,), (0,)), ((), ()))
NN = (((1,), (0,)), ((), ()))


def mm(a, b, dims):
    return lax.dot_general(a, b, dims, preferred_element_type=F32)


def iota(shape, dim):
    return lax.broadcasted_iota(jnp.int32, shape, dim)


def mean(x):
    return jnp.sum(x, axis=-1, keepdims=True) * (1.0 / D)


def norm_gelu(hidden):
    centred = hidden - mean(hidden)
    inverse = lax.rsqrt(mean(centred * centred) + 1e-05)
    normed = centred * inverse
    cdf = 0.5 + 0.5 * lax.erf(normed * 0.7071067811865476)
    slope = cdf + normed * jnp.exp(-0.5 * normed * normed) * 0.3989422804014327
    return normed, inverse, normed * cdf, slope


def norm_back(grad, normed, inverse):
    return inverse * (grad - mean(grad) - normed * mean(grad * normed))


def rank_weights():
    row_slot = iota((512, 512), 0)
    row_slot = (row_slot // 16) * 2 + (row_slot // 4) % 2
    column_slot = iota((512, 512), 1)
    column_slot = (column_slot // 16) * 2 + (column_slot // 4) % 2
    weight = jnp.where(row_slot < column_slot, 1.0, 0.0) + jnp.where(
        row_slot == column_slot, 64.0, 0.0
    )
    return weight.astype(BF16)


def pick_waves(got, ranks):
    lane_pick = (iota((SEG, 128), 1) == 127).astype(BF16)
    token_row = mm(lane_pick, got, NT)
    column = iota((SEG, 512), 1)
    carries = jnp.logical_and(column % 16 >= 8, column % 4 == 3)
    filled = jnp.where(jnp.logical_and(carries, token_row > 0.5), 1.0, 0.0).astype(BF16)
    place = mm(filled, ranks, NN) - 64.0
    target = place + ((column // 8) % 2 * 32 + (column % 4) * 8).astype(F32)
    target = jnp.where(place > -0.5, target, -1.0)
    picking = jnp.where(iota((64, 512), 0).astype(F32) == target[0:1], 1.0, 0.0).astype(BF16)
    picked = mm(picking, got, NN)
    last = picked[56:64]
    length = last[:, 126:127] + 256.0
    tokens = last[:, 127:128]
    low_last = jnp.where(iota((SEG, 128), 1) < 126, last, 0.0)
    pieces = [picked[8 * i : 8 * i + 8] + picked[32 + 8 * i : 40 + 8 * i] for i in range(3)]
    pieces.append(picked[24:32] + low_last)
    return jnp.concatenate(pieces, axis=1), length, tokens


def first_taps(wave, length):
    inside = iota((SEG, D), 1).astype(F32) < length
    average = jnp.sum(jnp.where(inside, wave, 0.0), axis=1, keepdims=True) / length
    centred = jnp.where(inside, wave - average, 0.0)
    variance = jnp.sum(centred * centred, axis=1, keepdims=True) / length
    normal = centred * lax.rsqrt(variance + 1e-07)
    padded = jnp.concatenate([normal, jnp.zeros((SEG, 256), F32)], axis=1)
    rows = []
    for j in range(J):
        tile, shift = (20 * j) // 128, (20 * j) % 128
        pair = padded[:, tile * 128 : tile * 128 + 256]
        if shift:
            pair = pltpu.roll(pair, 256 - shift, axis=1)
        rows.append(pair[:, :128])
    taps = jnp.concatenate(rows, axis=0)
    return jnp.where(iota((ROWS, 128), 1) < 32, taps, 0.0)


def before_waves(r):
    r["ranks"][...] = rank_weights()
    row, column = iota((ROWS2, ROWS2), 0), iota((ROWS2, ROWS2), 1)
    order = jnp.where(column == (row % SEG) * F2 + row // SEG, 1.0, 0.0).astype(BF16)
    r["c2"][...] = mm(order, r["cot"][...], NN)


def spread_first(w0, r):
    tap_row, tap_column = iota((128, 128), 0), iota((128, 128), 1)
    for c in range(4):
        placing = jnp.logical_and(tap_row % 32 == tap_column + 5 * c, tap_row < 64)
        placing = jnp.logical_and(placing, tap_column < 10)
        r["w0x"][c] = mm(jnp.where(placing, 1.0, 0.0).astype(BF16), w0, NT).astype(BF16)


def forward_first(got, r):
    wave, length, tokens = pick_waves(got, r["ranks"][...])
    taps = first_taps(wave, length)
    high = taps.astype(BF16).astype(F32)
    both = high + pltpu.roll(taps - high, 32, axis=1)
    both_narrow = both.astype(BF16)
    narrow_lane = iota((ROWS, 128), 1)
    for c in range(4):
        moved = pltpu.roll(both, 128 - 5 * c, axis=1) if c else both
        keep = narrow_lane % 32 < 10
        moved = jnp.where(jnp.logical_and(keep, narrow_lane < 64), moved, 0.0)
        r["x4"][c * ROWS : (c + 1) * ROWS] = moved.astype(BF16)
    for c in range(4):
        r["z0"][c * ROWS : (c + 1) * ROWS] = mm(both_narrow, r["w0x"][c], NN)
    l2 = ((((length - 10.0) * 0.2).astype(jnp.int32) + 1 - 3) // 2 + 1 - 3) // 2 + 1
    r["info"][0:8] = jnp.broadcast_to(l2.astype(F32), (SEG, 128))
    r["info"][8:16] = jnp.broadcast_to(tokens, (SEG, 128))

    for c in range(4):

        def body(m, carry, c=c):
            at = pl.multiple_of(m * 16, 16)
            rows = pl.ds(pl.multiple_of(c * ROWS + m * 16, 16), 16)
            here = pl.ds(at, 16)
            normed, inverse, active, slope = norm_gelu(r["z0"][rows])
            r["z0"][rows] = normed
            r["s0"][rows] = slope
            r["r0"][rows] = jnp.broadcast_to(inverse, (16, 128))
            narrow = active.astype(BF16)
            if c < 3:
                r["p1"][here, c * D : (c + 1) * D] = narrow
            if c == 0:
                r["shift"][here] = active
            else:
                odd = pl.ds(pl.multiple_of(ROWS + m * 16, 16), 16)
                if c >= 2:
                    r["p1"][odd, (c - 2) * D : (c - 1) * D] = narrow
            return carry

        lax.fori_loop(0, ROWS // 16, body, 0, unroll=UNROLL)
    r["shift"][ROWS : ROWS + 8] = jnp.zeros((8, D), F32)

    def shifted(m, carry):
        rows = pl.ds(pl.multiple_of(8 + m * 16, 8), 16)
        odd = pl.ds(pl.multiple_of(ROWS + m * 16, 16), 16)
        r["p1"][odd, 2 * D :] = r["shift"][rows].astype(BF16)
        return carry

    lax.fori_loop(0, ROWS // 16, shifted, 0, unroll=UNROLL)


def forward_second(w1_ref, r):
    r["z1"][...] = mm(r["p1"][...], w1_ref[...], NT)

    def even(m, carry):
        rows = pl.ds(pl.multiple_of(m * 16, 16), 16)
        normed, inverse, active, slope = norm_gelu(r["z1"][rows])
        r["z1"][rows] = normed
        r["s1"][rows] = slope
        r["r1"][rows] = jnp.broadcast_to(inverse, (16, 128))
        r["shift"][rows] = active
        return carry

    lax.fori_loop(0, ROWS // 16, even, 0, unroll=UNROLL)

    def odd(m, carry):
        rows = pl.ds(pl.multiple_of(ROWS + m * 16, 16), 16)
        here = pl.ds(pl.multiple_of(m * 16, 16), 16)
        normed, inverse, active, slope = norm_gelu(r["z1"][rows])
        r["z1"][rows] = normed
        r["s1"][rows] = slope
        r["r1"][rows] = jnp.broadcast_to(inverse, (16, 128))
        r["p2"][here, D : 2 * D] = active.astype(BF16)
        return carry

    lax.fori_loop(0, ROWS // 16, odd, 0, unroll=UNROLL)

    def spread(m, carry):
        here = pl.ds(pl.multiple_of(m * 16, 16), 16)
        after = pl.ds(pl.multiple_of(8 + m * 16, 8), 16)
        r["p2"][here, 0:D] = r["shift"][here].astype(BF16)
        r["p2"][here, 2 * D :] = r["shift"][after].astype(BF16)
        return carry

    lax.fori_loop(0, ROWS // 16, spread, 0, unroll=UNROLL)


def third_layer(w2_ref, r):
    r["z2"][...] = mm(r["p2"][0:ROWS2], w2_ref[...], NT)
    limit = jnp.concatenate([r["info"][0:8, 0:1]] * 2, axis=0)
    tokens = jnp.concatenate([r["info"][8:16, 0:1]] * 2, axis=0)
    half = (iota((16, 1), 0) // 8).astype(F32)

    def body(m, carry):
        rows = pl.ds(pl.multiple_of(m * 16, 16), 16)
        normed, inverse, active, slope = norm_gelu(r["z2"][rows])
        frame = half + (2 * m).astype(F32)
        weight = jnp.where(frame < limit, tokens, 0.0)
        grad = r["c2"][rows] * weight * slope
        r["d2"][rows] = norm_back(grad, normed, inverse).astype(BF16)
        return carry

    lax.fori_loop(0, ROWS2 // 16, body, 0, unroll=UNROLL)


def grad_third(rows, r):
    r["g0"][rows] = mm(r["d2"][:, rows], r["p2"][0:ROWS2], TN).astype(BF16)


def back_second(w2_ref, r):
    r["u"][0:8] = jnp.zeros((8, 3 * D), F32)
    r["u"][8 + ROWS2 : 32 + ROWS2] = jnp.zeros((24, 3 * D), F32)
    r["u"][8 : 8 + ROWS2] = mm(r["d2"][...], w2_ref[...], NN)

    def even(m, carry):
        rows = pl.ds(pl.multiple_of(m * 16, 16), 16)
        after = pl.ds(pl.multiple_of(8 + m * 16, 8), 16)
        up = r["u"][after, 0:D] + r["u"][rows, 2 * D :]
        delta = norm_back(up * r["s1"][rows], r["z1"][rows], r["r1"][rows, 0:1])
        r["d1"][rows] = delta.astype(BF16)
        return carry

    lax.fori_loop(0, ROWS // 16, even, 0, unroll=UNROLL)

    def odd(m, carry):
        rows = pl.ds(pl.multiple_of(ROWS + m * 16, 16), 16)
        after = pl.ds(pl.multiple_of(8 + m * 16, 8), 16)
        up = r["u"][after, D : 2 * D]
        delta = norm_back(up * r["s1"][rows], r["z1"][rows], r["r1"][rows, 0:1])
        r["d1"][rows] = delta.astype(BF16)
        return carry

    lax.fori_loop(0, ROWS // 16, odd, 0, unroll=UNROLL)


def grad_second(rows, r):
    r["g1"][rows] = mm(r["d1"][:, rows], r["p1"][...], TN).astype(BF16)


def back_first(w1_ref, r):
    r["ue"][...] = mm(r["d1"][0:ROWS], w1_ref[...], NN)
    r["uo"][0:8] = jnp.zeros((8, 3 * D), F32)
    r["uo"][8:] = mm(r["d1"][ROWS:], w1_ref[...], NN)
    for c in range(4):

        def body(m, carry, c=c):
            here = pl.ds(pl.multiple_of(m * 16, 16), 16)
            after = pl.ds(pl.multiple_of(8 + m * 16, 8), 16)
            rows = pl.ds(pl.multiple_of(c * ROWS + m * 16, 16), 16)
            if c == 0:
                up = r["ue"][here, 0:D] + r["uo"][here, 2 * D :]
            elif c == 1:
                up = r["ue"][here, D : 2 * D]
            elif c == 2:
                up = r["ue"][here, 2 * D :] + r["uo"][after, 0:D]
            else:
                up = r["uo"][after, D : 2 * D]
            delta = norm_back(up * r["s0"][rows], r["z0"][rows], r["r0"][rows, 0:1])
            r["d0"][rows] = delta.astype(BF16)
            return carry

        lax.fori_loop(0, ROWS // 16, body, 0, unroll=UNROLL)


def grad_first(out_ref, r):
    found = mm(r["d0"][...], r["x4"][...], TN)
    found = found + pltpu.roll(found, 96, axis=1)
    found = jnp.where(iota((D, 128), 1) < 10, found, 0.0)
    out_ref[...] = found.astype(out_ref.dtype)


COMPUTE_SCRATCH = {
    "ranks": ((512, 512), BF16),
    "w0x": ((4, 128, D), BF16),
    "x4": ((4 * ROWS, 128), BF16),
    "z0": ((4 * ROWS, D), F32),
    "s0": ((4 * ROWS, D), F32),
    "r0": ((4 * ROWS, 128), F32),
    "d0": ((4 * ROWS, D), BF16),
    "info": ((16, 128), F32),
    "shift": ((ROWS + 8, D), F32),
    "p1": ((2 * ROWS, 3 * D), BF16),
    "z1": ((2 * ROWS, D), F32),
    "s1": ((2 * ROWS, D), F32),
    "r1": ((2 * ROWS, 128), F32),
    "d1": ((2 * ROWS, D), BF16),
    "p2": ((ROWS, 3 * D), BF16),
    "z2": ((ROWS2, D), F32),
    "c2": ((ROWS2, D), F32),
    "d2": ((ROWS2, D), BF16),
    "u": ((ROWS2 + 32, 3 * D), F32),
    "ue": ((ROWS, 3 * D), F32),
    "uo": ((ROWS + 8, 3 * D), F32),
}


def place():
    dp, batch = lax.axis_index("dp"), lax.axis_index("batch")
    return dp, batch, dp // 2, dp % 2, batch // 4, batch % 4


def signal_to(sem, dp, batch):
    pl.semaphore_signal(sem, inc=1, device_id=(dp, batch), device_id_type=pl.DeviceIdType.MESH)


def remote(src, dst, send, recv, dp, batch):
    return pltpu.make_async_remote_copy(
        src_ref=src,
        dst_ref=dst,
        send_sem=send,
        recv_sem=recv,
        device_id=(dp, batch),
        device_id_type=pl.DeviceIdType.MESH,
    )


def landed(ref, sem):
    pltpu.make_async_copy(ref, ref, sem).wait()


def loop(first, last, step):
    def body(i, carry):
        step(i)
        return carry

    lax.fori_loop(first, last, body, 0)


def pack_waves(wave, dest, length, tokens):
    high = wave.astype(BF16).astype(F32)
    low = wave - high
    lane, row = iota((SEG, 128), 1), iota((SEG, 128), 0)
    target = lane // 32 * 8 + (lane // 8) % 4
    extra = jnp.zeros((SEG, 128), F32)
    for s in range(SEG):
        here = dest[s]
        rank = 0
        for t in range(s):
            rank = rank + jnp.where(dest[t] == here, 1, 0)
        target = target + jnp.where(lane % 8 == s, here * 16 + rank * 4, 0)
        detail = jnp.where(lane == 126, length[s] - 256, tokens[s]).astype(F32)
        extra = jnp.where(row == s, detail, extra)
    rows = [high[:, 128 * i : 128 * i + 128] for i in range(4)]
    rows += [low[:, 128 * i : 128 * i + 128] for i in range(3)]
    rows.append(jnp.where(lane < 126, low[:, 384:], extra))
    data = jnp.concatenate(rows, axis=0).astype(BF16)
    select = jnp.where(iota((512, 64), 0) == target[0:1, 0:64], 1.0, 0.0).astype(BF16)
    return mm(select, data, NN).astype(BF16)


HALF = 768
CUT = 768
COUNT = D * 10 + 6 * D * D

SCRATCH = {
    "wave": ((SEG, D), F32),
    "w0t": ((10, 64), BF16),
    "cot": ((ROWS2, D), BF16),
    "mine0": ((64, 128), BF16),
    "send": ((32, 16, 128), BF16),
    "got": ((32, 16, 128), BF16),
    "f0": ((D, 128), BF16),
    "f1": ((D, 3 * D), BF16),
    "f2": ((D, 3 * D), BF16),
    "g0": ((D, 3 * D), BF16),
    "g1": ((D, 3 * D), BF16),
    "gf": ((D, 128), BF16),
    "rc0": ((4, 64, 3 * D), BF16),
    "rc1": ((4, 64, 3 * D), BF16),
    "rcf": ((4, 64, 128), BF16),
    "ys0": ((4, 64, 3 * D), BF16),
    "ys1": ((4, 64, 3 * D), BF16),
    "ysf": ((4, 64, 128), BF16),
    "yr0": ((4, 64, HALF), BF16),
    "yr1": ((4, 64, HALF), BF16),
    "yrf": ((4, 64, 128), BF16),
    "bx0": ((4, 4, 16, HALF), BF16),
    "bx1": ((4, 4, 16, HALF), BF16),
    "xs0": ((64, HALF), BF16),
    "xs1": ((64, HALF), BF16),
    "xsf": ((64, 128), BF16),
    "xr0": ((4, 16, HALF), BF16),
    "xr1": ((4, 16, HALF), BF16),
    "xrf": ((4, 16, 128), BF16),
    "by0": ((4, 16, HALF), BF16),
    "by1": ((4, 16, HALF), BF16),
    "bz0": ((4, 16, HALF), BF16),
    "bz1": ((4, 16, HALF), BF16),
    "zs0": ((8, 16, 256), BF16),
    "zs1": ((8, 16, 256), BF16),
    "zr0": ((8, 16, 256), BF16),
    "zr1": ((8, 16, 256), BF16),
    "fz0": ((8, 16, 256), BF16),
    "fz1": ((8, 16, 256), BF16),
}
SCRATCH["fr0"] = ((4, 16, 3 * D), BF16)
SCRATCH["fr1"] = ((4, 16, 3 * D + 128), BF16)
SCRATCH["stat"] = ((16, 128), F32)
SCRATCH.update(COMPUTE_SCRATCH)
for kind in ("t", "s"):
    for axis in "zg":
        SCRATCH["all" + kind + axis] = ((16, 8, 128), F32)
        SCRATCH["my" + kind + axis] = ((8, 128), F32)

SEMS = {
    "load": 7,
    "wave": 0,
    "w0row": 4,
    "pass0": 4,
    "rowa": 8,
    "rowb": 8,
    "rowx": 32,
    "passa": 8,
    "passb": 8,
    "core": 12,
    "y": 12,
    "bx": 8,
    "x": 12,
    "by": 8,
    "z": 2,
    "fz": 2,
    "fx": 8,
    "sum": 4,
    "out": 3,
}


def whole_kernel(
    wave_in, dest_in, length_in, tokens_in, cot_in, w0_in, w1_in, w2_in,
    third_out, second_out, stat_out, dest, length, tokens, *rest,
):
    r = dict(zip(SCRATCH, rest))
    sems = rest[len(SCRATCH) :]
    sent = dict(zip(SEMS, sems[0::2]))
    came = dict(zip(SEMS, sems[1::2]))
    dp, batch, y, core, z, x = place()
    sibling = y * 2 + 1 - core

    column, plane = z * 2 + core, y * 4 + x

    def column_peer(k):
        other = lax.rem(column + k, 16)
        return y * 2 + other % 2, other // 2 * 4 + x

    def plane_peer(k):
        other = lax.rem(plane + k, 16)
        return other // 4 * 2 + core, z * 4 + other % 4

    def y_peer(k):
        return lax.rem(y + k, 4) * 2 + core

    def z_peer(k):
        return lax.rem(z + k, 8) * 4 + x

    def x_peer(k):
        return z * 4 + lax.rem(x + k, 4)

    def block(ref, who, start=0, width=3 * D):
        return ref.at[pl.ds(pl.multiple_of(who * 64, 64), 64), start : start + width]

    def quarter(ref, who, which, start, width):
        return ref.at[pl.ds(pl.multiple_of(who * 64 + which * 16, 16), 16), start : start + width]

    barrier = pltpu.get_barrier_semaphore()
    loads = [
        (wave_in, r["wave"]),
        (dest_in, dest),
        (length_in, length),
        (tokens_in, tokens),
        (cot_in, r["cot"]),
        (w0_in, r["w0t"]),
    ]
    loads = [pltpu.make_async_copy(a, b, came["load"].at[i]) for i, (a, b) in enumerate(loads)]
    full = (r["f1"], r["f2"])
    loads.append(pltpu.make_async_copy(w1_in, block(full[0], dp), came["load"].at[6]))
    loads.append(pltpu.make_async_copy(w2_in, block(full[1], dp), sent["load"].at[6]))
    for copy in loads:
        copy.start()
    loop(1, 32, lambda k: signal_to(barrier, dp, lax.rem(batch + k, 32)))
    loop(0, 8, lambda k: signal_to(barrier, sibling, z_peer(k)))
    loop(4, 16, lambda k: signal_to(barrier, lax.rem(y + k // 4, 4) * 2 + core, z * 4 + k % 4))

    def sum_copy(kind, axis, k):
        which = 2 * (kind == "s") + (axis == "g")
        mine, every = r["my" + kind + axis], r["all" + kind + axis]
        if axis == "z":
            me, to = column, column_peer(k)
        else:
            me, to = plane, plane_peer(k)
        return remote(mine, every.at[me], sent["sum"].at[which], came["sum"].at[which], *to)

    def sum_start(kind, axis, value):
        r["my" + kind + axis][...] = value
        loop(1, 16, lambda k: sum_copy(kind, axis, k).start())
        r["all" + kind + axis][column if axis == "z" else plane] = value

    def sum_end(kind, axis):
        every = r["all" + kind + axis]
        landed(every.at[0:15], came["sum"].at[2 * (kind == "s") + (axis == "g")])
        return jnp.sum(every[...], axis=0)

    def sum_sent(kind, axis):
        every = r["all" + kind + axis]
        landed(every.at[0:15], sent["sum"].at[2 * (kind == "s") + (axis == "g")])

    def wave_copy(k):
        to = lax.rem(batch + k, 32)
        return remote(r["send"].at[to], r["got"].at[batch], sent["wave"], came["wave"], dp, to)

    def w0_copy(k):
        return remote(
            r["mine0"], block(r["f0"], dp, 0, 128), sent["w0row"].at[k], came["w0row"].at[k], y_peer(k), batch
        )

    def pass0_copy(k):
        owner = y_peer(4 - k)
        here = block(r["f0"], owner, 0, 128)
        source = here if k else r["mine0"]
        return remote(source, here, sent["pass0"].at[k], came["pass0"].at[k], sibling, batch)

    def rowa_copy(w, k):
        here = block(full[w], dp, 0, CUT)
        return remote(here, here, sent["rowa"].at[w * 4 + k], came["rowa"].at[w * 4 + k], y_peer(k), batch)

    def rowb_copy(w, k):
        here = quarter(full[w], dp, x, CUT, 3 * D - CUT)
        return remote(here, here, sent["rowb"].at[w * 4 + k], came["rowb"].at[w * 4 + k], y_peer(k), batch)

    def rowx_copy(w, k, j):
        here = quarter(full[w], y_peer(4 - k), x, CUT, 3 * D - CUT)
        at = w * 16 + k * 4 + j
        return remote(here, here, sent["rowx"].at[at], came["rowx"].at[at], dp, x_peer(j))

    def passa_copy(w, k):
        here = block(full[w], y_peer(4 - k), 0, CUT)
        return remote(here, here, sent["passa"].at[w * 4 + k], came["passa"].at[w * 4 + k], sibling, batch)

    def passb_copy(w, k):
        here = block(full[w], y_peer(4 - k), CUT, 3 * D - CUT)
        return remote(here, here, sent["passb"].at[w * 4 + k], came["passb"].at[w * 4 + k], sibling, batch)

    loads[6].wait()
    loads[7].wait()
    pl.semaphore_wait(barrier, 51)
    for w in range(2):
        for k in (2, 1, 3):
            rowb_copy(w, k).start()
    for i in range(6):
        if i != 4:
            loads[i].wait()
    total = tokens[0]
    for s in range(1, SEG):
        total = total + tokens[s]
    eye = jnp.where(iota((10, 128), 0) == iota((10, 128), 1), 1.0, 0.0).astype(BF16)
    r["mine0"][...] = mm(r["w0t"][...], eye, TN).astype(BF16)
    for k in (2, 1, 3):
        w0_copy(k).start()
    pass0_copy(0).start()
    r["send"][...] = pack_waves(r["wave"][...], dest, length, tokens).reshape(32, 16, 128)
    loop(11, 42, lambda k: wave_copy(1 + lax.rem(k, 31)).start())
    for w in range(2):
        for k in (2, 1, 3):
            rowa_copy(w, k).start()
    for w in range(2):
        passa_copy(w, 0).start()
        passb_copy(w, 0).start()
    r["got"][batch] = r["send"][batch]
    block(r["f0"], dp, 0, 128)[...] = r["mine0"][...]
    sum_start("t", "z", jnp.broadcast_to(total.astype(F32), (8, 128)))
    for k in (1, 3, 2):
        w0_copy(k).wait_recv()
        pass0_copy(k).start()
    for w in range(2):
        for k in (1, 3, 2):
            rowb_copy(w, k).wait_recv()
            for j in (2, 1, 3):
                rowx_copy(w, k, j).start()

    def pass_on(w):
        for k in (1, 3, 2):
            rowa_copy(w, k).wait_recv()
            passa_copy(w, k).start()
        for k in (1, 3, 2):
            for j in (1, 3, 2):
                rowx_copy(w, k, j).wait_recv()
            passb_copy(w, k).start()

    def gathered(w):
        for k in range(4):
            passa_copy(w, k).wait_recv()
            passb_copy(w, k).wait_recv()

    loads[4].wait()
    before_waves(r)
    for k in range(4):
        pass0_copy(k).wait_recv()
    spread_first(r["f0"][...], r)
    landed(r["send"].at[0:31], came["wave"])
    forward_first(r["got"][...].reshape(512, 128), r)
    pass_on(0)
    sum_start("t", "g", sum_end("t", "z"))
    gathered(0)
    forward_second(full[0], r)
    pass_on(1)
    gathered(1)

    def core_copy(p, k):
        step = lax.rem(y + k, 4)
        grads = r["g" + str(p)]
        width = 128 if p == "f" else 3 * D
        at = (2 if p == "f" else p) * 4 + k
        return remote(
            block(grads, step * 2 + 1 - core, 0, width), r["rc" + str(p)].at[step],
            sent["core"].at[at], came["core"].at[at], sibling, batch,
        )

    def y_copy(p, k):
        to = lax.rem(y + k, 4)
        width = 128 if p == "f" else HALF
        at = (2 if p == "f" else p) * 4 + k
        return remote(
            r["ys" + str(p)].at[to, :, 0:width], r["yr" + str(p)].at[y],
            sent["y"].at[at], came["y"].at[at], to * 2 + core, batch,
        )

    def bx_copy(p, k):
        to = lax.rem(x + k, 4)
        rows = pl.ds(pl.multiple_of(to * 16, 16), 16)
        return remote(
            r["ys" + str(p)].at[:, rows, HALF:], r["bx" + str(p)].at[x],
            sent["bx"].at[p * 4 + k], came["bx"].at[p * 4 + k], dp, z * 4 + to,
        )

    def x_copy(p, k):
        to = lax.rem(x + k, 4)
        rows = pl.ds(pl.multiple_of(to * 16, 16), 16)
        at = (2 if p == "f" else p) * 4 + k
        return remote(
            r["xs" + str(p)].at[rows], r["xr" + str(p)].at[x],
            sent["x"].at[at], came["x"].at[at], dp, z * 4 + to,
        )

    def by_copy(p, k):
        to = lax.rem(y + k, 4)
        return remote(
            r["by" + str(p)].at[to], r["bz" + str(p)].at[y],
            sent["by"].at[p * 4 + k], came["by"].at[p * 4 + k], to * 2 + core, batch,
        )

    def z_copy(p, k):
        to = lax.rem(z + k, 8)
        return remote(
            r["zs" + str(p)].at[to], r["zr" + str(p)].at[z], sent["z"].at[p], came["z"].at[p], dp, z_peer(k)
        )

    def fz_copy(p, k):
        here = r["fz" + str(p)].at[z]
        return remote(here, here, sent["fz"].at[p], came["fz"].at[p], dp, z_peer(k))

    def fx_copy(p, k):
        here = r["fr" + str(p)].at[x]
        return remote(here, here, sent["fx"].at[p * 4 + k], came["fx"].at[p * 4 + k], dp, x_peer(k))

    def core_start(p, grad=None):
        for k in (2, 1, 3, 0):
            if grad is not None:
                grad(pl.ds(pl.multiple_of(lax.rem(y + k, 4) * 128, 128), 128), r)
            core_copy(p, k).start()

    def core_end(p):
        for k in (2, 1, 3, 0):
            step = lax.rem(y + k, 4)
            core_copy(p, k).wait_recv()
            for m in range(4):
                rows = pl.ds(pl.multiple_of((step * 2 + core) * 64 + m * 16, 16), 16)
                here = slice(m * 16, m * 16 + 16)
                own = r["g" + str(p)][rows].astype(F32)
                r["ys" + str(p)][step, here] = (own + r["rc" + str(p)][step, here].astype(F32)).astype(BF16)
            if k:
                y_copy(p, k).start()
        if p != "f":
            for k in (2, 1, 3):
                bx_copy(p, k).start()

    def y_end(p):
        width = 128 if p == "f" else HALF
        for k in (1, 3, 2):
            y_copy(p, k).wait_recv()
        for m in range(4):
            here = slice(m * 16, m * 16 + 16)
            found = r["ys" + str(p)][y, here, 0:width].astype(F32)
            for k in (1, 2, 3):
                found = found + r["yr" + str(p)][lax.rem(y + k, 4), here].astype(F32)
            r["xs" + str(p)][here] = found.astype(BF16)
        for k in (2, 1, 3):
            x_copy(p, k).start()

    def bx_end(p):
        for k in (1, 3, 2):
            bx_copy(p, k).wait_recv()
        rows = pl.ds(pl.multiple_of(x * 16, 16), 16)
        for step in range(4):
            found = r["ys" + str(p)][step, rows, HALF:].astype(F32)
            for k in (1, 2, 3):
                found = found + r["bx" + str(p)][lax.rem(x + k, 4), step].astype(F32)
            r["by" + str(p)][step] = found.astype(BF16)
        for k in (2, 1, 3):
            by_copy(p, k).start()

    def x_end(p):
        for k in (1, 3, 2):
            x_copy(p, k).wait_recv()
        found = r["xs" + str(p)][pl.ds(pl.multiple_of(x * 16, 16), 16)].astype(F32)
        for k in (1, 2, 3):
            found = found + r["xr" + str(p)][lax.rem(x + k, 4)].astype(F32)
        return found

    def by_end(p):
        for k in (1, 3, 2):
            by_copy(p, k).wait_recv()
        found = r["by" + str(p)][y].astype(F32)
        for k in (1, 2, 3):
            found = found + r["bz" + str(p)][lax.rem(y + k, 4)].astype(F32)
        return found

    def z_start(p):
        low, high = x_end(p), by_end(p)
        out = r["zs" + str(p)]
        for q in range(3):
            out[q] = low[:, q * 256 : q * 256 + 256].astype(BF16)
            out[q + 3] = high[:, q * 256 : q * 256 + 256].astype(BF16)
        out[6] = jnp.zeros((16, 256), BF16)
        out[7] = jnp.zeros((16, 256), BF16)
        if p == 1:
            out[6, :, 0:128] = x_end("f").astype(BF16)
        loop(1, 8, lambda k: z_copy(p, k).start())
        r["zr" + str(p)][z] = out[z]

    def z_end(p, per_token, other=None):
        landed(r["zr" + str(p)].at[0:7], came["z"].at[p])
        found = jnp.sum(r["zr" + str(p)][...].astype(F32), axis=0)
        r["fz" + str(p)][z] = found.astype(BF16)
        found = found * per_token
        squares = jnp.sum(found * found, keepdims=True)
        if p == 1:
            sum_start("s", "z", jnp.broadcast_to(squares + other, (8, 128)))
        loop(1, 8, lambda k: fz_copy(p, k).start())
        return squares

    def fx_start(p):
        landed(r["fz" + str(p)].at[0:7], came["fz"].at[p])
        out = r["fr" + str(p)]
        for q in range(6):
            out[x, :, q * 256 : q * 256 + 256] = r["fz" + str(p)][q]
        if p == 1:
            out[x, :, 3 * D :] = r["fz1"][6, :, 0:128]
        for k in (2, 1, 3):
            fx_copy(p, k).start()

    third_layer(full[1], r)
    core_start(0, grad_third)
    back_second(full[1], r)
    core_end(0)
    core_start(1, grad_second)
    back_first(full[0], r)
    core_end(1)
    grad_first(r["gf"], r)
    core_start("f")
    core_end("f")
    y_end(0)
    bx_end(0)
    token_sum = sum_end("t", "g")
    per_token = (1.0 / token_sum)[0:1, 0:1]
    z_start(0)
    y_end(1)
    bx_end(1)
    y_end("f")
    z_start(1)
    squares = z_end(0, per_token)
    fx_start(0)
    z_end(1, per_token, squares)
    fx_start(1)
    outs = [(r["fr0"], third_out), (r["fr1"], second_out), (r["stat"], stat_out)]
    outs = [pltpu.make_async_copy(a, b, came["out"].at[i]) for i, (a, b) in enumerate(outs)]
    for k in (1, 3, 2):
        fx_copy(0, k).wait_recv()
    outs[0].start()
    sum_start("s", "g", sum_end("s", "z"))
    for k in (1, 3, 2):
        fx_copy(1, k).wait_recv()
    outs[1].start()
    rms = jnp.sqrt(sum_end("s", "g") * (1.0 / COUNT))
    factor = (1.0 / (token_sum * jnp.maximum(rms, 1.0)))[0:1, 0:1]
    r["stat"][0:8] = jnp.broadcast_to(factor, (8, 128))
    r["stat"][8:16] = rms
    outs[2].start()

    landed(r["send"].at[0:31], sent["wave"])
    for k in range(4):
        pass0_copy(k).wait_send()
        if k:
            w0_copy(k).wait_send()
        for w in range(2):
            passa_copy(w, k).wait_send()
            passb_copy(w, k).wait_send()
            if k:
                rowa_copy(w, k).wait_send()
                rowb_copy(w, k).wait_send()
                for j in range(1, 4):
                    rowx_copy(w, k, j).wait_send()
        for p in (0, 1, "f"):
            core_copy(p, k).wait_send()
            if k:
                y_copy(p, k).wait_send()
                x_copy(p, k).wait_send()
                if p != "f":
                    bx_copy(p, k).wait_send()
                    by_copy(p, k).wait_send()
                    fx_copy(p, k).wait_send()
    for p in range(2):
        landed(r["zr" + str(p)].at[0:7], sent["z"].at[p])
        landed(r["fz" + str(p)].at[0:7], sent["fz"].at[p])
    for kind in "ts":
        for axis in "zg":
            sum_sent(kind, axis)
    for copy in outs:
        copy.wait()


def whole(wave, dest, length, tokens, cot, w0, w1, w2):
    anywhere = pl.BlockSpec(memory_space=pl.ANY)
    sems = []
    for count in SEMS.values():
        sems += [pltpu.SemaphoreType.DMA((count,)) if count else pltpu.SemaphoreType.DMA] * 2
    return pl.pallas_call(
        whole_kernel,
        out_shape=(
            jax.ShapeDtypeStruct((4, 16, 3 * D), BF16),
            jax.ShapeDtypeStruct((4, 16, 3 * D + 128), BF16),
            jax.ShapeDtypeStruct((16, 128), F32),
        ),
        in_specs=[anywhere] * 8,
        out_specs=(anywhere,) * 3,
        scratch_shapes=[pltpu.SMEM((SEG,), jnp.int32)] * 3
        + [pltpu.VMEM(s, t) for s, t in SCRATCH.values()]
        + sems,
        compiler_params=pltpu.CompilerParams(
            collective_id=0, has_side_effects=True, vmem_limit_bytes=58 << 20
        ),
        cost_estimate=pl.CostEstimate(flops=3000000000, bytes_accessed=3000000, transcendentals=1400000),
    )(wave, dest, length, tokens, cot, w0, w1, w2)


def scale_kernel(third, second, stat, third_out, second_out, first_out, rms_out):
    factor = stat[0:1, 0:1]
    third_out[...] = third[...].astype(F32) * factor
    second_out[...] = second[:, 0 : 3 * D].astype(F32) * factor
    first = second[:, 3 * D :].astype(F32) * factor
    square = jnp.concatenate([first, jnp.zeros((64, 128), F32)], axis=0)
    first_out[...] = square.T[0:10, 0:64]
    rms_out[0] = jnp.max(stat[8:16])


def local(wave, length, dest, tokens, cot, w0, w1, w2):
    third, second, stat = whole(wave, dest, length, tokens, cot.reshape(ROWS2, D), w0.T, w1, w2)
    vmem = pl.BlockSpec(memory_space=pltpu.VMEM)
    third, second, first, rms = pl.pallas_call(
        scale_kernel,
        out_shape=(
            jax.ShapeDtypeStruct((64, 3 * D), F32),
            jax.ShapeDtypeStruct((64, 3 * D), F32),
            jax.ShapeDtypeStruct((10, 64), F32),
            jax.ShapeDtypeStruct((1,), F32),
        ),
        in_specs=[vmem] * 3,
        out_specs=(vmem, vmem, vmem, pl.BlockSpec(memory_space=pltpu.SMEM)),
        compiler_params=pltpu.CompilerParams(vmem_limit_bytes=58 << 20),
    )(third.reshape(64, 3 * D), second.reshape(64, 3 * D + 128), stat)
    return first.T, second, third, rms


def solution(mesh):
    row = P(("dp", "batch"))
    return jax.shard_map(
        local,
        mesh=mesh,
        in_specs=(row, row, row, row, row, P("dp"), P("dp"), P("dp")),
        out_specs=(P("dp"), P("dp"), P("dp"), P()),
        check_vma=False,
    )
```

```python
import functools

import jax
import jax.numpy as jnp
from jax import lax
from jax.experimental import pallas as pl
from jax.experimental.pallas import tpu as pltpu
from jax.sharding import PartitionSpec as P

F32 = jnp.float32
BF16 = jnp.bfloat16
D = 512
SEG = 8
J = 26
ROWS = J * SEG
F2 = 24
UNROLL = True
ROWS2 = F2 * SEG
NT = (((1,), (1,)), ((), ()))
TN = (((0,), (0,)), ((), ()))
NN = (((1,), (0,)), ((), ()))


def mm(a, b, dims):
    return lax.dot_general(a, b, dims, preferred_element_type=F32)


def iota(shape, dim):
    return lax.broadcasted_iota(jnp.int32, shape, dim)


def mean(x):
    return jnp.sum(x, axis=-1, keepdims=True) * (1.0 / D)


def norm_gelu(hidden):
    centred = hidden - mean(hidden)
    inverse = lax.rsqrt(mean(centred * centred) + 1e-05)
    normed = centred * inverse
    cdf = 0.5 + 0.5 * lax.erf(normed * 0.7071067811865476)
    slope = cdf + normed * jnp.exp(-0.5 * normed * normed) * 0.3989422804014327
    return normed, inverse, normed * cdf, slope


def norm_back(grad, normed, inverse):
    return inverse * (grad - mean(grad) - normed * mean(grad * normed))


def rank_weights():
    row_slot = iota((512, 512), 0)
    row_slot = (row_slot // 16) * 2 + (row_slot // 4) % 2
    column_slot = iota((512, 512), 1)
    column_slot = (column_slot // 16) * 2 + (column_slot // 4) % 2
    weight = jnp.where(row_slot < column_slot, 1.0, 0.0) + jnp.where(
        row_slot == column_slot, 64.0, 0.0
    )
    return weight.astype(BF16)


def pick_waves(got, ranks):
    lane_pick = (iota((SEG, 128), 1) == 127).astype(BF16)
    token_row = mm(lane_pick, got, NT)
    column = iota((SEG, 512), 1)
    carries = jnp.logical_and(column % 16 >= 8, column % 4 == 3)
    filled = jnp.where(jnp.logical_and(carries, token_row > 0.5), 1.0, 0.0).astype(BF16)
    place = mm(filled, ranks, NN) - 64.0
    target = place + ((column // 8) % 2 * 32 + (column % 4) * 8).astype(F32)
    target = jnp.where(place > -0.5, target, -1.0)
    picking = jnp.where(iota((64, 512), 0).astype(F32) == target[0:1], 1.0, 0.0).astype(BF16)
    picked = mm(picking, got, NN)
    last = picked[56:64]
    length = last[:, 126:127] + 256.0
    tokens = last[:, 127:128]
    low_last = jnp.where(iota((SEG, 128), 1) < 126, last, 0.0)
    pieces = [picked[8 * i : 8 * i + 8] + picked[32 + 8 * i : 40 + 8 * i] for i in range(3)]
    pieces.append(picked[24:32] + low_last)
    return jnp.concatenate(pieces, axis=1), length, tokens


def first_taps(wave, length):
    inside = iota((SEG, D), 1).astype(F32) < length
    average = jnp.sum(jnp.where(inside, wave, 0.0), axis=1, keepdims=True) / length
    centred = jnp.where(inside, wave - average, 0.0)
    variance = jnp.sum(centred * centred, axis=1, keepdims=True) / length
    normal = centred * lax.rsqrt(variance + 1e-07)
    padded = jnp.concatenate([normal, jnp.zeros((SEG, 256), F32)], axis=1)
    rows = []
    for j in range(J):
        tile, shift = (20 * j) // 128, (20 * j) % 128
        pair = padded[:, tile * 128 : tile * 128 + 256]
        if shift:
            pair = pltpu.roll(pair, 256 - shift, axis=1)
        rows.append(pair[:, :128])
    taps = jnp.concatenate(rows, axis=0)
    return jnp.where(iota((ROWS, 128), 1) < 32, taps, 0.0)


def before_waves(r):
    r["ranks"][...] = rank_weights()
    row, column = iota((ROWS2, ROWS2), 0), iota((ROWS2, ROWS2), 1)
    order = jnp.where(column == (row % SEG) * F2 + row // SEG, 1.0, 0.0).astype(BF16)
    r["c2"][...] = mm(order, r["cot"][...], NN)


def spread_first(w0, r):
    tap_row, tap_column = iota((128, 128), 0), iota((128, 128), 1)
    for c in range(4):
        placing = jnp.logical_and(tap_row % 32 == tap_column + 5 * c, tap_row < 64)
        placing = jnp.logical_and(placing, tap_column < 10)
        r["w0x"][c] = mm(jnp.where(placing, 1.0, 0.0).astype(BF16), w0, NT).astype(BF16)


def forward_first(got, r):
    wave, length, tokens = pick_waves(got, r["ranks"][...])
    taps = first_taps(wave, length)
    high = taps.astype(BF16).astype(F32)
    both = high + pltpu.roll(taps - high, 32, axis=1)
    both_narrow = both.astype(BF16)
    narrow_lane = iota((ROWS, 128), 1)
    for c in range(4):
        moved = pltpu.roll(both, 128 - 5 * c, axis=1) if c else both
        keep = narrow_lane % 32 < 10
        moved = jnp.where(jnp.logical_and(keep, narrow_lane < 64), moved, 0.0)
        r["x4"][c * ROWS : (c + 1) * ROWS] = moved.astype(BF16)
    for c in range(4):
        r["z0"][c * ROWS : (c + 1) * ROWS] = mm(both_narrow, r["w0x"][c], NN)
    l2 = ((((length - 10.0) * 0.2).astype(jnp.int32) + 1 - 3) // 2 + 1 - 3) // 2 + 1
    r["info"][0:8] = jnp.broadcast_to(l2.astype(F32), (SEG, 128))
    r["info"][8:16] = jnp.broadcast_to(tokens, (SEG, 128))

    for c in range(4):

        def body(m, carry, c=c):
            at = pl.multiple_of(m * 16, 16)
            rows = pl.ds(pl.multiple_of(c * ROWS + m * 16, 16), 16)
            here = pl.ds(at, 16)
            normed, inverse, active, slope = norm_gelu(r["z0"][rows])
            r["z0"][rows] = normed
            r["s0"][rows] = slope
            r["r0"][rows] = jnp.broadcast_to(inverse, (16, 128))
            narrow = active.astype(BF16)
            if c < 3:
                r["p1"][here, c * D : (c + 1) * D] = narrow
            if c == 0:
                r["shift"][here] = active
            else:
                odd = pl.ds(pl.multiple_of(ROWS + m * 16, 16), 16)
                if c >= 2:
                    r["p1"][odd, (c - 2) * D : (c - 1) * D] = narrow
            return carry

        lax.fori_loop(0, ROWS // 16, body, 0, unroll=UNROLL)
    r["shift"][ROWS : ROWS + 8] = jnp.zeros((8, D), F32)

    def shifted(m, carry):
        rows = pl.ds(pl.multiple_of(8 + m * 16, 8), 16)
        odd = pl.ds(pl.multiple_of(ROWS + m * 16, 16), 16)
        r["p1"][odd, 2 * D :] = r["shift"][rows].astype(BF16)
        return carry

    lax.fori_loop(0, ROWS // 16, shifted, 0, unroll=UNROLL)


def forward_second(w1_ref, r):
    r["z1"][...] = mm(r["p1"][...], w1_ref[...], NT)

    def even(m, carry):
        rows = pl.ds(pl.multiple_of(m * 16, 16), 16)
        normed, inverse, active, slope = norm_gelu(r["z1"][rows])
        r["z1"][rows] = normed
        r["s1"][rows] = slope
        r["r1"][rows] = jnp.broadcast_to(inverse, (16, 128))
        r["shift"][rows] = active
        return carry

    lax.fori_loop(0, ROWS // 16, even, 0, unroll=UNROLL)

    def odd(m, carry):
        rows = pl.ds(pl.multiple_of(ROWS + m * 16, 16), 16)
        here = pl.ds(pl.multiple_of(m * 16, 16), 16)
        normed, inverse, active, slope = norm_gelu(r["z1"][rows])
        r["z1"][rows] = normed
        r["s1"][rows] = slope
        r["r1"][rows] = jnp.broadcast_to(inverse, (16, 128))
        r["p2"][here, D : 2 * D] = active.astype(BF16)
        return carry

    lax.fori_loop(0, ROWS // 16, odd, 0, unroll=UNROLL)

    def spread(m, carry):
        here = pl.ds(pl.multiple_of(m * 16, 16), 16)
        after = pl.ds(pl.multiple_of(8 + m * 16, 8), 16)
        r["p2"][here, 0:D] = r["shift"][here].astype(BF16)
        r["p2"][here, 2 * D :] = r["shift"][after].astype(BF16)
        return carry

    lax.fori_loop(0, ROWS // 16, spread, 0, unroll=UNROLL)


def third_layer(w2_ref, r):
    r["z2"][...] = mm(r["p2"][0:ROWS2], w2_ref[...], NT)
    limit = jnp.concatenate([r["info"][0:8, 0:1]] * 2, axis=0)
    tokens = jnp.concatenate([r["info"][8:16, 0:1]] * 2, axis=0)
    half = (iota((16, 1), 0) // 8).astype(F32)

    def body(m, carry):
        rows = pl.ds(pl.multiple_of(m * 16, 16), 16)
        normed, inverse, active, slope = norm_gelu(r["z2"][rows])
        frame = half + (2 * m).astype(F32)
        weight = jnp.where(frame < limit, tokens, 0.0)
        grad = r["c2"][rows] * weight * slope
        r["d2"][rows] = norm_back(grad, normed, inverse).astype(BF16)
        return carry

    lax.fori_loop(0, ROWS2 // 16, body, 0, unroll=UNROLL)


def grad_third(rows, r):
    r["g0"][rows] = mm(r["d2"][:, rows], r["p2"][0:ROWS2], TN).astype(BF16)


def back_second(w2_ref, r):
    r["u"][0:8] = jnp.zeros((8, 3 * D), F32)
    r["u"][8 + ROWS2 : 32 + ROWS2] = jnp.zeros((24, 3 * D), F32)
    r["u"][8 : 8 + ROWS2] = mm(r["d2"][...], w2_ref[...], NN)

    def even(m, carry):
        rows = pl.ds(pl.multiple_of(m * 16, 16), 16)
        after = pl.ds(pl.multiple_of(8 + m * 16, 8), 16)
        up = r["u"][after, 0:D] + r["u"][rows, 2 * D :]
        delta = norm_back(up * r["s1"][rows], r["z1"][rows], r["r1"][rows, 0:1])
        r["d1"][rows] = delta.astype(BF16)
        return carry

    lax.fori_loop(0, ROWS // 16, even, 0, unroll=UNROLL)

    def odd(m, carry):
        rows = pl.ds(pl.multiple_of(ROWS + m * 16, 16), 16)
        after = pl.ds(pl.multiple_of(8 + m * 16, 8), 16)
        up = r["u"][after, D : 2 * D]
        delta = norm_back(up * r["s1"][rows], r["z1"][rows], r["r1"][rows, 0:1])
        r["d1"][rows] = delta.astype(BF16)
        return carry

    lax.fori_loop(0, ROWS // 16, odd, 0, unroll=UNROLL)


def grad_second(rows, r):
    r["g1"][rows] = mm(r["d1"][:, rows], r["p1"][...], TN).astype(BF16)


def back_first(w1_ref, r):
    r["ue"][...] = mm(r["d1"][0:ROWS], w1_ref[...], NN)
    r["uo"][0:8] = jnp.zeros((8, 3 * D), F32)
    r["uo"][8:] = mm(r["d1"][ROWS:], w1_ref[...], NN)
    for c in range(4):

        def body(m, carry, c=c):
            here = pl.ds(pl.multiple_of(m * 16, 16), 16)
            after = pl.ds(pl.multiple_of(8 + m * 16, 8), 16)
            rows = pl.ds(pl.multiple_of(c * ROWS + m * 16, 16), 16)
            if c == 0:
                up = r["ue"][here, 0:D] + r["uo"][here, 2 * D :]
            elif c == 1:
                up = r["ue"][here, D : 2 * D]
            elif c == 2:
                up = r["ue"][here, 2 * D :] + r["uo"][after, 0:D]
            else:
                up = r["uo"][after, D : 2 * D]
            delta = norm_back(up * r["s0"][rows], r["z0"][rows], r["r0"][rows, 0:1])
            r["d0"][rows] = delta.astype(BF16)
            return carry

        lax.fori_loop(0, ROWS // 16, body, 0, unroll=UNROLL)


def grad_first(out_ref, r):
    found = mm(r["d0"][...], r["x4"][...], TN)
    found = found + pltpu.roll(found, 96, axis=1)
    found = jnp.where(iota((D, 128), 1) < 10, found, 0.0)
    out_ref[...] = found.astype(out_ref.dtype)


COMPUTE_SCRATCH = {
    "ranks": ((512, 512), BF16),
    "w0x": ((4, 128, D), BF16),
    "x4": ((4 * ROWS, 128), BF16),
    "z0": ((4 * ROWS, D), F32),
    "s0": ((4 * ROWS, D), F32),
    "r0": ((4 * ROWS, 128), F32),
    "d0": ((4 * ROWS, D), BF16),
    "info": ((16, 128), F32),
    "shift": ((ROWS + 8, D), F32),
    "p1": ((2 * ROWS, 3 * D), BF16),
    "z1": ((2 * ROWS, D), F32),
    "s1": ((2 * ROWS, D), F32),
    "r1": ((2 * ROWS, 128), F32),
    "d1": ((2 * ROWS, D), BF16),
    "p2": ((ROWS, 3 * D), BF16),
    "z2": ((ROWS2, D), F32),
    "c2": ((ROWS2, D), F32),
    "d2": ((ROWS2, D), BF16),
    "u": ((ROWS2 + 32, 3 * D), F32),
    "ue": ((ROWS, 3 * D), F32),
    "uo": ((ROWS + 8, 3 * D), F32),
}


def place():
    dp, batch = lax.axis_index("dp"), lax.axis_index("batch")
    return dp, batch, dp // 2, dp % 2, batch // 4, batch % 4


def signal_to(sem, dp, batch):
    pl.semaphore_signal(sem, inc=1, device_id=(dp, batch), device_id_type=pl.DeviceIdType.MESH)


def remote(src, dst, send, recv, dp, batch):
    return pltpu.make_async_remote_copy(
        src_ref=src,
        dst_ref=dst,
        send_sem=send,
        recv_sem=recv,
        device_id=(dp, batch),
        device_id_type=pl.DeviceIdType.MESH,
    )


def landed(ref, sem):
    pltpu.make_async_copy(ref, ref, sem).wait()


def loop(first, last, step):
    def body(i, carry):
        step(i)
        return carry

    lax.fori_loop(first, last, body, 0)


def pack_waves(wave, dest, length, tokens):
    high = wave.astype(BF16).astype(F32)
    low = wave - high
    lane, row = iota((SEG, 128), 1), iota((SEG, 128), 0)
    target = lane // 32 * 8 + (lane // 8) % 4
    extra = jnp.zeros((SEG, 128), F32)
    for s in range(SEG):
        here = dest[s]
        rank = 0
        for t in range(s):
            rank = rank + jnp.where(dest[t] == here, 1, 0)
        target = target + jnp.where(lane % 8 == s, here * 16 + rank * 4, 0)
        detail = jnp.where(lane == 126, length[s] - 256, tokens[s]).astype(F32)
        extra = jnp.where(row == s, detail, extra)
    rows = [high[:, 128 * i : 128 * i + 128] for i in range(4)]
    rows += [low[:, 128 * i : 128 * i + 128] for i in range(3)]
    rows.append(jnp.where(lane < 126, low[:, 384:], extra))
    data = jnp.concatenate(rows, axis=0).astype(BF16)
    select = jnp.where(iota((512, 64), 0) == target[0:1, 0:64], 1.0, 0.0).astype(BF16)
    return mm(select, data, NN).astype(BF16)


HALF = 768
CUT = 768
COUNT = D * 10 + 6 * D * D

SCRATCH = {
    "wave": ((SEG, D), F32),
    "w0t": ((10, 64), BF16),
    "cot": ((ROWS2, D), BF16),
    "mine0": ((64, 128), BF16),
    "send": ((32, 16, 128), BF16),
    "got": ((32, 16, 128), BF16),
    "f0": ((D, 128), BF16),
    "f1": ((D, 3 * D), BF16),
    "f2": ((D, 3 * D), BF16),
    "g0": ((D, 3 * D), BF16),
    "g1": ((D, 3 * D), BF16),
    "gf": ((D, 128), BF16),
    "rc0": ((4, 64, 3 * D), BF16),
    "rc1": ((4, 64, 3 * D), BF16),
    "rcf": ((4, 64, 128), BF16),
    "ys0": ((4, 64, 3 * D), BF16),
    "ys1": ((4, 64, 3 * D), BF16),
    "ysf": ((4, 64, 128), BF16),
    "yr0": ((4, 64, HALF), BF16),
    "yr1": ((4, 64, HALF), BF16),
    "yrf": ((4, 64, 128), BF16),
    "bx0": ((4, 4, 16, HALF), BF16),
    "bx1": ((4, 4, 16, HALF), BF16),
    "xs0": ((64, HALF), BF16),
    "xs1": ((64, HALF), BF16),
    "xsf": ((64, 128), BF16),
    "xr0": ((4, 16, HALF), BF16),
    "xr1": ((4, 16, HALF), BF16),
    "xrf": ((4, 16, 128), BF16),
    "by0": ((4, 16, HALF), BF16),
    "by1": ((4, 16, HALF), BF16),
    "bz0": ((4, 16, HALF), BF16),
    "bz1": ((4, 16, HALF), BF16),
    "zs0": ((8, 16, 256), BF16),
    "zs1": ((8, 16, 256), BF16),
    "zr0": ((8, 16, 256), BF16),
    "zr1": ((8, 16, 256), BF16),
    "fz0": ((8, 16, 256), BF16),
    "fz1": ((8, 16, 256), BF16),
}
SCRATCH["fr0"] = ((4, 16, 3 * D), BF16)
SCRATCH["fr1"] = ((4, 16, 3 * D + 128), BF16)
SCRATCH["stat"] = ((8, 128), F32)
SCRATCH.update(COMPUTE_SCRATCH)
for kind in ("t", "s"):
    for axis in "zg":
        if kind + axis != "sg":
            SCRATCH["all" + kind + axis] = ((16, 8, 128), F32)
        SCRATCH["my" + kind + axis] = ((8, 128), F32)

SEMS = {
    "load": 7,
    "wave": 0,
    "w0row": 4,
    "pass0": 4,
    "rowa": 8,
    "rowb": 8,
    "rowx": 32,
    "passa": 8,
    "passb": 8,
    "core": 12,
    "y": 12,
    "bx": 8,
    "x": 12,
    "by": 8,
    "z": 2,
    "fz": 2,
    "fx": 8,
    "sum": 4,
    "out": 4,
}


def whole_kernel(
    wave_in, dest_in, length_in, tokens_in, cot_in, w0_in, w1_in, w2_in,
    third_out, second_out, squares_out, tokens_out, dest, length, tokens, *rest,
):
    r = dict(zip(SCRATCH, rest))
    sems = rest[len(SCRATCH) :]
    sent = dict(zip(SEMS, sems[0::2]))
    came = dict(zip(SEMS, sems[1::2]))
    dp, batch, y, core, z, x = place()
    sibling = y * 2 + 1 - core

    column, plane = z * 2 + core, y * 4 + x

    def column_peer(k):
        other = lax.rem(column + k, 16)
        return y * 2 + other % 2, other // 2 * 4 + x

    def plane_peer(k):
        other = lax.rem(plane + k, 16)
        return other // 4 * 2 + core, z * 4 + other % 4

    def y_peer(k):
        return lax.rem(y + k, 4) * 2 + core

    def z_peer(k):
        return lax.rem(z + k, 8) * 4 + x

    def x_peer(k):
        return z * 4 + lax.rem(x + k, 4)

    def block(ref, who, start=0, width=3 * D):
        return ref.at[pl.ds(pl.multiple_of(who * 64, 64), 64), start : start + width]

    def quarter(ref, who, which, start, width):
        return ref.at[pl.ds(pl.multiple_of(who * 64 + which * 16, 16), 16), start : start + width]

    barrier = pltpu.get_barrier_semaphore()
    loads = [
        (wave_in, r["wave"]),
        (dest_in, dest),
        (length_in, length),
        (tokens_in, tokens),
        (cot_in, r["cot"]),
        (w0_in, r["w0t"]),
    ]
    loads = [pltpu.make_async_copy(a, b, came["load"].at[i]) for i, (a, b) in enumerate(loads)]
    full = (r["f1"], r["f2"])
    loads.append(pltpu.make_async_copy(w1_in, block(full[0], dp), came["load"].at[6]))
    loads.append(pltpu.make_async_copy(w2_in, block(full[1], dp), sent["load"].at[6]))
    for copy in loads:
        copy.start()
    loop(1, 32, lambda k: signal_to(barrier, dp, lax.rem(batch + k, 32)))
    loop(0, 8, lambda k: signal_to(barrier, sibling, z_peer(k)))
    loop(4, 16, lambda k: signal_to(barrier, lax.rem(y + k // 4, 4) * 2 + core, z * 4 + k % 4))

    def sum_copy(kind, axis, k):
        which = 2 * (kind == "s") + (axis == "g")
        mine = r["my" + kind + axis]
        every = squares_out if which == 3 else r["all" + kind + axis]
        if axis == "z":
            me, to = column, column_peer(k)
        else:
            me, to = plane, plane_peer(k)
        return remote(mine, every.at[me], sent["sum"].at[which], came["sum"].at[which], *to)

    def sum_start(kind, axis, value):
        r["my" + kind + axis][...] = value
        loop(1, 16, lambda k: sum_copy(kind, axis, k).start())
        r["all" + kind + axis][column if axis == "z" else plane] = value

    def sum_end(kind, axis):
        every = r["all" + kind + axis]
        landed(every.at[0:15], came["sum"].at[2 * (kind == "s") + (axis == "g")])
        return jnp.sum(every[...], axis=0)

    def sum_sent(kind, axis):
        every = r["alltg"]
        landed(every.at[0:15], sent["sum"].at[2 * (kind == "s") + (axis == "g")])

    def wave_copy(k):
        to = lax.rem(batch + k, 32)
        return remote(r["send"].at[to], r["got"].at[batch], sent["wave"], came["wave"], dp, to)

    def w0_copy(k):
        return remote(
            r["mine0"], block(r["f0"], dp, 0, 128), sent["w0row"].at[k], came["w0row"].at[k], y_peer(k), batch
        )

    def pass0_copy(k):
        owner = y_peer(4 - k)
        here = block(r["f0"], owner, 0, 128)
        source = here if k else r["mine0"]
        return remote(source, here, sent["pass0"].at[k], came["pass0"].at[k], sibling, batch)

    def rowa_copy(w, k):
        here = block(full[w], dp, 0, CUT)
        return remote(here, here, sent["rowa"].at[w * 4 + k], came["rowa"].at[w * 4 + k], y_peer(k), batch)

    def rowb_copy(w, k):
        here = quarter(full[w], dp, x, CUT, 3 * D - CUT)
        return remote(here, here, sent["rowb"].at[w * 4 + k], came["rowb"].at[w * 4 + k], y_peer(k), batch)

    def rowx_copy(w, k, j):
        here = quarter(full[w], y_peer(4 - k), x, CUT, 3 * D - CUT)
        at = w * 16 + k * 4 + j
        return remote(here, here, sent["rowx"].at[at], came["rowx"].at[at], dp, x_peer(j))

    def passa_copy(w, k):
        here = block(full[w], y_peer(4 - k), 0, CUT)
        return remote(here, here, sent["passa"].at[w * 4 + k], came["passa"].at[w * 4 + k], sibling, batch)

    def passb_copy(w, k):
        here = block(full[w], y_peer(4 - k), CUT, 3 * D - CUT)
        return remote(here, here, sent["passb"].at[w * 4 + k], came["passb"].at[w * 4 + k], sibling, batch)

    loads[6].wait()
    loads[7].wait()
    pl.semaphore_wait(barrier, 51)
    for w in range(2):
        for k in (2, 1, 3):
            rowb_copy(w, k).start()
    for i in range(6):
        if i != 4:
            loads[i].wait()
    total = tokens[0]
    for s in range(1, SEG):
        total = total + tokens[s]
    eye = jnp.where(iota((10, 128), 0) == iota((10, 128), 1), 1.0, 0.0).astype(BF16)
    r["mine0"][...] = mm(r["w0t"][...], eye, TN).astype(BF16)
    for k in (2, 1, 3):
        w0_copy(k).start()
    pass0_copy(0).start()
    r["send"][...] = pack_waves(r["wave"][...], dest, length, tokens).reshape(32, 16, 128)
    loop(11, 42, lambda k: wave_copy(1 + lax.rem(k, 31)).start())
    for w in range(2):
        for k in (2, 1, 3):
            rowa_copy(w, k).start()
    for w in range(2):
        passa_copy(w, 0).start()
        passb_copy(w, 0).start()
    r["got"][batch] = r["send"][batch]
    block(r["f0"], dp, 0, 128)[...] = r["mine0"][...]
    sum_start("t", "z", jnp.broadcast_to(total.astype(F32), (8, 128)))
    for k in (1, 3, 2):
        w0_copy(k).wait_recv()
        pass0_copy(k).start()
    for w in range(2):
        for k in (1, 3, 2):
            rowb_copy(w, k).wait_recv()
            for j in (2, 1, 3):
                rowx_copy(w, k, j).start()

    def pass_on(w):
        for k in (1, 3, 2):
            rowa_copy(w, k).wait_recv()
            passa_copy(w, k).start()
        for k in (1, 3, 2):
            for j in (1, 3, 2):
                rowx_copy(w, k, j).wait_recv()
            passb_copy(w, k).start()

    def gathered(w):
        for k in range(4):
            passa_copy(w, k).wait_recv()
            passb_copy(w, k).wait_recv()

    loads[4].wait()
    before_waves(r)
    for k in range(4):
        pass0_copy(k).wait_recv()
    spread_first(r["f0"][...], r)
    landed(r["send"].at[0:31], came["wave"])
    forward_first(r["got"][...].reshape(512, 128), r)
    pass_on(0)
    sum_start("t", "g", sum_end("t", "z"))
    gathered(0)
    forward_second(full[0], r)
    pass_on(1)
    gathered(1)

    def core_copy(p, k):
        step = lax.rem(y + k, 4)
        grads = r["g" + str(p)]
        width = 128 if p == "f" else 3 * D
        at = (2 if p == "f" else p) * 4 + k
        return remote(
            block(grads, step * 2 + 1 - core, 0, width), r["rc" + str(p)].at[step],
            sent["core"].at[at], came["core"].at[at], sibling, batch,
        )

    def y_copy(p, k):
        to = lax.rem(y + k, 4)
        width = 128 if p == "f" else HALF
        at = (2 if p == "f" else p) * 4 + k
        return remote(
            r["ys" + str(p)].at[to, :, 0:width], r["yr" + str(p)].at[y],
            sent["y"].at[at], came["y"].at[at], to * 2 + core, batch,
        )

    def bx_copy(p, k):
        to = lax.rem(x + k, 4)
        rows = pl.ds(pl.multiple_of(to * 16, 16), 16)
        return remote(
            r["ys" + str(p)].at[:, rows, HALF:], r["bx" + str(p)].at[x],
            sent["bx"].at[p * 4 + k], came["bx"].at[p * 4 + k], dp, z * 4 + to,
        )

    def x_copy(p, k):
        to = lax.rem(x + k, 4)
        rows = pl.ds(pl.multiple_of(to * 16, 16), 16)
        at = (2 if p == "f" else p) * 4 + k
        return remote(
            r["xs" + str(p)].at[rows], r["xr" + str(p)].at[x],
            sent["x"].at[at], came["x"].at[at], dp, z * 4 + to,
        )

    def by_copy(p, k):
        to = lax.rem(y + k, 4)
        return remote(
            r["by" + str(p)].at[to], r["bz" + str(p)].at[y],
            sent["by"].at[p * 4 + k], came["by"].at[p * 4 + k], to * 2 + core, batch,
        )

    def z_copy(p, k):
        to = lax.rem(z + k, 8)
        return remote(
            r["zs" + str(p)].at[to], r["zr" + str(p)].at[z], sent["z"].at[p], came["z"].at[p], dp, z_peer(k)
        )

    def fz_copy(p, k):
        here = r["fz" + str(p)].at[z]
        return remote(here, here, sent["fz"].at[p], came["fz"].at[p], dp, z_peer(k))

    def fx_copy(p, k):
        here = r["fr" + str(p)].at[x]
        return remote(here, here, sent["fx"].at[p * 4 + k], came["fx"].at[p * 4 + k], dp, x_peer(k))

    def core_start(p, grad=None):
        for k in (2, 1, 3, 0):
            if grad is not None:
                grad(pl.ds(pl.multiple_of(lax.rem(y + k, 4) * 128, 128), 128), r)
            core_copy(p, k).start()

    def core_end(p):
        for k in (2, 1, 3, 0):
            step = lax.rem(y + k, 4)
            core_copy(p, k).wait_recv()
            for m in range(4):
                rows = pl.ds(pl.multiple_of((step * 2 + core) * 64 + m * 16, 16), 16)
                here = slice(m * 16, m * 16 + 16)
                own = r["g" + str(p)][rows].astype(F32)
                r["ys" + str(p)][step, here] = (own + r["rc" + str(p)][step, here].astype(F32)).astype(BF16)
            if k:
                y_copy(p, k).start()
        if p != "f":
            for k in (2, 1, 3):
                bx_copy(p, k).start()

    def y_end(p):
        width = 128 if p == "f" else HALF
        for k in (1, 3, 2):
            y_copy(p, k).wait_recv()
        for m in range(4):
            here = slice(m * 16, m * 16 + 16)
            found = r["ys" + str(p)][y, here, 0:width].astype(F32)
            for k in (1, 2, 3):
                found = found + r["yr" + str(p)][lax.rem(y + k, 4), here].astype(F32)
            r["xs" + str(p)][here] = found.astype(BF16)
        for k in (2, 1, 3):
            x_copy(p, k).start()

    def bx_end(p):
        for k in (1, 3, 2):
            bx_copy(p, k).wait_recv()
        rows = pl.ds(pl.multiple_of(x * 16, 16), 16)
        for step in range(4):
            found = r["ys" + str(p)][step, rows, HALF:].astype(F32)
            for k in (1, 2, 3):
                found = found + r["bx" + str(p)][lax.rem(x + k, 4), step].astype(F32)
            r["by" + str(p)][step] = found.astype(BF16)
        for k in (2, 1, 3):
            by_copy(p, k).start()

    def x_end(p):
        for k in (1, 3, 2):
            x_copy(p, k).wait_recv()
        found = r["xs" + str(p)][pl.ds(pl.multiple_of(x * 16, 16), 16)].astype(F32)
        for k in (1, 2, 3):
            found = found + r["xr" + str(p)][lax.rem(x + k, 4)].astype(F32)
        return found

    def by_end(p):
        for k in (1, 3, 2):
            by_copy(p, k).wait_recv()
        found = r["by" + str(p)][y].astype(F32)
        for k in (1, 2, 3):
            found = found + r["bz" + str(p)][lax.rem(y + k, 4)].astype(F32)
        return found

    def z_start(p):
        low, high = x_end(p), by_end(p)
        out = r["zs" + str(p)]
        for q in range(3):
            out[q] = low[:, q * 256 : q * 256 + 256].astype(BF16)
            out[q + 3] = high[:, q * 256 : q * 256 + 256].astype(BF16)
        out[6] = jnp.zeros((16, 256), BF16)
        out[7] = jnp.zeros((16, 256), BF16)
        if p == 1:
            out[6, :, 0:128] = x_end("f").astype(BF16)
        loop(1, 8, lambda k: z_copy(p, k).start())
        r["zr" + str(p)][z] = out[z]

    def z_end(p, per_token, other=None):
        landed(r["zr" + str(p)].at[0:7], came["z"].at[p])
        found = jnp.sum(r["zr" + str(p)][...].astype(F32), axis=0)
        r["fz" + str(p)][z] = found.astype(BF16)
        found = found * per_token
        squares = jnp.sum(found * found, keepdims=True)
        if p == 1:
            sum_start("s", "z", jnp.broadcast_to(squares + other, (8, 128)))
        loop(1, 8, lambda k: fz_copy(p, k).start())
        return squares

    def fx_start(p):
        landed(r["fz" + str(p)].at[0:7], came["fz"].at[p])
        out = r["fr" + str(p)]
        for q in range(6):
            out[x, :, q * 256 : q * 256 + 256] = r["fz" + str(p)][q]
        if p == 1:
            out[x, :, 3 * D :] = r["fz1"][6, :, 0:128]
        for k in (2, 1, 3):
            fx_copy(p, k).start()

    third_layer(full[1], r)
    core_start(0, grad_third)
    back_second(full[1], r)
    core_end(0)
    core_start(1, grad_second)
    back_first(full[0], r)
    core_end(1)
    grad_first(r["gf"], r)
    core_start("f")
    core_end("f")
    y_end(0)
    bx_end(0)
    token_sum = sum_end("t", "g")
    per_token = (1.0 / token_sum)[0:1, 0:1]
    z_start(0)
    y_end(1)
    bx_end(1)
    y_end("f")
    z_start(1)
    squares = z_end(0, per_token)
    fx_start(0)
    z_end(1, per_token, squares)
    fx_start(1)
    outs = [(r["fr0"], third_out), (r["fr1"], second_out), (r["mysg"], squares_out.at[plane]), (r["stat"], tokens_out)]
    outs = [pltpu.make_async_copy(a, b, came["out"].at[i]) for i, (a, b) in enumerate(outs)]
    r["stat"][...] = token_sum
    outs[3].start()
    for k in (1, 3, 2):
        fx_copy(0, k).wait_recv()
    outs[0].start()
    r["mysg"][...] = sum_end("s", "z")
    loop(1, 16, lambda k: sum_copy("s", "g", k).start())
    outs[2].start()
    for k in (1, 3, 2):
        fx_copy(1, k).wait_recv()
    outs[1].start()
    landed(r["send"].at[0:31], sent["wave"])
    for k in range(4):
        pass0_copy(k).wait_send()
        if k:
            w0_copy(k).wait_send()
        for w in range(2):
            passa_copy(w, k).wait_send()
            passb_copy(w, k).wait_send()
            if k:
                rowa_copy(w, k).wait_send()
                rowb_copy(w, k).wait_send()
                for j in range(1, 4):
                    rowx_copy(w, k, j).wait_send()
        for p in (0, 1, "f"):
            core_copy(p, k).wait_send()
            if k:
                y_copy(p, k).wait_send()
                x_copy(p, k).wait_send()
                if p != "f":
                    bx_copy(p, k).wait_send()
                    by_copy(p, k).wait_send()
                    fx_copy(p, k).wait_send()
    for p in range(2):
        landed(r["zr" + str(p)].at[0:7], sent["z"].at[p])
        landed(r["fz" + str(p)].at[0:7], sent["fz"].at[p])
    sum_sent("t", "z")
    sum_sent("t", "g")
    sum_sent("s", "z")
    for copy in outs:
        copy.wait()
    landed(squares_out.at[0:15], came["sum"].at[3])
    sum_sent("s", "g")


def whole(wave, dest, length, tokens, cot, w0, w1, w2):
    anywhere = pl.BlockSpec(memory_space=pl.ANY)
    sems = []
    for count in SEMS.values():
        sems += [pltpu.SemaphoreType.DMA((count,)) if count else pltpu.SemaphoreType.DMA] * 2
    return pl.pallas_call(
        whole_kernel,
        out_shape=(
            jax.ShapeDtypeStruct((4, 16, 3 * D), BF16),
            jax.ShapeDtypeStruct((4, 16, 3 * D + 128), BF16),
            jax.ShapeDtypeStruct((16, 8, 128), F32),
            jax.ShapeDtypeStruct((8, 128), F32),
        ),
        in_specs=[anywhere] * 8,
        out_specs=(anywhere,) * 4,
        scratch_shapes=[pltpu.SMEM((SEG,), jnp.int32)] * 3
        + [pltpu.VMEM(s, t) for s, t in SCRATCH.values()]
        + sems,
        compiler_params=pltpu.CompilerParams(
            collective_id=0, has_side_effects=True, vmem_limit_bytes=58 << 20
        ),
        cost_estimate=pl.CostEstimate(flops=3000000000, bytes_accessed=3000000, transcendentals=1400000),
    )(wave, dest, length, tokens, cot, w0, w1, w2)


def scale_kernel(third, second, squares, tokens, third_out, second_out, first_out, rms_out):
    rms = jnp.sqrt(jnp.sum(squares[...], axis=0) * (1.0 / COUNT))
    factor = (1.0 / (tokens[...] * jnp.maximum(rms, 1.0)))[0:1, 0:1]
    third_out[...] = third[...].astype(F32) * factor
    second_out[...] = second[:, 0 : 3 * D].astype(F32) * factor
    first = second[:, 3 * D :].astype(F32) * factor
    square = jnp.concatenate([first, jnp.zeros((64, 128), F32)], axis=0)
    first_out[...] = square.T[0:10, 0:64]
    rms_out[0] = jnp.max(rms)


def local(wave, length, dest, tokens, cot, w0, w1, w2):
    third, second, squares, total = whole(wave, dest, length, tokens, cot.reshape(ROWS2, D), w0.T, w1, w2)
    vmem = pl.BlockSpec(memory_space=pltpu.VMEM)
    third, second, first, rms = pl.pallas_call(
        scale_kernel,
        out_shape=(
            jax.ShapeDtypeStruct((64, 3 * D), F32),
            jax.ShapeDtypeStruct((64, 3 * D), F32),
            jax.ShapeDtypeStruct((10, 64), F32),
            jax.ShapeDtypeStruct((1,), F32),
        ),
        in_specs=[vmem] * 4,
        out_specs=(vmem, vmem, vmem, pl.BlockSpec(memory_space=pltpu.SMEM)),
        compiler_params=pltpu.CompilerParams(vmem_limit_bytes=58 << 20),
    )(third.reshape(64, 3 * D), second.reshape(64, 3 * D + 128), squares, total)
    return first.T, second, third, rms


def solution(mesh):
    row = P(("dp", "batch"))
    return jax.shard_map(
        local,
        mesh=mesh,
        in_specs=(row, row, row, row, row, P("dp"), P("dp"), P("dp")),
        out_specs=(P("dp"), P("dp"), P("dp"), P()),
        check_vma=False,
    )
```

```python
import functools

import jax
import jax.numpy as jnp
from jax import lax
from jax.experimental import pallas as pl
from jax.experimental.pallas import tpu as pltpu
from jax.sharding import PartitionSpec as P

F32 = jnp.float32
BF16 = jnp.bfloat16
D = 512
SEG = 8
J = 26
ROWS = J * SEG
F2 = 24
UNROLL = True
ROWS2 = F2 * SEG
NT = (((1,), (1,)), ((), ()))
TN = (((0,), (0,)), ((), ()))
NN = (((1,), (0,)), ((), ()))


def mm(a, b, dims):
    return lax.dot_general(a, b, dims, preferred_element_type=F32)


def iota(shape, dim):
    return lax.broadcasted_iota(jnp.int32, shape, dim)


def mean(x):
    return jnp.sum(x, axis=-1, keepdims=True) * (1.0 / D)


def norm_gelu(hidden):
    centred = hidden - mean(hidden)
    inverse = lax.rsqrt(mean(centred * centred) + 1e-05)
    normed = centred * inverse
    cdf = 0.5 + 0.5 * lax.erf(normed * 0.7071067811865476)
    slope = cdf + normed * jnp.exp(-0.5 * normed * normed) * 0.3989422804014327
    return normed, inverse, normed * cdf, slope


def norm_back(grad, normed, inverse):
    return inverse * (grad - mean(grad) - normed * mean(grad * normed))


def rank_weights():
    row_slot = iota((512, 512), 0)
    row_slot = (row_slot // 16) * 2 + (row_slot // 4) % 2
    column_slot = iota((512, 512), 1)
    column_slot = (column_slot // 16) * 2 + (column_slot // 4) % 2
    weight = jnp.where(row_slot < column_slot, 1.0, 0.0) + jnp.where(
        row_slot == column_slot, 64.0, 0.0
    )
    return weight.astype(BF16)


def pick_waves(got, ranks):
    lane_pick = (iota((SEG, 128), 1) == 127).astype(BF16)
    token_row = mm(lane_pick, got, NT)
    column = iota((SEG, 512), 1)
    carries = jnp.logical_and(column % 16 >= 8, column % 4 == 3)
    filled = jnp.where(jnp.logical_and(carries, token_row > 0.5), 1.0, 0.0).astype(BF16)
    place = mm(filled, ranks, NN) - 64.0
    target = place + ((column // 8) % 2 * 32 + (column % 4) * 8).astype(F32)
    target = jnp.where(place > -0.5, target, -1.0)
    picking = jnp.where(iota((64, 512), 0).astype(F32) == target[0:1], 1.0, 0.0).astype(BF16)
    picked = mm(picking, got, NN)
    last = picked[56:64]
    length = last[:, 126:127] + 256.0
    tokens = last[:, 127:128]
    low_last = jnp.where(iota((SEG, 128), 1) < 126, last, 0.0)
    pieces = [picked[8 * i : 8 * i + 8] + picked[32 + 8 * i : 40 + 8 * i] for i in range(3)]
    pieces.append(picked[24:32] + low_last)
    return jnp.concatenate(pieces, axis=1), length, tokens


def first_taps(wave, length):
    inside = iota((SEG, D), 1).astype(F32) < length
    average = jnp.sum(jnp.where(inside, wave, 0.0), axis=1, keepdims=True) / length
    centred = jnp.where(inside, wave - average, 0.0)
    variance = jnp.sum(centred * centred, axis=1, keepdims=True) / length
    normal = centred * lax.rsqrt(variance + 1e-07)
    padded = jnp.concatenate([normal, jnp.zeros((SEG, 256), F32)], axis=1)
    rows = []
    for j in range(J):
        tile, shift = (20 * j) // 128, (20 * j) % 128
        pair = padded[:, tile * 128 : tile * 128 + 256]
        if shift:
            pair = pltpu.roll(pair, 256 - shift, axis=1)
        rows.append(pair[:, :128])
    taps = jnp.concatenate(rows, axis=0)
    return jnp.where(iota((ROWS, 128), 1) < 32, taps, 0.0)


def before_waves(r):
    r["ranks"][...] = rank_weights()
    row, column = iota((ROWS2, ROWS2), 0), iota((ROWS2, ROWS2), 1)
    order = jnp.where(column == (row % SEG) * F2 + row // SEG, 1.0, 0.0).astype(BF16)
    r["c2"][...] = mm(order, r["cot"][...], NN)


def spread_first(w0, r):
    tap_row, tap_column = iota((128, 128), 0), iota((128, 128), 1)
    for c in range(4):
        placing = jnp.logical_and(tap_row % 32 == tap_column + 5 * c, tap_row < 64)
        placing = jnp.logical_and(placing, tap_column < 10)
        r["w0x"][c] = mm(jnp.where(placing, 1.0, 0.0).astype(BF16), w0, NT).astype(BF16)


def forward_first(got, r):
    wave, length, tokens = pick_waves(got, r["ranks"][...])
    taps = first_taps(wave, length)
    high = taps.astype(BF16).astype(F32)
    both = high + pltpu.roll(taps - high, 32, axis=1)
    both_narrow = both.astype(BF16)
    narrow_lane = iota((ROWS, 128), 1)
    for c in range(4):
        moved = pltpu.roll(both, 128 - 5 * c, axis=1) if c else both
        keep = narrow_lane % 32 < 10
        moved = jnp.where(jnp.logical_and(keep, narrow_lane < 64), moved, 0.0)
        r["x4"][c * ROWS : (c + 1) * ROWS] = moved.astype(BF16)
    for c in range(4):
        r["z0"][c * ROWS : (c + 1) * ROWS] = mm(both_narrow, r["w0x"][c], NN)
    l2 = ((((length - 10.0) * 0.2).astype(jnp.int32) + 1 - 3) // 2 + 1 - 3) // 2 + 1
    r["info"][0:8] = jnp.broadcast_to(l2.astype(F32), (SEG, 128))
    r["info"][8:16] = jnp.broadcast_to(tokens, (SEG, 128))

    for c in range(4):

        def body(m, carry, c=c):
            at = pl.multiple_of(m * 16, 16)
            rows = pl.ds(pl.multiple_of(c * ROWS + m * 16, 16), 16)
            here = pl.ds(at, 16)
            normed, inverse, active, slope = norm_gelu(r["z0"][rows])
            r["z0"][rows] = normed
            r["s0"][rows] = slope
            r["r0"][rows] = jnp.broadcast_to(inverse, (16, 128))
            narrow = active.astype(BF16)
            if c < 3:
                r["p1"][here, c * D : (c + 1) * D] = narrow
            if c == 0:
                r["shift"][here] = active
            else:
                odd = pl.ds(pl.multiple_of(ROWS + m * 16, 16), 16)
                if c >= 2:
                    r["p1"][odd, (c - 2) * D : (c - 1) * D] = narrow
            return carry

        lax.fori_loop(0, ROWS // 16, body, 0, unroll=UNROLL)
    r["shift"][ROWS : ROWS + 8] = jnp.zeros((8, D), F32)

    def shifted(m, carry):
        rows = pl.ds(pl.multiple_of(8 + m * 16, 8), 16)
        odd = pl.ds(pl.multiple_of(ROWS + m * 16, 16), 16)
        r["p1"][odd, 2 * D :] = r["shift"][rows].astype(BF16)
        return carry

    lax.fori_loop(0, ROWS // 16, shifted, 0, unroll=UNROLL)


def forward_second(w1_ref, r):
    r["z1"][...] = mm(r["p1"][...], w1_ref[...], NT)

    def even(m, carry):
        rows = pl.ds(pl.multiple_of(m * 16, 16), 16)
        normed, inverse, active, slope = norm_gelu(r["z1"][rows])
        r["z1"][rows] = normed
        r["s1"][rows] = slope
        r["r1"][rows] = jnp.broadcast_to(inverse, (16, 128))
        r["shift"][rows] = active
        return carry

    lax.fori_loop(0, ROWS // 16, even, 0, unroll=UNROLL)

    def odd(m, carry):
        rows = pl.ds(pl.multiple_of(ROWS + m * 16, 16), 16)
        here = pl.ds(pl.multiple_of(m * 16, 16), 16)
        normed, inverse, active, slope = norm_gelu(r["z1"][rows])
        r["z1"][rows] = normed
        r["s1"][rows] = slope
        r["r1"][rows] = jnp.broadcast_to(inverse, (16, 128))
        r["p2"][here, D : 2 * D] = active.astype(BF16)
        return carry

    lax.fori_loop(0, ROWS // 16, odd, 0, unroll=UNROLL)

    def spread(m, carry):
        here = pl.ds(pl.multiple_of(m * 16, 16), 16)
        after = pl.ds(pl.multiple_of(8 + m * 16, 8), 16)
        r["p2"][here, 0:D] = r["shift"][here].astype(BF16)
        r["p2"][here, 2 * D :] = r["shift"][after].astype(BF16)
        return carry

    lax.fori_loop(0, ROWS // 16, spread, 0, unroll=UNROLL)


def third_layer(w2_ref, r):
    r["z2"][...] = mm(r["p2"][0:ROWS2], w2_ref[...], NT)
    limit = jnp.concatenate([r["info"][0:8, 0:1]] * 2, axis=0)
    tokens = jnp.concatenate([r["info"][8:16, 0:1]] * 2, axis=0)
    half = (iota((16, 1), 0) // 8).astype(F32)

    def body(m, carry):
        rows = pl.ds(pl.multiple_of(m * 16, 16), 16)
        normed, inverse, active, slope = norm_gelu(r["z2"][rows])
        frame = half + (2 * m).astype(F32)
        weight = jnp.where(frame < limit, tokens, 0.0)
        grad = r["c2"][rows] * weight * slope
        r["d2"][rows] = norm_back(grad, normed, inverse).astype(BF16)
        return carry

    lax.fori_loop(0, ROWS2 // 16, body, 0, unroll=UNROLL)


def grad_third(rows, r):
    r["g0"][rows] = mm(r["d2"][:, rows], r["p2"][0:ROWS2], TN).astype(BF16)


def back_second(w2_ref, r):
    r["u"][0:8] = jnp.zeros((8, 3 * D), F32)
    r["u"][8 + ROWS2 : 32 + ROWS2] = jnp.zeros((24, 3 * D), F32)
    r["u"][8 : 8 + ROWS2] = mm(r["d2"][...], w2_ref[...], NN)

    def even(m, carry):
        rows = pl.ds(pl.multiple_of(m * 16, 16), 16)
        after = pl.ds(pl.multiple_of(8 + m * 16, 8), 16)
        up = r["u"][after, 0:D] + r["u"][rows, 2 * D :]
        delta = norm_back(up * r["s1"][rows], r["z1"][rows], r["r1"][rows, 0:1])
        r["d1"][rows] = delta.astype(BF16)
        return carry

    lax.fori_loop(0, ROWS // 16, even, 0, unroll=UNROLL)

    def odd(m, carry):
        rows = pl.ds(pl.multiple_of(ROWS + m * 16, 16), 16)
        after = pl.ds(pl.multiple_of(8 + m * 16, 8), 16)
        up = r["u"][after, D : 2 * D]
        delta = norm_back(up * r["s1"][rows], r["z1"][rows], r["r1"][rows, 0:1])
        r["d1"][rows] = delta.astype(BF16)
        return carry

    lax.fori_loop(0, ROWS // 16, odd, 0, unroll=UNROLL)


def grad_second(rows, r):
    r["g1"][rows] = mm(r["d1"][:, rows], r["p1"][...], TN).astype(BF16)


def back_first(w1_ref, r):
    r["ue"][...] = mm(r["d1"][0:ROWS], w1_ref[...], NN)
    r["uo"][0:8] = jnp.zeros((8, 3 * D), F32)
    r["uo"][8:] = mm(r["d1"][ROWS:], w1_ref[...], NN)
    for c in range(4):

        def body(m, carry, c=c):
            here = pl.ds(pl.multiple_of(m * 16, 16), 16)
            after = pl.ds(pl.multiple_of(8 + m * 16, 8), 16)
            rows = pl.ds(pl.multiple_of(c * ROWS + m * 16, 16), 16)
            if c == 0:
                up = r["ue"][here, 0:D] + r["uo"][here, 2 * D :]
            elif c == 1:
                up = r["ue"][here, D : 2 * D]
            elif c == 2:
                up = r["ue"][here, 2 * D :] + r["uo"][after, 0:D]
            else:
                up = r["uo"][after, D : 2 * D]
            delta = norm_back(up * r["s0"][rows], r["z0"][rows], r["r0"][rows, 0:1])
            r["d0"][rows] = delta.astype(BF16)
            return carry

        lax.fori_loop(0, ROWS // 16, body, 0, unroll=UNROLL)


def grad_first(out_ref, r):
    found = mm(r["d0"][...], r["x4"][...], TN)
    found = found + pltpu.roll(found, 96, axis=1)
    found = jnp.where(iota((D, 128), 1) < 10, found, 0.0)
    out_ref[...] = found.astype(out_ref.dtype)


COMPUTE_SCRATCH = {
    "ranks": ((512, 512), BF16),
    "w0x": ((4, 128, D), BF16),
    "x4": ((4 * ROWS, 128), BF16),
    "z0": ((4 * ROWS, D), F32),
    "s0": ((4 * ROWS, D), F32),
    "r0": ((4 * ROWS, 128), F32),
    "d0": ((4 * ROWS, D), BF16),
    "info": ((16, 128), F32),
    "shift": ((ROWS + 8, D), F32),
    "p1": ((2 * ROWS, 3 * D), BF16),
    "z1": ((2 * ROWS, D), F32),
    "s1": ((2 * ROWS, D), F32),
    "r1": ((2 * ROWS, 128), F32),
    "d1": ((2 * ROWS, D), BF16),
    "p2": ((ROWS, 3 * D), BF16),
    "z2": ((ROWS2, D), F32),
    "c2": ((ROWS2, D), F32),
    "d2": ((ROWS2, D), BF16),
    "u": ((ROWS2 + 32, 3 * D), F32),
    "ue": ((ROWS, 3 * D), F32),
    "uo": ((ROWS + 8, 3 * D), F32),
}


def place():
    dp, batch = lax.axis_index("dp"), lax.axis_index("batch")
    return dp, batch, dp // 2, dp % 2, batch // 4, batch % 4


def signal_to(sem, dp, batch):
    pl.semaphore_signal(sem, inc=1, device_id=(dp, batch), device_id_type=pl.DeviceIdType.MESH)


def remote(src, dst, send, recv, dp, batch):
    return pltpu.make_async_remote_copy(
        src_ref=src,
        dst_ref=dst,
        send_sem=send,
        recv_sem=recv,
        device_id=(dp, batch),
        device_id_type=pl.DeviceIdType.MESH,
    )


def landed(ref, sem):
    pltpu.make_async_copy(ref, ref, sem).wait()


def loop(first, last, step):
    def body(i, carry):
        step(i)
        return carry

    lax.fori_loop(first, last, body, 0)


def pack_waves(wave, dest, length, tokens):
    high = wave.astype(BF16).astype(F32)
    low = wave - high
    lane, row = iota((SEG, 128), 1), iota((SEG, 128), 0)
    target = lane // 32 * 8 + (lane // 8) % 4
    extra = jnp.zeros((SEG, 128), F32)
    for s in range(SEG):
        here = dest[s]
        rank = 0
        for t in range(s):
            rank = rank + jnp.where(dest[t] == here, 1, 0)
        target = target + jnp.where(lane % 8 == s, here * 16 + rank * 4, 0)
        detail = jnp.where(lane == 126, length[s] - 256, tokens[s]).astype(F32)
        extra = jnp.where(row == s, detail, extra)
    rows = [high[:, 128 * i : 128 * i + 128] for i in range(4)]
    rows += [low[:, 128 * i : 128 * i + 128] for i in range(3)]
    rows.append(jnp.where(lane < 126, low[:, 384:], extra))
    data = jnp.concatenate(rows, axis=0).astype(BF16)
    select = jnp.where(iota((512, 64), 0) == target[0:1, 0:64], 1.0, 0.0).astype(BF16)
    return mm(select, data, NN).astype(BF16)


HALF = 768
CUT = 768
COUNT = D * 10 + 6 * D * D

SCRATCH = {
    "wave": ((SEG, D), F32),
    "w0t": ((10, 64), BF16),
    "cot": ((ROWS2, D), BF16),
    "mine0": ((64, 128), BF16),
    "send": ((32, 16, 128), BF16),
    "got": ((32, 16, 128), BF16),
    "f0": ((D, 128), BF16),
    "f1": ((D, 3 * D), BF16),
    "f2": ((D, 3 * D), BF16),
    "g0": ((D, 3 * D), BF16),
    "g1": ((D, 3 * D), BF16),
    "gf": ((D, 128), BF16),
    "rc0": ((4, 64, 3 * D), BF16),
    "rc1": ((4, 64, 3 * D), BF16),
    "rcf": ((4, 64, 128), BF16),
    "ys0": ((4, 64, 3 * D), BF16),
    "ys1": ((4, 64, 3 * D), BF16),
    "ysf": ((4, 64, 128), BF16),
    "yr0": ((4, 64, HALF), BF16),
    "yr1": ((4, 64, HALF), BF16),
    "yrf": ((4, 64, 128), BF16),
    "bx0": ((4, 4, 16, HALF), BF16),
    "bx1": ((4, 4, 16, HALF), BF16),
    "xs0": ((64, HALF), BF16),
    "xs1": ((64, HALF), BF16),
    "xsf": ((64, 128), BF16),
    "xr0": ((4, 16, HALF), BF16),
    "xr1": ((4, 16, HALF), BF16),
    "xrf": ((4, 16, 128), BF16),
    "by0": ((4, 16, HALF), BF16),
    "by1": ((4, 16, HALF), BF16),
    "bz0": ((4, 16, HALF), BF16),
    "bz1": ((4, 16, HALF), BF16),
    "zs0": ((8, 16, 256), BF16),
    "zs1": ((8, 16, 256), BF16),
    "zr0": ((8, 16, 256), BF16),
    "zr1": ((8, 16, 256), BF16),
    "fz0": ((8, 16, 256), BF16),
    "fz1": ((8, 16, 256), BF16),
}
SCRATCH["fr0"] = ((4, 16, 3 * D), BF16)
SCRATCH["fr1"] = ((4, 16, 3 * D + 128), BF16)
SCRATCH["stat"] = ((8, 128), F32)
SCRATCH.update(COMPUTE_SCRATCH)
for kind in ("t", "s"):
    for axis in "zg":
        if kind + axis != "sg":
            SCRATCH["all" + kind + axis] = ((16, 8, 128), F32)
        SCRATCH["my" + kind + axis] = ((8, 128), F32)

SEMS = {
    "load": 7,
    "wave": 0,
    "w0row": 4,
    "pass0": 4,
    "rowa": 8,
    "rowb": 8,
    "rowx": 32,
    "passa": 8,
    "passb": 8,
    "core": 12,
    "y": 12,
    "bx": 8,
    "x": 12,
    "by": 8,
    "z": 2,
    "fz": 2,
    "fx": 8,
    "sum": 4,
    "out": 4,
}


def whole_kernel(
    wave_in, dest_in, length_in, tokens_in, cot_in, w0_in, w1_in, w2_in,
    third_out, second_out, squares_out, tokens_out, dest, length, tokens, *rest,
):
    r = dict(zip(SCRATCH, rest))
    sems = rest[len(SCRATCH) :]
    sent = dict(zip(SEMS, sems[0::2]))
    came = dict(zip(SEMS, sems[1::2]))
    dp, batch, y, core, z, x = place()
    sibling = y * 2 + 1 - core

    column, plane = z * 2 + core, y * 4 + x

    def column_peer(k):
        other = lax.rem(column + k, 16)
        return y * 2 + other % 2, other // 2 * 4 + x

    def plane_peer(k):
        other = lax.rem(plane + k, 16)
        return other // 4 * 2 + core, z * 4 + other % 4

    def y_peer(k):
        return lax.rem(y + k, 4) * 2 + core

    def z_peer(k):
        return lax.rem(z + k, 8) * 4 + x

    def x_peer(k):
        return z * 4 + lax.rem(x + k, 4)

    def block(ref, who, start=0, width=3 * D):
        return ref.at[pl.ds(pl.multiple_of(who * 64, 64), 64), start : start + width]

    def quarter(ref, who, which, start, width):
        return ref.at[pl.ds(pl.multiple_of(who * 64 + which * 16, 16), 16), start : start + width]

    barrier = pltpu.get_barrier_semaphore()
    loads = [
        (wave_in, r["wave"]),
        (dest_in, dest),
        (length_in, length),
        (tokens_in, tokens),
        (cot_in, r["cot"]),
        (w0_in, r["w0t"]),
    ]
    loads = [pltpu.make_async_copy(a, b, came["load"].at[i]) for i, (a, b) in enumerate(loads)]
    full = (r["f1"], r["f2"])
    loads.append(pltpu.make_async_copy(w1_in, block(full[0], dp), came["load"].at[6]))
    loads.append(pltpu.make_async_copy(w2_in, block(full[1], dp), sent["load"].at[6]))
    for copy in loads:
        copy.start()
    loop(1, 32, lambda k: signal_to(barrier, dp, lax.rem(batch + k, 32)))
    loop(0, 8, lambda k: signal_to(barrier, sibling, z_peer(k)))
    loop(4, 16, lambda k: signal_to(barrier, lax.rem(y + k // 4, 4) * 2 + core, z * 4 + k % 4))

    def sum_copy(kind, axis, k):
        which = 2 * (kind == "s") + (axis == "g")
        mine = r["my" + kind + axis]
        every = squares_out if which == 3 else r["all" + kind + axis]
        if axis == "z":
            me, to = column, column_peer(k)
        else:
            me, to = plane, plane_peer(k)
        return remote(mine, every.at[me], sent["sum"].at[which], came["sum"].at[which], *to)

    def sum_start(kind, axis, value):
        r["my" + kind + axis][...] = value
        loop(1, 16, lambda k: sum_copy(kind, axis, k).start())
        r["all" + kind + axis][column if axis == "z" else plane] = value

    def sum_end(kind, axis):
        every = r["all" + kind + axis]
        landed(every.at[0:15], came["sum"].at[2 * (kind == "s") + (axis == "g")])
        return jnp.sum(every[...], axis=0)

    def sum_sent(kind, axis):
        every = r["alltg"]
        landed(every.at[0:15], sent["sum"].at[2 * (kind == "s") + (axis == "g")])

    def wave_copy(k):
        to = lax.rem(batch + k, 32)
        return remote(r["send"].at[to], r["got"].at[batch], sent["wave"], came["wave"], dp, to)

    def w0_copy(k):
        return remote(
            r["mine0"], block(r["f0"], dp, 0, 128), sent["w0row"].at[k], came["w0row"].at[k], y_peer(k), batch
        )

    def pass0_copy(k):
        owner = y_peer(4 - k)
        here = block(r["f0"], owner, 0, 128)
        source = here if k else r["mine0"]
        return remote(source, here, sent["pass0"].at[k], came["pass0"].at[k], sibling, batch)

    def rowa_copy(w, k):
        here = block(full[w], dp, 0, CUT)
        return remote(here, here, sent["rowa"].at[w * 4 + k], came["rowa"].at[w * 4 + k], y_peer(k), batch)

    def rowb_copy(w, k):
        here = quarter(full[w], dp, x, CUT, 3 * D - CUT)
        return remote(here, here, sent["rowb"].at[w * 4 + k], came["rowb"].at[w * 4 + k], y_peer(k), batch)

    def rowx_copy(w, k, j):
        here = quarter(full[w], y_peer(4 - k), x, CUT, 3 * D - CUT)
        at = w * 16 + k * 4 + j
        return remote(here, here, sent["rowx"].at[at], came["rowx"].at[at], dp, x_peer(j))

    def passa_copy(w, k):
        here = block(full[w], y_peer(4 - k), 0, CUT)
        return remote(here, here, sent["passa"].at[w * 4 + k], came["passa"].at[w * 4 + k], sibling, batch)

    def passb_copy(w, k):
        here = block(full[w], y_peer(4 - k), CUT, 3 * D - CUT)
        return remote(here, here, sent["passb"].at[w * 4 + k], came["passb"].at[w * 4 + k], sibling, batch)

    loads[6].wait()
    loads[7].wait()
    pl.semaphore_wait(barrier, 51)
    for w in range(2):
        for k in (2, 1, 3):
            rowb_copy(w, k).start()
    for i in range(6):
        if i != 4:
            loads[i].wait()
    total = tokens[0]
    for s in range(1, SEG):
        total = total + tokens[s]
    eye = jnp.where(iota((10, 128), 0) == iota((10, 128), 1), 1.0, 0.0).astype(BF16)
    r["mine0"][...] = mm(r["w0t"][...], eye, TN).astype(BF16)
    for k in (2, 1, 3):
        w0_copy(k).start()
    pass0_copy(0).start()
    r["send"][...] = pack_waves(r["wave"][...], dest, length, tokens).reshape(32, 16, 128)
    loop(11, 42, lambda k: wave_copy(1 + lax.rem(k, 31)).start())
    for w in range(2):
        for k in (2, 1, 3):
            rowa_copy(w, k).start()
    for w in range(2):
        passa_copy(w, 0).start()
        passb_copy(w, 0).start()
    r["got"][batch] = r["send"][batch]
    block(r["f0"], dp, 0, 128)[...] = r["mine0"][...]
    sum_start("t", "z", jnp.broadcast_to(total.astype(F32), (8, 128)))
    for k in (1, 3, 2):
        w0_copy(k).wait_recv()
        pass0_copy(k).start()
    for w in range(2):
        for k in (1, 3, 2):
            rowb_copy(w, k).wait_recv()
            for j in (2, 1, 3):
                rowx_copy(w, k, j).start()

    def pass_on(w):
        for k in (1, 3, 2):
            rowa_copy(w, k).wait_recv()
            passa_copy(w, k).start()
        for k in (1, 3, 2):
            for j in (1, 3, 2):
                rowx_copy(w, k, j).wait_recv()
            passb_copy(w, k).start()

    def gathered(w):
        for k in range(4):
            passa_copy(w, k).wait_recv()
            passb_copy(w, k).wait_recv()

    loads[4].wait()
    before_waves(r)
    for k in range(4):
        pass0_copy(k).wait_recv()
    spread_first(r["f0"][...], r)
    landed(r["send"].at[0:31], came["wave"])
    forward_first(r["got"][...].reshape(512, 128), r)
    pass_on(0)
    sum_start("t", "g", sum_end("t", "z"))
    gathered(0)
    forward_second(full[0], r)
    pass_on(1)
    gathered(1)

    def core_copy(p, k):
        step = lax.rem(y + k, 4)
        grads = r["g" + str(p)]
        width = 128 if p == "f" else 3 * D
        at = (2 if p == "f" else p) * 4 + k
        return remote(
            block(grads, step * 2 + 1 - core, 0, width), r["rc" + str(p)].at[step],
            sent["core"].at[at], came["core"].at[at], sibling, batch,
        )

    def y_copy(p, k):
        to = lax.rem(y + k, 4)
        width = 128 if p == "f" else HALF
        at = (2 if p == "f" else p) * 4 + k
        return remote(
            r["ys" + str(p)].at[to, :, 0:width], r["yr" + str(p)].at[y],
            sent["y"].at[at], came["y"].at[at], to * 2 + core, batch,
        )

    def bx_copy(p, k):
        to = lax.rem(x + k, 4)
        rows = pl.ds(pl.multiple_of(to * 16, 16), 16)
        return remote(
            r["ys" + str(p)].at[:, rows, HALF:], r["bx" + str(p)].at[x],
            sent["bx"].at[p * 4 + k], came["bx"].at[p * 4 + k], dp, z * 4 + to,
        )

    def x_copy(p, k):
        to = lax.rem(x + k, 4)
        rows = pl.ds(pl.multiple_of(to * 16, 16), 16)
        at = (2 if p == "f" else p) * 4 + k
        return remote(
            r["xs" + str(p)].at[rows], r["xr" + str(p)].at[x],
            sent["x"].at[at], came["x"].at[at], dp, z * 4 + to,
        )

    def by_copy(p, k):
        to = lax.rem(y + k, 4)
        return remote(
            r["by" + str(p)].at[to], r["bz" + str(p)].at[y],
            sent["by"].at[p * 4 + k], came["by"].at[p * 4 + k], to * 2 + core, batch,
        )

    def z_copy(p, k):
        to = lax.rem(z + k, 8)
        return remote(
            r["zs" + str(p)].at[to], r["zr" + str(p)].at[z], sent["z"].at[p], came["z"].at[p], dp, z_peer(k)
        )

    def fz_copy(p, k):
        here = r["fz" + str(p)].at[z]
        return remote(here, here, sent["fz"].at[p], came["fz"].at[p], dp, z_peer(k))

    def fx_copy(p, k):
        here = r["fr" + str(p)].at[x]
        return remote(here, (third_out, second_out)[p].at[x], sent["fx"].at[p * 4 + k], came["fx"].at[p * 4 + k], dp, x_peer(k))

    def core_start(p, grad=None):
        for k in (2, 1, 3, 0):
            if grad is not None:
                grad(pl.ds(pl.multiple_of(lax.rem(y + k, 4) * 128, 128), 128), r)
            core_copy(p, k).start()

    def core_end(p):
        for k in (2, 1, 3, 0):
            step = lax.rem(y + k, 4)
            core_copy(p, k).wait_recv()
            for m in range(4):
                rows = pl.ds(pl.multiple_of((step * 2 + core) * 64 + m * 16, 16), 16)
                here = slice(m * 16, m * 16 + 16)
                own = r["g" + str(p)][rows].astype(F32)
                r["ys" + str(p)][step, here] = (own + r["rc" + str(p)][step, here].astype(F32)).astype(BF16)
            if k:
                y_copy(p, k).start()
        if p != "f":
            for k in (2, 1, 3):
                bx_copy(p, k).start()

    def y_end(p):
        width = 128 if p == "f" else HALF
        for k in (1, 3, 2):
            y_copy(p, k).wait_recv()
        for m in range(4):
            here = slice(m * 16, m * 16 + 16)
            found = r["ys" + str(p)][y, here, 0:width].astype(F32)
            for k in (1, 2, 3):
                found = found + r["yr" + str(p)][lax.rem(y + k, 4), here].astype(F32)
            r["xs" + str(p)][here] = found.astype(BF16)
        for k in (2, 1, 3):
            x_copy(p, k).start()

    def bx_end(p):
        for k in (1, 3, 2):
            bx_copy(p, k).wait_recv()
        rows = pl.ds(pl.multiple_of(x * 16, 16), 16)
        for step in range(4):
            found = r["ys" + str(p)][step, rows, HALF:].astype(F32)
            for k in (1, 2, 3):
                found = found + r["bx" + str(p)][lax.rem(x + k, 4), step].astype(F32)
            r["by" + str(p)][step] = found.astype(BF16)
        for k in (2, 1, 3):
            by_copy(p, k).start()

    def x_end(p):
        for k in (1, 3, 2):
            x_copy(p, k).wait_recv()
        found = r["xs" + str(p)][pl.ds(pl.multiple_of(x * 16, 16), 16)].astype(F32)
        for k in (1, 2, 3):
            found = found + r["xr" + str(p)][lax.rem(x + k, 4)].astype(F32)
        return found

    def by_end(p):
        for k in (1, 3, 2):
            by_copy(p, k).wait_recv()
        found = r["by" + str(p)][y].astype(F32)
        for k in (1, 2, 3):
            found = found + r["bz" + str(p)][lax.rem(y + k, 4)].astype(F32)
        return found

    def z_start(p):
        low, high = x_end(p), by_end(p)
        out = r["zs" + str(p)]
        for q in range(3):
            out[q] = low[:, q * 256 : q * 256 + 256].astype(BF16)
            out[q + 3] = high[:, q * 256 : q * 256 + 256].astype(BF16)
        out[6] = jnp.zeros((16, 256), BF16)
        out[7] = jnp.zeros((16, 256), BF16)
        if p == 1:
            out[6, :, 0:128] = x_end("f").astype(BF16)
        loop(1, 8, lambda k: z_copy(p, k).start())
        r["zr" + str(p)][z] = out[z]

    def z_end(p, per_token, other=None):
        landed(r["zr" + str(p)].at[0:7], came["z"].at[p])
        found = jnp.sum(r["zr" + str(p)][...].astype(F32), axis=0)
        r["fz" + str(p)][z] = found.astype(BF16)
        found = found * per_token
        squares = jnp.sum(found * found, keepdims=True)
        if p == 1:
            sum_start("s", "z", jnp.broadcast_to(squares + other, (8, 128)))
        loop(1, 8, lambda k: fz_copy(p, k).start())
        return squares

    def fx_start(p):
        landed(r["fz" + str(p)].at[0:7], came["fz"].at[p])
        out = r["fr" + str(p)]
        for q in range(6):
            out[x, :, q * 256 : q * 256 + 256] = r["fz" + str(p)][q]
        if p == 1:
            out[x, :, 3 * D :] = r["fz1"][6, :, 0:128]
        for k in (2, 1, 3):
            fx_copy(p, k).start()

    third_layer(full[1], r)
    core_start(0, grad_third)
    back_second(full[1], r)
    core_end(0)
    core_start(1, grad_second)
    back_first(full[0], r)
    core_end(1)
    grad_first(r["gf"], r)
    core_start("f")
    core_end("f")
    y_end(0)
    bx_end(0)
    token_sum = sum_end("t", "g")
    per_token = (1.0 / token_sum)[0:1, 0:1]
    z_start(0)
    y_end(1)
    bx_end(1)
    y_end("f")
    z_start(1)
    squares = z_end(0, per_token)
    fx_start(0)
    z_end(1, per_token, squares)
    outs = [(r["fr0"].at[x], third_out.at[x]), (r["fr1"].at[x], second_out.at[x]), (r["mysg"], squares_out.at[plane]), (r["stat"], tokens_out)]
    outs = [pltpu.make_async_copy(a, b, came["out"].at[i]) for i, (a, b) in enumerate(outs)]
    r["stat"][...] = token_sum
    r["mysg"][...] = sum_end("s", "z")
    loop(1, 16, lambda k: sum_copy("s", "g", k).start())
    outs[2].start()
    fx_start(1)
    outs[1].start()
    outs[0].start()
    r["stat"][...] = token_sum
    outs[3].start()
    for p in range(2):
        for k in (1, 3, 2):
            fx_copy(p, k).wait_recv()
    landed(r["send"].at[0:31], sent["wave"])
    for k in range(4):
        pass0_copy(k).wait_send()
        if k:
            w0_copy(k).wait_send()
        for w in range(2):
            passa_copy(w, k).wait_send()
            passb_copy(w, k).wait_send()
            if k:
                rowa_copy(w, k).wait_send()
                rowb_copy(w, k).wait_send()
                for j in range(1, 4):
                    rowx_copy(w, k, j).wait_send()
        for p in (0, 1, "f"):
            core_copy(p, k).wait_send()
            if k:
                y_copy(p, k).wait_send()
                x_copy(p, k).wait_send()
                if p != "f":
                    bx_copy(p, k).wait_send()
                    by_copy(p, k).wait_send()
                    fx_copy(p, k).wait_send()
    for p in range(2):
        landed(r["zr" + str(p)].at[0:7], sent["z"].at[p])
        landed(r["fz" + str(p)].at[0:7], sent["fz"].at[p])
    sum_sent("t", "z")
    sum_sent("t", "g")
    sum_sent("s", "z")
    for copy in outs:
        copy.wait()
    landed(squares_out.at[0:15], came["sum"].at[3])
    sum_sent("s", "g")


def whole(wave, dest, length, tokens, cot, w0, w1, w2):
    anywhere = pl.BlockSpec(memory_space=pl.ANY)
    sems = []
    for count in SEMS.values():
        sems += [pltpu.SemaphoreType.DMA((count,)) if count else pltpu.SemaphoreType.DMA] * 2
    return pl.pallas_call(
        whole_kernel,
        out_shape=(
            jax.ShapeDtypeStruct((4, 16, 3 * D), BF16),
            jax.ShapeDtypeStruct((4, 16, 3 * D + 128), BF16),
            jax.ShapeDtypeStruct((16, 8, 128), F32),
            jax.ShapeDtypeStruct((8, 128), F32),
        ),
        in_specs=[anywhere] * 8,
        out_specs=(anywhere,) * 4,
        scratch_shapes=[pltpu.SMEM((SEG,), jnp.int32)] * 3
        + [pltpu.VMEM(s, t) for s, t in SCRATCH.values()]
        + sems,
        compiler_params=pltpu.CompilerParams(
            collective_id=0, has_side_effects=True, vmem_limit_bytes=58 << 20
        ),
        cost_estimate=pl.CostEstimate(flops=3000000000, bytes_accessed=3000000, transcendentals=1400000),
    )(wave, dest, length, tokens, cot, w0, w1, w2)


def scale_kernel(third, second, squares, tokens, third_out, second_out, first_out, rms_out):
    rms = jnp.sqrt(jnp.sum(squares[...], axis=0) * (1.0 / COUNT))
    factor = (1.0 / (tokens[...] * jnp.maximum(rms, 1.0)))[0:1, 0:1]
    third_out[...] = third[...].astype(F32) * factor
    second_out[...] = second[:, 0 : 3 * D].astype(F32) * factor
    first = second[:, 3 * D :].astype(F32) * factor
    square = jnp.concatenate([first, jnp.zeros((64, 128), F32)], axis=0)
    first_out[...] = square.T[0:10, 0:64]
    rms_out[0] = jnp.max(rms)


def local(wave, length, dest, tokens, cot, w0, w1, w2):
    third, second, squares, total = whole(wave, dest, length, tokens, cot.reshape(ROWS2, D), w0.T, w1, w2)
    vmem = pl.BlockSpec(memory_space=pltpu.VMEM)
    third, second, first, rms = pl.pallas_call(
        scale_kernel,
        out_shape=(
            jax.ShapeDtypeStruct((64, 3 * D), F32),
            jax.ShapeDtypeStruct((64, 3 * D), F32),
            jax.ShapeDtypeStruct((10, 64), F32),
            jax.ShapeDtypeStruct((1,), F32),
        ),
        in_specs=[vmem] * 4,
        out_specs=(vmem, vmem, vmem, pl.BlockSpec(memory_space=pltpu.SMEM)),
        compiler_params=pltpu.CompilerParams(vmem_limit_bytes=58 << 20),
    )(third.reshape(64, 3 * D), second.reshape(64, 3 * D + 128), squares, total)
    return first.T, second, third, rms


def solution(mesh):
    row = P(("dp", "batch"))
    return jax.shard_map(
        local,
        mesh=mesh,
        in_specs=(row, row, row, row, row, P("dp"), P("dp"), P("dp")),
        out_specs=(P("dp"), P("dp"), P("dp"), P()),
        check_vma=False,
    )
```
